32 devices in a mesh: row: 4 (over z), col: 8 (over y, x, core).
Axes of the slice: x: 2, y: 2, z: 4, core: 2. Of those that a mesh axis runs over, the one named last changes fastest.
Arguments:
- point_data: float32 [4, 8192], P(None, ('row', 'col')), may hold values from 0 to 4, as said below
- right_side: float32 [64, 8192], P(None, ('row', 'col')), may hold values from -45 to 45
- pair_list: int32 [2, 468], replicated, may hold values from 0 to 63, as said below
Outputs:
- solution: float32 [64, 8192], P(None, ('row', 'col'))
- residual: float32 [64, 8192], P(None, ('row', 'col'))
The draws below stay inside these ranges and needn't reach their ends.
Inputs may be any that keep to these rules, and one draw needn't show every extreme that they name: `point_data`: the points of block b lie in one unit cell of a 4 x 4 x 4 grid, one block to a cell; row 3 lies in 0.2 to 0.6. `pair_list`: each column (I, J) has I < J and names two blocks whose cells lie within one cell of each other along every dimension; every such pair is listed exactly once. The columns stand grouped by the device (I // 2 // 8, (J // 2) % 8) of the row and col axes, groups in row-major order.
All inputs are finite; a program needn't handle non-finite values.
Results may differ from the reference program's by a relative error of at most 0.018.
Values may be sent and summed in bfloat16 or wider, within the bound.
No kernel may reach another device: no remote copies, remote signals or barrier semaphores. Data moves between devices by JAX's collectives and lax.ppermute only.
A program may use at most 64 MiB of HBM per device.

```python
import math
import jax
import jax.numpy as jnp
import numpy as np
from jax import lax

BLOCK = 128
COLS = 64
ITERS = 3
SIDE = 4
BLK_DEV = 2
COL_DEVS = 8
NB = 64
N = 8192
DEPTH = 4


def block_layout(key):
    return jax.random.permutation(jax.random.fold_in(key, 11), NB)


def neighbour_cells():
    index = np.arange(SIDE * SIDE * DEPTH)
    along_x = index // (SIDE * DEPTH)
    along_y = index // DEPTH % SIDE
    along_z = index % DEPTH
    lower_cells = []
    upper_cells = []
    for shift_x in (-1, 0, 1):
        for shift_y in (-1, 0, 1):
            for shift_z in (-1, 0, 1):
                moved_x = along_x + shift_x
                moved_y = along_y + shift_y
                moved_z = along_z + shift_z
                inside = (moved_x >= 0) & (moved_x < SIDE) & (moved_y >= 0) & (moved_y < SIDE) & (moved_z >= 0) & (moved_z < DEPTH)
                target = (moved_x * SIDE + moved_y) * DEPTH + moved_z
                keep = inside & (target > index)
                lower_cells.append(index[keep])
                upper_cells.append(target[keep])
    return (np.concatenate(lower_cells), np.concatenate(upper_cells))


def draw_pair_list(key, part):
    layout = block_layout(key)
    block_of_cell = jnp.argsort(layout)
    lower_cells, upper_cells = neighbour_cells()
    one_block = block_of_cell[jnp.asarray(lower_cells, jnp.int32)]
    other_block = block_of_cell[jnp.asarray(upper_cells, jnp.int32)]
    low_block = jnp.minimum(one_block, other_block)
    high_block = jnp.maximum(one_block, other_block)
    device_of = low_block // BLK_DEV // COL_DEVS * COL_DEVS + high_block // BLK_DEV % COL_DEVS
    ordering = jnp.argsort(device_of * NB + low_block, stable=True)
    return jnp.stack([low_block[ordering], high_block[ordering]]).astype(jnp.int32)


def draw_point_data(key, part):
    layout = block_layout(key)
    cell_x = layout // (SIDE * DEPTH)
    cell_y = layout // DEPTH % SIDE
    cell_z = layout % DEPTH
    corner = jnp.stack([cell_x, cell_y, cell_z]).astype(jnp.float32)
    inner_key, scale_key = jax.random.split(jax.random.fold_in(key, 23))
    uniform = jax.random.uniform(inner_key, (3, NB, BLOCK), jnp.float32)
    inside = uniform
    scales = jnp.exp(jax.random.uniform(scale_key, (NB, BLOCK), jnp.float32, math.log(0.2), math.log(0.6)))
    coords = corner[:, :, None] + inside
    return jnp.concatenate([coords, scales[None]], axis=0).reshape(4, NB * BLOCK).astype(jnp.float32)


def draw_right_side(key, part):
    base_key, row_key, column_key = jax.random.split(jax.random.fold_in(key, 31), 3)
    position = jnp.arange(N).astype(jnp.float32) / N
    trend = 0.5 + position
    row_scale = jnp.exp(jax.random.uniform(row_key, (N,), jnp.float32, math.log(0.3), math.log(3.0)))
    column_scale = jnp.exp(jax.random.uniform(column_key, (COLS,), jnp.float32, math.log(0.5), math.log(2.0)))
    base = jnp.clip(jax.random.normal(base_key, (COLS, N), jnp.float32), -5.0, 5.0)
    return (base * (row_scale * trend)[None, :] * column_scale[:, None]).astype(jnp.float32)


def setup_inputs(seed: int = 0) -> dict:
    arg_keys = jax.random.split(jax.random.key(seed), 4)
    return {
        "point_data": draw_point_data(jax.random.fold_in(arg_keys[3], 71), 0),
        "right_side": draw_right_side(jax.random.fold_in(arg_keys[3], 71), 0),
        "pair_list": draw_pair_list(jax.random.fold_in(arg_keys[3], 71), 0),
    }


long_range = 1.0
short_range = 0.35
nugget = 1.0
pair_batch = 64
diagonal_batch = 16

def wendland(distance, reach):
    scaled = distance / reach
    remain = jnp.maximum(1.0 - scaled, 0.0)
    square = remain * remain
    return square * square * (4.0 * scaled + 1.0)

def covariance_tiles(row_points, column_points):
    delta_x = row_points[:, 0, :, None] - column_points[:, 0, None, :]
    delta_y = row_points[:, 1, :, None] - column_points[:, 1, None, :]
    delta_z = row_points[:, 2, :, None] - column_points[:, 2, None, :]
    distance = jnp.sqrt(delta_x * delta_x + delta_y * delta_y + delta_z * delta_z)
    kernel = wendland(distance, long_range) + wendland(distance, short_range)
    return row_points[:, 3, :, None] * kernel * column_points[:, 3, None, :]

def round_tiles(values):
    return lax.optimization_barrier(values.astype(jnp.bfloat16)).astype(jnp.float32)

def apply_operator(direction, blocks, lower_block, upper_block, keep_pair):
    rounded = round_tiles(direction)
    direction_blocks = rounded.reshape(COLS, NB, BLOCK)
    diagonal_points = blocks.reshape(NB // diagonal_batch, diagonal_batch, 4, BLOCK)
    diagonal_dirs = direction_blocks.reshape(COLS, NB // diagonal_batch, diagonal_batch, BLOCK).transpose(1, 0, 2, 3)

    def diagonal_step(inputs):
        points_here, dirs_here = inputs
        tiles_here = round_tiles(covariance_tiles(points_here, points_here))
        return jnp.einsum('tij,ctj->cti', tiles_here, dirs_here)
    diagonal = lax.map(diagonal_step, (diagonal_points, diagonal_dirs))
    diagonal = diagonal.transpose(1, 0, 2, 3).reshape(COLS, NB * BLOCK)

    def pair_step(totals, inputs):
        low_here, high_here, keep_here = inputs
        tiles_here = covariance_tiles(blocks[low_here], blocks[high_here])
        tiles_here = round_tiles(jnp.where(keep_here[:, None, None], tiles_here, 0.0))
        totals = totals.at[:, low_here].add(jnp.einsum('tij,ctj->cti', tiles_here, direction_blocks[:, high_here]))
        totals = totals.at[:, high_here].add(jnp.einsum('tij,cti->ctj', tiles_here, direction_blocks[:, low_here]))
        return (totals, None)
    empty = jnp.zeros((COLS, NB, BLOCK), jnp.float32)
    totals, _ = lax.scan(pair_step, empty, (lower_block, upper_block, keep_pair))
    return nugget * direction + diagonal + totals.reshape(COLS, NB * BLOCK)

def reference(point_data, right_side, pair_list):
    blocks = point_data.reshape(4, NB, BLOCK).transpose(1, 0, 2)
    listed = pair_list.shape[1]
    padded = (listed + pair_batch - 1) // pair_batch * pair_batch
    filler = jnp.zeros((padded - listed,), jnp.int32)
    lower_block = jnp.concatenate([pair_list[0].astype(jnp.int32), filler]).reshape(-1, pair_batch)
    upper_block = jnp.concatenate([pair_list[1].astype(jnp.int32), filler]).reshape(-1, pair_batch)
    keep_pair = (jnp.arange(padded) < listed).reshape(-1, pair_batch)
    solution = jnp.zeros_like(right_side)
    residual = right_side
    direction = right_side
    norm_now = lax.optimization_barrier(jnp.sum(residual * residual, axis=1))
    for step in range(ITERS):
        image = apply_operator(direction, blocks, lower_block, upper_block, keep_pair)
        alpha = norm_now / lax.optimization_barrier(jnp.sum(direction * image, axis=1))
        solution = solution + alpha[:, None] * direction
        residual = residual - alpha[:, None] * image
        if step + 1 < ITERS:
            norm_next = lax.optimization_barrier(jnp.sum(residual * residual, axis=1))
            direction = residual + (norm_next / norm_now)[:, None] * direction
            norm_now = norm_next
    return (solution, residual)
```

```python
import functools
import jax
import jax.numpy as jnp
from jax import lax
from jax.experimental import pallas as pl
from jax.experimental.pallas import tpu as pltpu
from jax.sharding import PartitionSpec as P

BLOCK = 128
ITERS = 3


long_range = 1.0
short_range = 0.35
nugget = 1.0
tiles_per_step = 8
rows_here = 4
chunk = 4
chunks_per_step = 8
tile_bytes_limit = 24 * 2**20
kernel_bytes = 12 * 2**20
f32 = jnp.float32
bf16 = jnp.bfloat16


def wendland(distance, reach):
    scaled = distance / reach
    remain = jnp.maximum(1.0 - scaled, 0.0)
    square = remain * remain
    return square * square * (4.0 * scaled + 1.0)


def covariance_tiles(row_points, column_points):
    delta_x = row_points[:, 0, :, None] - column_points[:, 0, None, :]
    delta_y = row_points[:, 1, :, None] - column_points[:, 1, None, :]
    delta_z = row_points[:, 2, :, None] - column_points[:, 2, None, :]
    distance = jnp.sqrt(delta_x * delta_x + delta_y * delta_y + delta_z * delta_z)
    kernel = wendland(distance, long_range) + wendland(distance, short_range)
    return row_points[:, 3, :, None] * kernel * column_points[:, 3, None, :]


def as_blocks(points):
    return points.reshape(4, -1, BLOCK).transpose(1, 0, 2)


def by_points(point_data, right_side, pair_list):
    col_devices = lax.axis_size("col")
    my_row = lax.axis_index("row")
    my_column = lax.axis_index("col")
    points = point_data.shape[1]
    blocks_here = points // BLOCK
    realizations = right_side.shape[0]
    own_blocks = as_blocks(point_data)
    row_blocks = as_blocks(lax.all_gather(point_data, "col", axis=1, tiled=True))
    column_blocks = as_blocks(lax.all_gather(point_data, "row", axis=1, tiled=True))
    row_count = row_blocks.shape[0]
    column_count = column_blocks.shape[0]
    lower_block = pair_list[0]
    upper_block = pair_list[1]
    this_device = my_row * col_devices + my_column
    device_of = (
        lower_block // blocks_here // col_devices * col_devices
        + upper_block // blocks_here % col_devices
    )
    roster_first_pair = jnp.sum((device_of < this_device).astype(jnp.int32))
    roster_pair_count = jnp.sum((device_of == this_device).astype(jnp.int32))
    roster_row_slot = jnp.clip(lower_block - my_row * col_devices * blocks_here, 0, row_count - 1)
    roster_column_slot = jnp.clip(
        upper_block // blocks_here // col_devices * blocks_here + upper_block % blocks_here,
        0,
        column_count - 1,
    )
    roster_step_count = (roster_pair_count + tiles_per_step - 1) // tiles_per_step
    plan = (
        roster_first_pair,
        roster_pair_count,
        roster_row_slot,
        roster_column_slot,
        roster_step_count,
        lower_block.shape[0],
    )
    first_pair, pair_count, row_slot, column_slot, step_count, listed = plan
    own_tiles = covariance_tiles(own_blocks, own_blocks).astype(jnp.bfloat16)

    def pick_tiles(step):
        offsets = step * tiles_per_step + jnp.arange(tiles_per_step)
        usable = offsets < pair_count
        picked = jnp.minimum(first_pair + offsets, listed - 1)
        row_pick = row_slot[picked]
        column_pick = column_slot[picked]
        tiles_now = covariance_tiles(row_blocks[row_pick], column_blocks[column_pick])
        tiles_now = jnp.where(usable[:, None, None], tiles_now, 0.0).astype(jnp.bfloat16)
        return (tiles_now, row_pick, column_pick)

    def inner(operands):
        stacked = jnp.stack(
            [jnp.sum(one_side * other_side, axis=1) for one_side, other_side in operands]
        )
        return lax.psum(stacked, ("row", "col"))

    solution = jnp.zeros_like(right_side)
    residual = right_side
    direction = right_side
    norm_now = inner(((residual, residual),))[0]
    for step in range(ITERS):
        rounded = direction.astype(jnp.bfloat16)
        product_row_direction = lax.all_gather(rounded, "col", axis=1, tiled=True)
        product_column_direction = lax.all_gather(rounded, "row", axis=1, tiled=True)
        row_direction = product_row_direction
        column_direction = product_column_direction
        row_direction = row_direction.reshape(realizations, row_count, BLOCK)
        column_direction = column_direction.reshape(realizations, column_count, BLOCK)

        def add_step(step, totals):
            into_rows, into_columns = totals
            tiles_now, row_pick, column_pick = pick_tiles(step)
            to_rows = jnp.einsum(
                "tij,ctj->cti",
                tiles_now,
                column_direction[:, column_pick],
                preferred_element_type=jnp.float32,
            )
            to_columns = jnp.einsum(
                "tij,cti->ctj",
                tiles_now,
                row_direction[:, row_pick],
                preferred_element_type=jnp.float32,
            )
            return (
                into_rows.at[:, row_pick].add(to_rows),
                into_columns.at[:, column_pick].add(to_columns),
            )

        empty_rows = jnp.zeros((realizations, row_count, BLOCK), jnp.float32)
        empty_columns = jnp.zeros((realizations, column_count, BLOCK), jnp.float32)
        into_rows, into_columns = lax.fori_loop(
            0, step_count, add_step, (empty_rows, empty_columns)
        )
        product_into_rows = into_rows.reshape(realizations, -1)
        product_into_columns = into_columns.reshape(realizations, -1)
        from_rows = lax.psum_scatter(product_into_rows, "col", scatter_dimension=1, tiled=True)
        from_columns = lax.psum_scatter(
            product_into_columns.astype(jnp.bfloat16), "row", scatter_dimension=1, tiled=True
        ).astype(jnp.float32)
        diagonal = jnp.einsum(
            "tij,ctj->cti",
            own_tiles,
            rounded.reshape(realizations, blocks_here, BLOCK),
            preferred_element_type=jnp.float32,
        )
        image = (
            nugget * direction + diagonal.reshape(realizations, points) + from_rows + from_columns
        )
        alpha = norm_now / inner(((direction, image),))[0]
        solution = solution + alpha[:, None] * direction
        residual = residual - alpha[:, None] * image
        if step + 1 < ITERS:
            norm_next = inner(((residual, residual),))[0]
            direction = residual + (norm_next / norm_now)[:, None] * direction
            norm_now = norm_next
    return (solution, residual)


def tile_schedule(listed, blocks):
    half = (listed + 1) // 2
    entries = half + blocks // 2
    sizes = range(12, 25)
    width = min(sizes, key=lambda size: (-(-entries // size) * size, -size))
    steps = -(-entries // width)
    longest = (2 * half + blocks // 2 + 3 * blocks) // chunk
    chunks = -(-longest // chunks_per_step) * chunks_per_step + chunks_per_step
    return half, width, steps, chunks


def radial(squared):
    squared = jnp.maximum(squared, 1e-30)
    distance = squared * lax.rsqrt(squared)
    near = jnp.maximum(long_range - distance, 0.0)
    close = jnp.maximum(short_range - distance, 0.0)

    def falling(remain, reach):
        square = remain * remain
        return square * square * (5.0 / reach**4 - 4.0 / reach**5 * remain)

    return (falling(near, long_range) + falling(close, short_range)).astype(bf16)


def three_parts(values):
    first = values.astype(bf16).astype(f32)
    rest = values - first
    second = rest.astype(bf16).astype(f32)
    return first, second, rest - second


def row_number(shape):
    return lax.broadcasted_iota(jnp.int32, shape, len(shape) - 2)


def store_scaled(fields_ref, direction, scale):
    scaled = jnp.where(row_number(direction.shape) < rows_here, direction * scale, 0.0)
    blocks = direction.shape[0]
    doubled = jnp.concatenate([scaled, jnp.zeros_like(scaled)], axis=1)
    fields_ref[0:blocks] = doubled.astype(bf16)
    fields_ref[blocks] = jnp.zeros((16, BLOCK), bf16)


def multiply(owner_ref, entry_ref, count, tiles_ref, fields_ref, totals_ref):
    totals_ref[...] = jnp.zeros_like(totals_ref)

    def step(number, carry):
        products = []
        for part in range(chunks_per_step):
            fields = []
            tiles = []
            for slot in range(chunk):
                entry = entry_ref[(number * chunks_per_step + part) * chunk + slot]
                fields.append(fields_ref[entry & 65535])
                tiles.append(tiles_ref[entry >> 16])
            product = jnp.dot(
                jnp.concatenate(fields, axis=1),
                jnp.concatenate(tiles, axis=0),
                preferred_element_type=f32,
            )
            products.append(product[0:8])
        for part in range(chunks_per_step):
            totals_ref[owner_ref[number * chunks_per_step + part]] += products[part]
        return carry

    lax.fori_loop(0, (count + chunks_per_step - 1) // chunks_per_step, step, 0)


def first_kernel(
    plan,
    core_ref,
    pair_ref,
    gathered_ref,
    tiles_ref,
    product_ref,
    owner_ref,
    entry_ref,
    count_ref,
    left_ref,
    right_ref,
    fields_ref,
    totals_ref,
    length_ref,
    open_ref,
):
    half, width, steps, chunks = plan
    blocks = gathered_ref.shape[0]
    listed = pair_ref.shape[1]
    core = core_ref[0]
    slots = width * steps
    highest = jnp.max(jnp.max(gathered_ref[...], axis=0), axis=1, keepdims=True)
    lowest = jnp.min(jnp.min(gathered_ref[...], axis=0), axis=1, keepdims=True)
    centre = 0.5 * (highest + lowest)

    def prepare(block, carry):
        row = row_number((8, BLOCK))
        is_coordinate = (row >= 4) & (row < 7)
        shifted = jnp.where(is_coordinate, gathered_ref[block] - centre, 0.0)
        squared = jnp.sum(shifted * shifted, axis=0, keepdims=True)
        left = jnp.where(row == 7, 1.0, jnp.where(row == 0, squared, shifted))
        right = jnp.where(row == 7, squared, jnp.where(row == 0, 1.0, -2.0 * shifted))
        left_1, left_2, left_3 = three_parts(left)
        right_1, right_2, right_3 = three_parts(right)
        left_all = jnp.concatenate([left_1, left_1, left_2, left_2, left_1, left_3], axis=0)
        right_all = jnp.concatenate([right_1, right_2, right_1, right_2, right_3, right_1], axis=0)
        left_ref[block] = left_all.T.astype(bf16)
        right_ref[block] = right_all.astype(bf16)
        length_ref[block] = 0
        return carry

    lax.fori_loop(0, blocks, prepare, 0, unroll=4)
    length_ref[blocks] = 0
    open_ref[blocks] = 0
    spare = chunks * chunk
    empty = blocks

    def append(block, entry, usable, used):
        length = length_ref[block]
        place = length & (chunk - 1)
        fresh = place == 0
        where = jnp.where(fresh, used, open_ref[block])
        begins = fresh & usable
        target = jnp.where(usable, block, blocks)
        length_ref[target] = length + 1
        open_ref[target] = where
        for slot in range(1, chunk):
            entry_ref[jnp.where(begins, where * chunk + slot, spare)] = empty
        entry_ref[jnp.where(usable, where * chunk + place, spare)] = entry
        owner_ref[jnp.where(usable, where, chunks)] = block
        return used + begins.astype(jnp.int32)

    def make_tiles(step, used):
        for slot in range(width):
            number = step * width + slot
            is_pair = number < half
            pair = core * half + number
            is_diagonal = (number >= half) & (number < half + blocks // 2)
            pair_usable = is_pair & (pair < listed)
            safe = jnp.minimum(pair, listed - 1)
            own = jnp.minimum(core * (blocks // 2) + number - half, blocks - 1)
            low = jnp.where(is_pair, pair_ref[0, safe], own)
            high = jnp.where(is_pair, pair_ref[1, safe], own)
            squared = jnp.dot(left_ref[low], right_ref[high], preferred_element_type=f32)
            tile = radial(squared)
            tiles_ref[number] = tile
            tiles_ref[slots + number] = tile.T
            used = append(high, number * 65536 + low, pair_usable | is_diagonal, used)
            used = append(low, (slots + number) * 65536 + high, pair_usable, used)
        return used

    used = lax.fori_loop(0, steps, make_tiles, 0)
    count_ref[0] = used
    for part in range(chunks_per_step):
        owner_ref[used + part] = blocks
        for slot in range(chunk):
            entry_ref[(used + part) * chunk + slot] = empty
    store_scaled(fields_ref, gathered_ref[...], gathered_ref[:, 7:8, :])
    multiply(owner_ref, entry_ref, used, tiles_ref, fields_ref, totals_ref)
    product_ref[...] = totals_ref[0:blocks]


def total(values):
    return jnp.sum(jnp.sum(values, axis=0), axis=1, keepdims=True)[None]


def advance(mine_ref, other_ref, scale, direction, residual):
    row = row_number((1, 8, 1))
    image = nugget * direction + scale * (mine_ref[...] + other_ref[...])
    norm_now = total(residual * residual)
    along = total(direction * image)
    alpha = norm_now / jnp.where(row < rows_here, along, 1.0)
    return alpha * direction, residual - alpha * image, norm_now


def next_kernel(
    first,
    owner_ref,
    entry_ref,
    count_ref,
    gathered_ref,
    mine_ref,
    other_ref,
    *rest,
):
    if first:
        tiles_ref, product_ref, state_out_ref, fields_ref, totals_ref = rest
        row = row_number(gathered_ref.shape)
        direction = jnp.where(row < rows_here, gathered_ref[...], 0.0)
        residual = direction
    else:
        state_ref, tiles_ref, product_ref, state_out_ref, fields_ref, totals_ref = rest
        direction = state_ref[2]
        residual = state_ref[1]
    scale = gathered_ref[:, 7:8, :]
    moved, residual, norm_now = advance(mine_ref, other_ref, scale, direction, residual)
    norm_next = total(residual * residual)
    row = row_number((1, 8, 1))
    beta = norm_next / jnp.where(row < rows_here, norm_now, 1.0)
    direction = residual + beta * direction
    state_out_ref[0] = moved if first else state_ref[0] + moved
    state_out_ref[1] = residual
    state_out_ref[2] = direction
    store_scaled(fields_ref, direction, scale)
    multiply(owner_ref, entry_ref, count_ref[0], tiles_ref, fields_ref, totals_ref)
    product_ref[...] = totals_ref[0 : gathered_ref.shape[0]]


def last_kernel(core_ref, gathered_ref, mine_ref, other_ref, state_ref, result_ref):
    scale = gathered_ref[:, 7:8, :]
    moved, residual, _ = advance(mine_ref, other_ref, scale, state_ref[2], state_ref[1])
    chosen = jnp.where(core_ref[0] == 0, state_ref[0] + moved, residual)
    result_ref[...] = chosen[:, 0:rows_here, :]


def by_realizations(point_data, right_side, pair_list):
    col_devices = lax.axis_size("col")
    devices = lax.axis_size("row") * col_devices
    chips = devices // 2
    blocks_here = point_data.shape[1] // BLOCK
    blocks = blocks_here * devices
    core = lax.rem(lax.axis_index("col"), 2).astype(jnp.int32).reshape(1)
    axes = ("row", "col")
    vector = pl.BlockSpec(memory_space=pltpu.VMEM)
    scalar = pl.BlockSpec(memory_space=pltpu.SMEM)
    plan = tile_schedule(pair_list.shape[1], blocks)
    half, width, steps, chunks = plan
    slots = width * steps

    points = point_data.reshape(1, 4, blocks_here, BLOCK).transpose(0, 2, 1, 3)
    fields = right_side.reshape(chips, rows_here, blocks_here, BLOCK).transpose(0, 2, 1, 3)
    points = jnp.broadcast_to(points, (chips, blocks_here, 4, BLOCK))
    outgoing = jnp.concatenate([fields, points], axis=2)
    outgoing = jnp.broadcast_to(outgoing[:, None], (chips, 2, blocks_here, 8, BLOCK))
    outgoing = outgoing.reshape(devices, blocks_here, 8, BLOCK)
    gathered = lax.all_to_all(outgoing, axes, 0, 0, tiled=True).reshape(blocks, 8, BLOCK)

    field_shape = jax.ShapeDtypeStruct((blocks, 8, BLOCK), f32)
    state_shape = jax.ShapeDtypeStruct((3, blocks, 8, BLOCK), f32)
    work = [pltpu.VMEM((blocks + 1, 16, BLOCK), bf16), pltpu.VMEM((blocks + 1, 8, BLOCK), f32)]
    limits = pltpu.CompilerParams(vmem_limit_bytes=kernel_bytes)
    tiles, mine, owner, entry, count = pl.pallas_call(
        functools.partial(first_kernel, plan),
        out_shape=(
            pltpu.VMEM((2 * slots, BLOCK, BLOCK), bf16),
            field_shape,
            jax.ShapeDtypeStruct((chunks + 8,), jnp.int32),
            jax.ShapeDtypeStruct((chunks * chunk + 8,), jnp.int32),
            jax.ShapeDtypeStruct((1,), jnp.int32),
        ),
        in_specs=[scalar, scalar, vector],
        out_specs=(vector, vector, scalar, scalar, scalar),
        scratch_shapes=[
            pltpu.VMEM((blocks, BLOCK, 48), bf16),
            pltpu.VMEM((blocks, 48, BLOCK), bf16),
            *work,
            pltpu.SMEM((blocks + 8,), jnp.int32),
            pltpu.SMEM((blocks + 8,), jnp.int32),
        ],
        compiler_params=limits,
    )(core, pair_list, gathered)
    tiles = pltpu.with_memory_space_constraint(tiles, pltpu.VMEM)
    swap = [(place, place ^ 1) for place in range(col_devices)]
    state = None
    for step in range(1, ITERS):
        other = lax.ppermute(mine, "col", swap)
        first = step == 1
        carried = () if first else (state,)
        mine, state = pl.pallas_call(
            functools.partial(next_kernel, first),
            out_shape=(field_shape, state_shape),
            in_specs=[scalar, scalar, scalar] + [vector] * (4 + len(carried)),
            out_specs=(vector, vector),
            scratch_shapes=work,
            compiler_params=limits,
        )(owner, entry, count, gathered, mine, other, *carried, tiles)
    other = lax.ppermute(mine, "col", swap)
    result = pl.pallas_call(
        last_kernel,
        out_shape=jax.ShapeDtypeStruct((blocks, rows_here, BLOCK), f32),
        in_specs=[scalar] + [vector] * 4,
        out_specs=vector,
        compiler_params=limits,
    )(core, gathered, mine, other, state)
    result = result.reshape(devices, blocks_here, rows_here, BLOCK)
    received = lax.all_to_all(result, axes, 0, 0, tiled=True)
    received = received.reshape(chips, 2, blocks_here, rows_here, BLOCK)
    received = received.transpose(1, 0, 3, 2, 4).reshape(2, right_side.shape[0], -1)
    return received[0], received[1]


def per_device(point_data, right_side, pair_list):
    col_devices = lax.axis_size("col")
    devices = lax.axis_size("row") * col_devices
    blocks = point_data.shape[1] // BLOCK * devices
    _, width, steps, _ = tile_schedule(pair_list.shape[1], blocks)
    tile_bytes = 2 * width * steps * BLOCK * BLOCK * 2
    paired = col_devices % 2 == 0 and blocks % 2 == 0
    if paired and right_side.shape[0] == rows_here * (devices // 2) and tile_bytes <= tile_bytes_limit:
        return by_realizations(point_data, right_side, pair_list)
    return by_points(point_data, right_side, pair_list)


def solution(mesh):
    placed = (P(None, ("row", "col")), P(None, ("row", "col")), P())
    return jax.shard_map(
        per_device,
        mesh=mesh,
        in_specs=placed,
        out_specs=(P(None, ("row", "col")), P(None, ("row", "col"))),
        check_vma=False,
    )
```

```python
import functools
import jax
import jax.numpy as jnp
from jax import lax
from jax.experimental import pallas as pl
from jax.experimental.pallas import tpu as pltpu
from jax.sharding import PartitionSpec as P

BLOCK = 128
ITERS = 3


long_range = 1.0
short_range = 0.35
nugget = 1.0
tiles_per_step = 8
rows_here = 4
chunk = 4
chunks_per_step = 8
tile_bytes_limit = 24 * 2**20
kernel_bytes = 12 * 2**20
f32 = jnp.float32
bf16 = jnp.bfloat16


def wendland(distance, reach):
    scaled = distance / reach
    remain = jnp.maximum(1.0 - scaled, 0.0)
    square = remain * remain
    return square * square * (4.0 * scaled + 1.0)


def covariance_tiles(row_points, column_points):
    delta_x = row_points[:, 0, :, None] - column_points[:, 0, None, :]
    delta_y = row_points[:, 1, :, None] - column_points[:, 1, None, :]
    delta_z = row_points[:, 2, :, None] - column_points[:, 2, None, :]
    distance = jnp.sqrt(delta_x * delta_x + delta_y * delta_y + delta_z * delta_z)
    kernel = wendland(distance, long_range) + wendland(distance, short_range)
    return row_points[:, 3, :, None] * kernel * column_points[:, 3, None, :]


def as_blocks(points):
    return points.reshape(4, -1, BLOCK).transpose(1, 0, 2)


def by_points(point_data, right_side, pair_list):
    col_devices = lax.axis_size("col")
    my_row = lax.axis_index("row")
    my_column = lax.axis_index("col")
    points = point_data.shape[1]
    blocks_here = points // BLOCK
    realizations = right_side.shape[0]
    own_blocks = as_blocks(point_data)
    row_blocks = as_blocks(lax.all_gather(point_data, "col", axis=1, tiled=True))
    column_blocks = as_blocks(lax.all_gather(point_data, "row", axis=1, tiled=True))
    row_count = row_blocks.shape[0]
    column_count = column_blocks.shape[0]
    lower_block = pair_list[0]
    upper_block = pair_list[1]
    this_device = my_row * col_devices + my_column
    device_of = (
        lower_block // blocks_here // col_devices * col_devices
        + upper_block // blocks_here % col_devices
    )
    roster_first_pair = jnp.sum((device_of < this_device).astype(jnp.int32))
    roster_pair_count = jnp.sum((device_of == this_device).astype(jnp.int32))
    roster_row_slot = jnp.clip(lower_block - my_row * col_devices * blocks_here, 0, row_count - 1)
    roster_column_slot = jnp.clip(
        upper_block // blocks_here // col_devices * blocks_here + upper_block % blocks_here,
        0,
        column_count - 1,
    )
    roster_step_count = (roster_pair_count + tiles_per_step - 1) // tiles_per_step
    plan = (
        roster_first_pair,
        roster_pair_count,
        roster_row_slot,
        roster_column_slot,
        roster_step_count,
        lower_block.shape[0],
    )
    first_pair, pair_count, row_slot, column_slot, step_count, listed = plan
    own_tiles = covariance_tiles(own_blocks, own_blocks).astype(jnp.bfloat16)

    def pick_tiles(step):
        offsets = step * tiles_per_step + jnp.arange(tiles_per_step)
        usable = offsets < pair_count
        picked = jnp.minimum(first_pair + offsets, listed - 1)
        row_pick = row_slot[picked]
        column_pick = column_slot[picked]
        tiles_now = covariance_tiles(row_blocks[row_pick], column_blocks[column_pick])
        tiles_now = jnp.where(usable[:, None, None], tiles_now, 0.0).astype(jnp.bfloat16)
        return (tiles_now, row_pick, column_pick)

    def inner(operands):
        stacked = jnp.stack(
            [jnp.sum(one_side * other_side, axis=1) for one_side, other_side in operands]
        )
        return lax.psum(stacked, ("row", "col"))

    solution = jnp.zeros_like(right_side)
    residual = right_side
    direction = right_side
    norm_now = inner(((residual, residual),))[0]
    for step in range(ITERS):
        rounded = direction.astype(jnp.bfloat16)
        product_row_direction = lax.all_gather(rounded, "col", axis=1, tiled=True)
        product_column_direction = lax.all_gather(rounded, "row", axis=1, tiled=True)
        row_direction = product_row_direction
        column_direction = product_column_direction
        row_direction = row_direction.reshape(realizations, row_count, BLOCK)
        column_direction = column_direction.reshape(realizations, column_count, BLOCK)

        def add_step(step, totals):
            into_rows, into_columns = totals
            tiles_now, row_pick, column_pick = pick_tiles(step)
            to_rows = jnp.einsum(
                "tij,ctj->cti",
                tiles_now,
                column_direction[:, column_pick],
                preferred_element_type=jnp.float32,
            )
            to_columns = jnp.einsum(
                "tij,cti->ctj",
                tiles_now,
                row_direction[:, row_pick],
                preferred_element_type=jnp.float32,
            )
            return (
                into_rows.at[:, row_pick].add(to_rows),
                into_columns.at[:, column_pick].add(to_columns),
            )

        empty_rows = jnp.zeros((realizations, row_count, BLOCK), jnp.float32)
        empty_columns = jnp.zeros((realizations, column_count, BLOCK), jnp.float32)
        into_rows, into_columns = lax.fori_loop(
            0, step_count, add_step, (empty_rows, empty_columns)
        )
        product_into_rows = into_rows.reshape(realizations, -1)
        product_into_columns = into_columns.reshape(realizations, -1)
        from_rows = lax.psum_scatter(product_into_rows, "col", scatter_dimension=1, tiled=True)
        from_columns = lax.psum_scatter(
            product_into_columns.astype(jnp.bfloat16), "row", scatter_dimension=1, tiled=True
        ).astype(jnp.float32)
        diagonal = jnp.einsum(
            "tij,ctj->cti",
            own_tiles,
            rounded.reshape(realizations, blocks_here, BLOCK),
            preferred_element_type=jnp.float32,
        )
        image = (
            nugget * direction + diagonal.reshape(realizations, points) + from_rows + from_columns
        )
        alpha = norm_now / inner(((direction, image),))[0]
        solution = solution + alpha[:, None] * direction
        residual = residual - alpha[:, None] * image
        if step + 1 < ITERS:
            norm_next = inner(((residual, residual),))[0]
            direction = residual + (norm_next / norm_now)[:, None] * direction
            norm_now = norm_next
    return (solution, residual)


def tile_schedule(listed, blocks):
    half = (listed + 1) // 2
    entries = half + blocks // 2
    sizes = range(12, 21)
    width = min(sizes, key=lambda size: (-(-entries // (2 * size)) * size, -size))
    steps = -(-entries // (2 * width)) * 2
    longest = (2 * half + blocks // 2 + 3 * blocks) // chunk
    chunks = -(-longest // chunks_per_step) * chunks_per_step + chunks_per_step
    return half, width, steps, chunks


def packing_kernel(point_hbm, field_hbm, outgoing_ref, point_ref, field_ref, arrived):
    devices, blocks_here = outgoing_ref.shape[0:2]
    copies = (
        pltpu.make_async_copy(point_hbm, point_ref, arrived.at[0]),
        pltpu.make_async_copy(field_hbm, field_ref, arrived.at[1]),
    )
    for copy in copies:
        copy.start()
    for copy in copies:
        copy.wait()
    for chip in range(devices // 2):
        for block in range(blocks_here):
            place = pl.ds(block * BLOCK, BLOCK)
            fields = field_ref[pl.ds(chip * rows_here, rows_here), place]
            both = jnp.concatenate([fields, point_ref[:, place]], axis=0)
            outgoing_ref[2 * chip, block] = both
            outgoing_ref[2 * chip + 1, block] = both


def entry_blocks(plan, blocks, core, pair_ref, number):
    half = plan[0]
    listed = pair_ref.shape[1]
    pair = core * half + number
    is_pair = number < half
    pair_usable = is_pair & (pair < listed)
    usable = pair_usable | ((number >= half) & (number < half + blocks // 2))
    safe = jnp.minimum(pair, listed - 1)
    own = jnp.minimum(core * (blocks // 2) + number - half, blocks - 1)
    low = jnp.where(is_pair, pair_ref[0, safe], own)
    high = jnp.where(is_pair, pair_ref[1, safe], own)
    return low, high, usable, pair_usable


def listing_kernel(
    plan, blocks, core_ref, pair_ref, owner_ref, entry_ref, count_ref, length_ref, open_ref
):
    _, width, steps, chunks = plan
    core = core_ref[0]
    slots = width * steps
    spare = chunks * chunk
    empty = blocks

    def clear(block, carry):
        length_ref[block] = 0
        open_ref[block] = 0
        return carry

    lax.fori_loop(0, blocks + 1, clear, 0)

    def append(block, entry, usable, used):
        length = length_ref[block]
        place = length & (chunk - 1)
        fresh = place == 0
        where = jnp.where(fresh, used, open_ref[block])
        begins = fresh & usable
        target = jnp.where(usable, block, blocks)
        length_ref[target] = length + 1
        open_ref[target] = where
        for slot in range(1, chunk):
            entry_ref[jnp.where(begins, where * chunk + slot, spare)] = empty
        entry_ref[jnp.where(usable, where * chunk + place, spare)] = entry
        owner_ref[jnp.where(usable, where, chunks)] = block
        return used + begins.astype(jnp.int32)

    def list_tiles(step, used):
        for slot in range(width):
            number = step * width + slot
            low, high, usable, pair_usable = entry_blocks(plan, blocks, core, pair_ref, number)
            used = append(high, number * 65536 + low, usable, used)
            used = append(low, (slots + number) * 65536 + high, pair_usable, used)
        return used

    used = lax.fori_loop(0, steps, list_tiles, 0)
    count_ref[0] = used
    for part in range(chunks_per_step):
        owner_ref[used + part] = blocks
        for slot in range(chunk):
            entry_ref[(used + part) * chunk + slot] = empty


def radial(squared):
    squared = jnp.maximum(squared, 1e-30)
    distance = squared * lax.rsqrt(squared)
    near = jnp.maximum(long_range - distance, 0.0)
    close = jnp.maximum(short_range - distance, 0.0)

    def falling(remain, reach):
        square = remain * remain
        return square * square * (5.0 / reach**4 - 4.0 / reach**5 * remain)

    return (falling(near, long_range) + falling(close, short_range)).astype(bf16)


def three_parts(values):
    first = values.astype(bf16).astype(f32)
    rest = values - first
    second = rest.astype(bf16).astype(f32)
    return first, second, rest - second


def row_number(shape):
    return lax.broadcasted_iota(jnp.int32, shape, len(shape) - 2)


def store_scaled(fields_ref, direction, scale):
    scaled = jnp.where(row_number(direction.shape) < rows_here, direction * scale, 0.0)
    blocks = direction.shape[0]
    doubled = jnp.concatenate([scaled, jnp.zeros_like(scaled)], axis=1)
    fields_ref[0:blocks] = doubled.astype(bf16)
    fields_ref[blocks] = jnp.zeros((16, BLOCK), bf16)


def multiply(owner_ref, entry_ref, count, tiles_ref, fields_ref, totals_ref):
    totals_ref[...] = jnp.zeros_like(totals_ref)

    def step(number, carry):
        products = []
        for part in range(chunks_per_step):
            fields = []
            tiles = []
            for slot in range(chunk):
                entry = entry_ref[(number * chunks_per_step + part) * chunk + slot]
                fields.append(fields_ref[entry & 65535])
                tiles.append(tiles_ref[entry >> 16])
            product = jnp.dot(
                jnp.concatenate(fields, axis=1),
                jnp.concatenate(tiles, axis=0),
                preferred_element_type=f32,
            )
            products.append(product[0:8])
        for part in range(chunks_per_step):
            totals_ref[owner_ref[number * chunks_per_step + part]] += products[part]
        return carry

    lax.fori_loop(0, (count + chunks_per_step - 1) // chunks_per_step, step, 0)


def first_kernel(
    plan,
    core_ref,
    count_ref,
    pair_ref,
    gathered_ref,
    tiles_ref,
    product_ref,
    left_ref,
    right_ref,
    fields_ref,
    totals_ref,
    *stages,
):
    _, width, steps, _ = plan
    blocks = gathered_ref.shape[0]
    core = core_ref[0]
    slots = width * steps
    highest = jnp.max(jnp.max(gathered_ref[...], axis=0), axis=1, keepdims=True)
    lowest = jnp.min(jnp.min(gathered_ref[...], axis=0), axis=1, keepdims=True)
    centre = 0.5 * (highest + lowest)

    def prepare(block, carry):
        row = row_number((8, BLOCK))
        is_coordinate = (row >= 4) & (row < 7)
        shifted = jnp.where(is_coordinate, gathered_ref[block] - centre, 0.0)
        squared = jnp.sum(shifted * shifted, axis=0, keepdims=True)
        left = jnp.where(row == 7, 1.0, jnp.where(row == 0, squared, shifted))
        right = jnp.where(row == 7, squared, jnp.where(row == 0, 1.0, -2.0 * shifted))
        left_1, left_2, left_3 = three_parts(left)
        right_1, right_2, right_3 = three_parts(right)
        left_all = jnp.concatenate([left_1, left_1, left_2, left_2, left_1, left_3], axis=0)
        right_all = jnp.concatenate([right_1, right_2, right_1, right_2, right_3, right_1], axis=0)
        left_ref[block] = left_all.T.astype(bf16)
        right_ref[block] = right_all.astype(bf16)
        return carry

    lax.fori_loop(0, blocks, prepare, 0, unroll=8)
    store_scaled(fields_ref, gathered_ref[...], gathered_ref[:, 7:8, :])
    totals_ref[...] = jnp.zeros_like(totals_ref)

    def make_tiles(step, stage):
        for slot in range(width):
            number = step * width + slot
            low, high, _, _ = entry_blocks(plan, blocks, core, pair_ref, number)
            squared = jnp.dot(left_ref[low], right_ref[high], preferred_element_type=f32)
            tile = radial(squared)
            turned = tile.T
            tiles_ref[number] = tile
            tiles_ref[slots + number] = turned
            stage[0][slot] = tile
            stage[1][slot] = turned

    def use_tiles(step, stage):
        products = []
        for slot in range(width):
            number = step * width + slot
            low, high, usable, pair_usable = entry_blocks(plan, blocks, core, pair_ref, number)
            usable = usable & (number >= 0)
            pair_usable = pair_usable & (number >= 0)
            ways = (
                (jnp.where(usable, low, blocks), jnp.where(usable, high, blocks)),
                (jnp.where(pair_usable, high, blocks), jnp.where(pair_usable, low, blocks)),
            )
            for (source, target), tiles in zip(ways, stage):
                product = jnp.dot(fields_ref[source], tiles[slot], preferred_element_type=f32)
                products.append((target, product[0:8]))
        for target, product in products:
            totals_ref[target] += product

    even, odd = stages[0:2], stages[2:4]

    def both_steps(pair, carry):
        make_tiles(2 * pair, even)
        use_tiles(2 * pair - 1, odd)
        make_tiles(2 * pair + 1, odd)
        use_tiles(2 * pair, even)
        return carry

    lax.fori_loop(0, steps // 2, both_steps, 0)
    use_tiles(steps - 1, odd)
    product_ref[...] = totals_ref[0:blocks]


def total(values):
    return jnp.sum(jnp.sum(values, axis=0), axis=1, keepdims=True)[None]


def advance(mine_ref, other_ref, scale, direction, residual):
    row = row_number((1, 8, 1))
    image = nugget * direction + scale * (mine_ref[...] + other_ref[...])
    norm_now = total(residual * residual)
    along = total(direction * image)
    alpha = norm_now / jnp.where(row < rows_here, along, 1.0)
    return alpha * direction, residual - alpha * image, norm_now


def next_kernel(
    first,
    owner_ref,
    entry_ref,
    count_ref,
    gathered_ref,
    mine_ref,
    other_ref,
    *rest,
):
    if first:
        tiles_ref, product_ref, state_out_ref, fields_ref, totals_ref = rest
        row = row_number(gathered_ref.shape)
        direction = jnp.where(row < rows_here, gathered_ref[...], 0.0)
        residual = direction
    else:
        state_ref, tiles_ref, product_ref, state_out_ref, fields_ref, totals_ref = rest
        direction = state_ref[2]
        residual = state_ref[1]
    scale = gathered_ref[:, 7:8, :]
    moved, residual, norm_now = advance(mine_ref, other_ref, scale, direction, residual)
    norm_next = total(residual * residual)
    row = row_number((1, 8, 1))
    beta = norm_next / jnp.where(row < rows_here, norm_now, 1.0)
    direction = residual + beta * direction
    state_out_ref[0] = moved if first else state_ref[0] + moved
    state_out_ref[1] = residual
    state_out_ref[2] = direction
    store_scaled(fields_ref, direction, scale)
    multiply(owner_ref, entry_ref, count_ref[0], tiles_ref, fields_ref, totals_ref)
    product_ref[...] = totals_ref[0 : gathered_ref.shape[0]]


def last_kernel(core_ref, gathered_ref, mine_ref, other_ref, state_ref, result_ref):
    scale = gathered_ref[:, 7:8, :]
    moved, residual, _ = advance(mine_ref, other_ref, scale, state_ref[2], state_ref[1])
    chosen = jnp.where(core_ref[0] == 0, state_ref[0] + moved, residual)
    result_ref[...] = chosen[:, 0:rows_here, :]


def by_realizations(point_data, right_side, pair_list):
    col_devices = lax.axis_size("col")
    devices = lax.axis_size("row") * col_devices
    chips = devices // 2
    blocks_here = point_data.shape[1] // BLOCK
    blocks = blocks_here * devices
    core = lax.rem(lax.axis_index("col"), 2).astype(jnp.int32).reshape(1)
    axes = ("row", "col")
    vector = pl.BlockSpec(memory_space=pltpu.VMEM)
    scalar = pl.BlockSpec(memory_space=pltpu.SMEM)
    plan = tile_schedule(pair_list.shape[1], blocks)
    half, width, steps, chunks = plan
    slots = width * steps

    limits = pltpu.CompilerParams(vmem_limit_bytes=kernel_bytes)
    outgoing = pl.pallas_call(
        packing_kernel,
        out_shape=jax.ShapeDtypeStruct((devices, blocks_here, 8, BLOCK), f32),
        in_specs=[pl.BlockSpec(memory_space=pltpu.HBM)] * 2,
        out_specs=vector,
        scratch_shapes=[
            pltpu.VMEM(point_data.shape, f32),
            pltpu.VMEM(right_side.shape, f32),
            pltpu.SemaphoreType.DMA((2,)),
        ],
        compiler_params=limits,
    )(
        pltpu.with_memory_space_constraint(point_data, pltpu.HBM),
        pltpu.with_memory_space_constraint(right_side, pltpu.HBM),
    )
    owner, entry, count = pl.pallas_call(
        functools.partial(listing_kernel, plan, blocks),
        out_shape=(
            jax.ShapeDtypeStruct((chunks + 8,), jnp.int32),
            jax.ShapeDtypeStruct((chunks * chunk + 8,), jnp.int32),
            jax.ShapeDtypeStruct((1,), jnp.int32),
        ),
        in_specs=[scalar, scalar],
        out_specs=(scalar, scalar, scalar),
        scratch_shapes=[pltpu.SMEM((blocks + 8,), jnp.int32)] * 2,
        cost_estimate=pl.CostEstimate(flops=8_000_000_000, bytes_accessed=20_000_000, transcendentals=0),
        compiler_params=limits,
    )(core, pair_list)
    gathered = lax.all_to_all(outgoing, axes, 0, 0, tiled=True).reshape(blocks, 8, BLOCK)

    field_shape = jax.ShapeDtypeStruct((blocks, 8, BLOCK), f32)
    state_shape = jax.ShapeDtypeStruct((3, blocks, 8, BLOCK), f32)
    work = [pltpu.VMEM((blocks + 1, 16, BLOCK), bf16), pltpu.VMEM((blocks + 1, 8, BLOCK), f32)]
    stage = pltpu.VMEM((width, BLOCK, BLOCK), bf16)
    tiles, mine = pl.pallas_call(
        functools.partial(first_kernel, plan),
        out_shape=(pltpu.VMEM((2 * slots, BLOCK, BLOCK), bf16), field_shape),
        in_specs=[scalar, scalar, scalar, vector],
        out_specs=(vector, vector),
        scratch_shapes=[
            pltpu.VMEM((blocks, BLOCK, 48), bf16),
            pltpu.VMEM((blocks, 48, BLOCK), bf16),
            *work,
            *[stage] * 4,
        ],
        compiler_params=limits,
    )(core, count, pair_list, gathered)
    tiles = pltpu.with_memory_space_constraint(tiles, pltpu.VMEM)
    swap = [(place, place ^ 1) for place in range(col_devices)]
    state = None
    for step in range(1, ITERS):
        other = lax.ppermute(mine, "col", swap)
        first = step == 1
        carried = () if first else (state,)
        mine, state = pl.pallas_call(
            functools.partial(next_kernel, first),
            out_shape=(field_shape, state_shape),
            in_specs=[scalar, scalar, scalar] + [vector] * (4 + len(carried)),
            out_specs=(vector, vector),
            scratch_shapes=work,
            compiler_params=limits,
        )(owner, entry, count, gathered, mine, other, *carried, tiles)
    other = lax.ppermute(mine, "col", swap)
    result = pl.pallas_call(
        last_kernel,
        out_shape=jax.ShapeDtypeStruct((blocks, rows_here, BLOCK), f32),
        in_specs=[scalar] + [vector] * 4,
        out_specs=vector,
        compiler_params=limits,
    )(core, gathered, mine, other, state)
    result = result.reshape(devices, blocks_here, rows_here, BLOCK)
    received = lax.all_to_all(result, axes, 0, 0, tiled=True)
    received = received.reshape(chips, 2, blocks_here, rows_here, BLOCK)
    received = received.transpose(1, 0, 3, 2, 4).reshape(2, right_side.shape[0], -1)
    return received[0], received[1]


def per_device(point_data, right_side, pair_list):
    col_devices = lax.axis_size("col")
    devices = lax.axis_size("row") * col_devices
    blocks = point_data.shape[1] // BLOCK * devices
    _, width, steps, _ = tile_schedule(pair_list.shape[1], blocks)
    tile_bytes = 2 * width * steps * BLOCK * BLOCK * 2
    paired = col_devices % 2 == 0 and blocks % 2 == 0
    if paired and right_side.shape[0] == rows_here * (devices // 2) and tile_bytes <= tile_bytes_limit:
        return by_realizations(point_data, right_side, pair_list)
    return by_points(point_data, right_side, pair_list)


def solution(mesh):
    placed = (P(None, ("row", "col")), P(None, ("row", "col")), P())
    return jax.shard_map(
        per_device,
        mesh=mesh,
        in_specs=placed,
        out_specs=(P(None, ("row", "col")), P(None, ("row", "col"))),
        check_vma=False,
    )
```

```python
import functools
import jax
import jax.numpy as jnp
from jax import lax
from jax.experimental import pallas as pl
from jax.experimental.pallas import tpu as pltpu
from jax.sharding import PartitionSpec as P

BLOCK = 128
ITERS = 3


long_range = 1.0
short_range = 0.35
nugget = 1.0
tiles_per_step = 8
rows_here = 4
chunk_bits = 2
chunk = 1 << chunk_bits
chunks_per_step = 16
tile_bytes_limit = 24 * 2**20
kernel_bytes = 12 * 2**20
f32 = jnp.float32
bf16 = jnp.bfloat16


def wendland(distance, reach):
    scaled = distance / reach
    remain = jnp.maximum(1.0 - scaled, 0.0)
    square = remain * remain
    return square * square * (4.0 * scaled + 1.0)


def covariance_tiles(row_points, column_points):
    delta_x = row_points[:, 0, :, None] - column_points[:, 0, None, :]
    delta_y = row_points[:, 1, :, None] - column_points[:, 1, None, :]
    delta_z = row_points[:, 2, :, None] - column_points[:, 2, None, :]
    distance = jnp.sqrt(delta_x * delta_x + delta_y * delta_y + delta_z * delta_z)
    kernel = wendland(distance, long_range) + wendland(distance, short_range)
    return row_points[:, 3, :, None] * kernel * column_points[:, 3, None, :]


def as_blocks(points):
    return points.reshape(4, -1, BLOCK).transpose(1, 0, 2)


def by_points(point_data, right_side, pair_list):
    col_devices = lax.axis_size("col")
    my_row = lax.axis_index("row")
    my_column = lax.axis_index("col")
    points = point_data.shape[1]
    blocks_here = points // BLOCK
    realizations = right_side.shape[0]
    own_blocks = as_blocks(point_data)
    row_blocks = as_blocks(lax.all_gather(point_data, "col", axis=1, tiled=True))
    column_blocks = as_blocks(lax.all_gather(point_data, "row", axis=1, tiled=True))
    row_count = row_blocks.shape[0]
    column_count = column_blocks.shape[0]
    lower_block = pair_list[0]
    upper_block = pair_list[1]
    this_device = my_row * col_devices + my_column
    device_of = (
        lower_block // blocks_here // col_devices * col_devices
        + upper_block // blocks_here % col_devices
    )
    roster_first_pair = jnp.sum((device_of < this_device).astype(jnp.int32))
    roster_pair_count = jnp.sum((device_of == this_device).astype(jnp.int32))
    roster_row_slot = jnp.clip(lower_block - my_row * col_devices * blocks_here, 0, row_count - 1)
    roster_column_slot = jnp.clip(
        upper_block // blocks_here // col_devices * blocks_here + upper_block % blocks_here,
        0,
        column_count - 1,
    )
    roster_step_count = (roster_pair_count + tiles_per_step - 1) // tiles_per_step
    plan = (
        roster_first_pair,
        roster_pair_count,
        roster_row_slot,
        roster_column_slot,
        roster_step_count,
        lower_block.shape[0],
    )
    first_pair, pair_count, row_slot, column_slot, step_count, listed = plan
    own_tiles = covariance_tiles(own_blocks, own_blocks).astype(jnp.bfloat16)

    def pick_tiles(step):
        offsets = step * tiles_per_step + jnp.arange(tiles_per_step)
        usable = offsets < pair_count
        picked = jnp.minimum(first_pair + offsets, listed - 1)
        row_pick = row_slot[picked]
        column_pick = column_slot[picked]
        tiles_now = covariance_tiles(row_blocks[row_pick], column_blocks[column_pick])
        tiles_now = jnp.where(usable[:, None, None], tiles_now, 0.0).astype(jnp.bfloat16)
        return (tiles_now, row_pick, column_pick)

    def inner(operands):
        stacked = jnp.stack(
            [jnp.sum(one_side * other_side, axis=1) for one_side, other_side in operands]
        )
        return lax.psum(stacked, ("row", "col"))

    solution = jnp.zeros_like(right_side)
    residual = right_side
    direction = right_side
    norm_now = inner(((residual, residual),))[0]
    for step in range(ITERS):
        rounded = direction.astype(jnp.bfloat16)
        product_row_direction = lax.all_gather(rounded, "col", axis=1, tiled=True)
        product_column_direction = lax.all_gather(rounded, "row", axis=1, tiled=True)
        row_direction = product_row_direction
        column_direction = product_column_direction
        row_direction = row_direction.reshape(realizations, row_count, BLOCK)
        column_direction = column_direction.reshape(realizations, column_count, BLOCK)

        def add_step(step, totals):
            into_rows, into_columns = totals
            tiles_now, row_pick, column_pick = pick_tiles(step)
            to_rows = jnp.einsum(
                "tij,ctj->cti",
                tiles_now,
                column_direction[:, column_pick],
                preferred_element_type=jnp.float32,
            )
            to_columns = jnp.einsum(
                "tij,cti->ctj",
                tiles_now,
                row_direction[:, row_pick],
                preferred_element_type=jnp.float32,
            )
            return (
                into_rows.at[:, row_pick].add(to_rows),
                into_columns.at[:, column_pick].add(to_columns),
            )

        empty_rows = jnp.zeros((realizations, row_count, BLOCK), jnp.float32)
        empty_columns = jnp.zeros((realizations, column_count, BLOCK), jnp.float32)
        into_rows, into_columns = lax.fori_loop(
            0, step_count, add_step, (empty_rows, empty_columns)
        )
        product_into_rows = into_rows.reshape(realizations, -1)
        product_into_columns = into_columns.reshape(realizations, -1)
        from_rows = lax.psum_scatter(product_into_rows, "col", scatter_dimension=1, tiled=True)
        from_columns = lax.psum_scatter(
            product_into_columns.astype(jnp.bfloat16), "row", scatter_dimension=1, tiled=True
        ).astype(jnp.float32)
        diagonal = jnp.einsum(
            "tij,ctj->cti",
            own_tiles,
            rounded.reshape(realizations, blocks_here, BLOCK),
            preferred_element_type=jnp.float32,
        )
        image = (
            nugget * direction + diagonal.reshape(realizations, points) + from_rows + from_columns
        )
        alpha = norm_now / inner(((direction, image),))[0]
        solution = solution + alpha[:, None] * direction
        residual = residual - alpha[:, None] * image
        if step + 1 < ITERS:
            norm_next = inner(((residual, residual),))[0]
            direction = residual + (norm_next / norm_now)[:, None] * direction
            norm_now = norm_next
    return (solution, residual)


def tile_schedule(listed, blocks):
    half = (listed + 1) // 2
    entries = half + blocks // 2
    sizes = range(12, 21)
    width = min(sizes, key=lambda size: (-(-entries // (2 * size)) * size, -size))
    steps = -(-entries // (2 * width)) * 2
    longest = (2 * half + blocks // 2 + 3 * blocks) // chunk
    chunks = -(-longest // chunks_per_step) * chunks_per_step + chunks_per_step
    return half, width, steps, chunks


def packing_kernel(point_hbm, field_hbm, outgoing_ref, point_ref, field_ref, arrived):
    devices, blocks_here = outgoing_ref.shape[0:2]
    copies = (
        pltpu.make_async_copy(point_hbm, point_ref, arrived.at[0]),
        pltpu.make_async_copy(field_hbm, field_ref, arrived.at[1]),
    )
    for copy in copies:
        copy.start()
    for copy in copies:
        copy.wait()
    for chip in range(devices // 2):
        for block in range(blocks_here):
            place = pl.ds(block * BLOCK, BLOCK)
            fields = field_ref[pl.ds(chip * rows_here, rows_here), place]
            both = jnp.concatenate([fields, point_ref[:, place]], axis=0)
            outgoing_ref[2 * chip, block] = both
            outgoing_ref[2 * chip + 1, block] = both


def entry_blocks(plan, blocks, core, pair_ref, number):
    half = plan[0]
    listed = pair_ref.shape[1]
    pair = core * half + number
    is_pair = number < half
    pair_usable = is_pair & (pair < listed)
    usable = pair_usable | ((number >= half) & (number < half + blocks // 2))
    safe = jnp.minimum(pair, listed - 1)
    own = jnp.minimum(core * (blocks // 2) + number - half, blocks - 1)
    low = jnp.where(is_pair, pair_ref[0, safe], own)
    high = jnp.where(is_pair, pair_ref[1, safe], own)
    return low, high, usable, pair_usable


def listing_kernel(plan, blocks, core_ref, pair_ref, owner_ref, entry_ref, count_ref, open_ref):
    half, width, steps, chunks = plan
    listed = pair_ref.shape[1]
    core = core_ref[0]
    slots = width * steps

    def clear(block, carry):
        open_ref[block] = 0
        return carry

    def pad(place, carry):
        entry_ref[place] = blocks
        return carry

    lax.fori_loop(0, blocks, clear, 0, unroll=16)
    lax.fori_loop(0, chunks * chunk, pad, 0, unroll=16)

    def append(block, entry, used):
        place = open_ref[block]
        fresh = (place & (chunk - 1)) == 0
        place = jnp.where(fresh, used, place)
        open_ref[block] = place + 1
        entry_ref[place] = entry
        owner_ref[place >> chunk_bits] = block
        return jnp.where(fresh, used + chunk, used)

    def list_pair(number, used):
        low = pair_ref[0, core * half + number]
        high = pair_ref[1, core * half + number]
        used = append(high, number * 65536 + low, used)
        return append(low, (slots + number) * 65536 + high, used)

    def list_diagonal(number, used):
        block = core * (blocks // 2) + number
        return append(block, (half + number) * 65536 + block, used)

    used = lax.fori_loop(0, listed // 2, list_pair, 0, unroll=8)
    if listed % 2:
        used = lax.fori_loop(half - 1, half - core, list_pair, used)
    used = lax.fori_loop(0, blocks // 2, list_diagonal, used, unroll=8)
    used = used >> chunk_bits
    count_ref[0] = used
    for part in range(chunks_per_step):
        owner_ref[used + part] = blocks


def radial(squared):
    squared = jnp.maximum(squared, 1e-30)
    distance = squared * lax.rsqrt(squared)
    near = jnp.maximum(1.0 - distance * (1.0 / long_range), 0.0)
    near_square = near * near
    wide = near_square * near_square * (1.25 - near)
    close = jnp.maximum(1.0 - distance * (1.0 / short_range), 0.0).astype(bf16)
    close_square = close * close
    narrow = close_square * close_square * (jnp.asarray(1.25, bf16) - close)
    return wide.astype(bf16) + narrow


def three_parts(values):
    first = values.astype(bf16).astype(f32)
    rest = values - first
    second = rest.astype(bf16).astype(f32)
    return first, second, rest - second


def row_number(shape):
    return lax.broadcasted_iota(jnp.int32, shape, len(shape) - 2)


def store_scaled(fields_ref, direction, scale):
    scaled = jnp.where(row_number(direction.shape) < rows_here, direction * (4.0 * scale), 0.0)
    blocks = direction.shape[0]
    doubled = jnp.concatenate([scaled, jnp.zeros_like(scaled)], axis=1)
    fields_ref[0:blocks] = doubled.astype(bf16)
    fields_ref[blocks] = jnp.zeros((16, BLOCK), bf16)


def multiply(owner_ref, entry_ref, count, tiles_ref, fields_ref, totals_ref):
    totals_ref[...] = jnp.zeros_like(totals_ref)

    def step(number, carry):
        products = []
        for part in range(chunks_per_step):
            fields = []
            tiles = []
            for slot in range(chunk):
                entry = entry_ref[(number * chunks_per_step + part) * chunk + slot]
                fields.append(fields_ref[entry & 65535])
                tiles.append(tiles_ref[entry >> 16])
            product = jnp.dot(
                jnp.concatenate(fields, axis=1),
                jnp.concatenate(tiles, axis=0),
                preferred_element_type=f32,
            )
            products.append(product[0:8])
        for part in range(chunks_per_step):
            totals_ref[owner_ref[number * chunks_per_step + part]] += products[part]
        return carry

    lax.fori_loop(0, (count + chunks_per_step - 1) // chunks_per_step, step, 0)


def first_kernel(
    plan,
    core_ref,
    count_ref,
    pair_ref,
    gathered_ref,
    tiles_ref,
    product_ref,
    left_ref,
    right_ref,
    fields_ref,
    totals_ref,
    *stages,
):
    _, width, steps, _ = plan
    blocks = gathered_ref.shape[0]
    core = core_ref[0]
    slots = width * steps
    highest = jnp.max(jnp.max(gathered_ref[...], axis=0), axis=1, keepdims=True)
    lowest = jnp.min(jnp.min(gathered_ref[...], axis=0), axis=1, keepdims=True)
    centre = 0.5 * (highest + lowest)

    def prepare(block, carry):
        row = row_number((8, BLOCK))
        is_coordinate = (row >= 4) & (row < 7)
        shifted = jnp.where(is_coordinate, gathered_ref[block] - centre, 0.0)
        squared = jnp.sum(shifted * shifted, axis=0, keepdims=True)
        left = jnp.where(row == 7, 1.0, jnp.where(row == 0, squared, shifted))
        right = jnp.where(row == 7, squared, jnp.where(row == 0, 1.0, -2.0 * shifted))
        left_1, left_2, left_3 = three_parts(left)
        right_1, right_2, right_3 = three_parts(right)
        left_all = jnp.concatenate([left_1, left_1, left_2, left_2, left_1, left_3], axis=0)
        right_all = jnp.concatenate([right_1, right_2, right_1, right_2, right_3, right_1], axis=0)
        left_ref[block] = left_all.T.astype(bf16)
        right_ref[block] = right_all.astype(bf16)
        return carry

    lax.fori_loop(0, blocks, prepare, 0, unroll=8)
    store_scaled(fields_ref, gathered_ref[...], gathered_ref[:, 7:8, :])
    totals_ref[...] = jnp.zeros_like(totals_ref)

    def make_tile(step, slot, stage):
        number = step * width + slot
        low, high, _, _ = entry_blocks(plan, blocks, core, pair_ref, number)
        squared = jnp.dot(left_ref[low], right_ref[high], preferred_element_type=f32)
        tile = radial(squared)
        turned = tile.T
        tiles_ref[number] = tile
        tiles_ref[slots + number] = turned
        stage[0][slot] = tile
        stage[1][slot] = turned

    def use_tile(step, slot, stage):
        number = step * width + slot
        low, high, usable, pair_usable = entry_blocks(plan, blocks, core, pair_ref, number)
        usable = usable & (number >= 0)
        pair_usable = pair_usable & (number >= 0)
        ways = (
            (jnp.where(usable, low, blocks), jnp.where(usable, high, blocks)),
            (jnp.where(pair_usable, high, blocks), jnp.where(pair_usable, low, blocks)),
        )
        products = []
        for (source, target), tiles in zip(ways, stage):
            product = jnp.dot(fields_ref[source], tiles[slot], preferred_element_type=f32)
            products.append((target, product[0:8]))
        return products

    def add_products(products):
        for target, product in products:
            totals_ref[target] += product

    def use_tiles(step, stage):
        for slot in range(width):
            add_products(use_tile(step, slot, stage))

    def both(step, new_stage, old_stage):
        waiting = []
        for slot in range(width):
            make_tile(step, slot, new_stage)
            waiting.append(use_tile(step - 1, slot, old_stage))
            if len(waiting) > 2:
                add_products(waiting.pop(0))
        for products in waiting:
            add_products(products)

    even, odd = stages[0:2], stages[2:4]

    def both_steps(pair, carry):
        both(2 * pair, even, odd)
        both(2 * pair + 1, odd, even)
        return carry

    lax.fori_loop(0, steps // 2, both_steps, 0)
    use_tiles(steps - 1, odd)
    product_ref[...] = totals_ref[0:blocks]


def total(values):
    return jnp.sum(jnp.sum(values, axis=0), axis=1, keepdims=True)[None]


def advance(mine_ref, other_ref, scale, direction, residual):
    row = row_number((1, 8, 1))
    image = nugget * direction + scale * (mine_ref[...] + other_ref[...])
    norm_now = total(residual * residual)
    along = total(direction * image)
    alpha = norm_now / jnp.where(row < rows_here, along, 1.0)
    return alpha * direction, residual - alpha * image, norm_now


def next_kernel(
    first,
    owner_ref,
    entry_ref,
    count_ref,
    gathered_ref,
    mine_ref,
    other_ref,
    *rest,
):
    if first:
        tiles_ref, product_ref, state_out_ref, fields_ref, totals_ref = rest
        row = row_number(gathered_ref.shape)
        direction = jnp.where(row < rows_here, gathered_ref[...], 0.0)
        residual = direction
    else:
        state_ref, tiles_ref, product_ref, state_out_ref, fields_ref, totals_ref = rest
        direction = state_ref[2]
        residual = state_ref[1]
    scale = gathered_ref[:, 7:8, :]
    moved, residual, norm_now = advance(mine_ref, other_ref, scale, direction, residual)
    norm_next = total(residual * residual)
    row = row_number((1, 8, 1))
    beta = norm_next / jnp.where(row < rows_here, norm_now, 1.0)
    direction = residual + beta * direction
    state_out_ref[0] = moved if first else state_ref[0] + moved
    state_out_ref[1] = residual
    state_out_ref[2] = direction
    store_scaled(fields_ref, direction, scale)
    multiply(owner_ref, entry_ref, count_ref[0], tiles_ref, fields_ref, totals_ref)
    product_ref[...] = totals_ref[0 : gathered_ref.shape[0]]


def last_kernel(core_ref, gathered_ref, mine_ref, other_ref, state_ref, result_ref):
    scale = gathered_ref[:, 7:8, :]
    moved, residual, _ = advance(mine_ref, other_ref, scale, state_ref[2], state_ref[1])
    chosen = jnp.where(core_ref[0] == 0, state_ref[0] + moved, residual)
    result_ref[...] = chosen[:, 0:rows_here, :]


def by_realizations(point_data, right_side, pair_list):
    col_devices = lax.axis_size("col")
    devices = lax.axis_size("row") * col_devices
    chips = devices // 2
    blocks_here = point_data.shape[1] // BLOCK
    blocks = blocks_here * devices
    core = lax.rem(lax.axis_index("col"), 2).astype(jnp.int32).reshape(1)
    axes = ("row", "col")
    vector = pl.BlockSpec(memory_space=pltpu.VMEM)
    scalar = pl.BlockSpec(memory_space=pltpu.SMEM)
    plan = tile_schedule(pair_list.shape[1], blocks)
    half, width, steps, chunks = plan
    slots = width * steps

    limits = pltpu.CompilerParams(vmem_limit_bytes=kernel_bytes)
    outgoing = pl.pallas_call(
        packing_kernel,
        out_shape=jax.ShapeDtypeStruct((devices, blocks_here, 8, BLOCK), f32),
        in_specs=[pl.BlockSpec(memory_space=pltpu.HBM)] * 2,
        out_specs=vector,
        scratch_shapes=[
            pltpu.VMEM(point_data.shape, f32),
            pltpu.VMEM(right_side.shape, f32),
            pltpu.SemaphoreType.DMA((2,)),
        ],
        compiler_params=limits,
    )(
        pltpu.with_memory_space_constraint(point_data, pltpu.HBM),
        pltpu.with_memory_space_constraint(right_side, pltpu.HBM),
    )
    owner, entry, count = pl.pallas_call(
        functools.partial(listing_kernel, plan, blocks),
        out_shape=(
            jax.ShapeDtypeStruct((chunks + 8,), jnp.int32),
            jax.ShapeDtypeStruct((chunks * chunk + 8,), jnp.int32),
            jax.ShapeDtypeStruct((1,), jnp.int32),
        ),
        in_specs=[scalar, scalar],
        out_specs=(scalar, scalar, scalar),
        scratch_shapes=[pltpu.SMEM((blocks,), jnp.int32)],
        cost_estimate=pl.CostEstimate(flops=8_000_000_000, bytes_accessed=20_000_000, transcendentals=0),
        compiler_params=limits,
    )(core, pair_list)
    gathered = lax.all_to_all(outgoing, axes, 0, 0, tiled=True).reshape(blocks, 8, BLOCK)

    field_shape = jax.ShapeDtypeStruct((blocks, 8, BLOCK), f32)
    state_shape = jax.ShapeDtypeStruct((3, blocks, 8, BLOCK), f32)
    work = [pltpu.VMEM((blocks + 1, 16, BLOCK), bf16), pltpu.VMEM((blocks + 1, 8, BLOCK), f32)]
    stage = pltpu.VMEM((width, BLOCK, BLOCK), bf16)
    tiles, mine = pl.pallas_call(
        functools.partial(first_kernel, plan),
        out_shape=(pltpu.VMEM((2 * slots, BLOCK, BLOCK), bf16), field_shape),
        in_specs=[scalar, scalar, scalar, vector],
        out_specs=(vector, vector),
        scratch_shapes=[
            pltpu.VMEM((blocks, BLOCK, 48), bf16),
            pltpu.VMEM((blocks, 48, BLOCK), bf16),
            *work,
            *[stage] * 4,
        ],
        compiler_params=limits,
    )(core, count, pair_list, gathered)
    tiles = pltpu.with_memory_space_constraint(tiles, pltpu.VMEM)
    swap = [(place, place ^ 1) for place in range(col_devices)]
    state = None
    for step in range(1, ITERS):
        other = lax.ppermute(mine, "col", swap)
        first = step == 1
        carried = () if first else (state,)
        mine, state = pl.pallas_call(
            functools.partial(next_kernel, first),
            out_shape=(field_shape, state_shape),
            in_specs=[scalar, scalar, scalar] + [vector] * (4 + len(carried)),
            out_specs=(vector, vector),
            scratch_shapes=work,
            compiler_params=limits,
        )(owner, entry, count, gathered, mine, other, *carried, tiles)
    other = lax.ppermute(mine, "col", swap)
    result = pl.pallas_call(
        last_kernel,
        out_shape=jax.ShapeDtypeStruct((blocks, rows_here, BLOCK), f32),
        in_specs=[scalar] + [vector] * 4,
        out_specs=vector,
        compiler_params=limits,
    )(core, gathered, mine, other, state)
    result = result.reshape(devices, blocks_here, rows_here, BLOCK)
    received = lax.all_to_all(result, axes, 0, 0, tiled=True)
    received = received.reshape(chips, 2, blocks_here, rows_here, BLOCK)
    received = received.transpose(1, 0, 3, 2, 4).reshape(2, right_side.shape[0], -1)
    return received[0], received[1]


def per_device(point_data, right_side, pair_list):
    col_devices = lax.axis_size("col")
    devices = lax.axis_size("row") * col_devices
    blocks = point_data.shape[1] // BLOCK * devices
    _, width, steps, _ = tile_schedule(pair_list.shape[1], blocks)
    tile_bytes = 2 * width * steps * BLOCK * BLOCK * 2
    paired = col_devices % 2 == 0 and blocks % 2 == 0
    if paired and right_side.shape[0] == rows_here * (devices // 2) and tile_bytes <= tile_bytes_limit:
        return by_realizations(point_data, right_side, pair_list)
    return by_points(point_data, right_side, pair_list)


def solution(mesh):
    placed = (P(None, ("row", "col")), P(None, ("row", "col")), P())
    return jax.shard_map(
        per_device,
        mesh=mesh,
        in_specs=placed,
        out_specs=(P(None, ("row", "col")), P(None, ("row", "col"))),
        check_vma=False,
    )
```

```python
import functools
import jax
import jax.numpy as jnp
from jax import lax
from jax.experimental import pallas as pl
from jax.experimental.pallas import tpu as pltpu
from jax.sharding import PartitionSpec as P

BLOCK = 128
ITERS = 3


long_range = 1.0
short_range = 0.35
nugget = 1.0
tiles_per_step = 8
rows_here = 4
chunk_bits = 2
chunk = 1 << chunk_bits
chunks_per_step = 32
tile_bytes_limit = 24 * 2**20
kernel_bytes = 12 * 2**20
f32 = jnp.float32
bf16 = jnp.bfloat16


def wendland(distance, reach):
    scaled = distance / reach
    remain = jnp.maximum(1.0 - scaled, 0.0)
    square = remain * remain
    return square * square * (4.0 * scaled + 1.0)


def covariance_tiles(row_points, column_points):
    delta_x = row_points[:, 0, :, None] - column_points[:, 0, None, :]
    delta_y = row_points[:, 1, :, None] - column_points[:, 1, None, :]
    delta_z = row_points[:, 2, :, None] - column_points[:, 2, None, :]
    distance = jnp.sqrt(delta_x * delta_x + delta_y * delta_y + delta_z * delta_z)
    kernel = wendland(distance, long_range) + wendland(distance, short_range)
    return row_points[:, 3, :, None] * kernel * column_points[:, 3, None, :]


def as_blocks(points):
    return points.reshape(4, -1, BLOCK).transpose(1, 0, 2)


def by_points(point_data, right_side, pair_list):
    col_devices = lax.axis_size("col")
    my_row = lax.axis_index("row")
    my_column = lax.axis_index("col")
    points = point_data.shape[1]
    blocks_here = points // BLOCK
    realizations = right_side.shape[0]
    own_blocks = as_blocks(point_data)
    row_blocks = as_blocks(lax.all_gather(point_data, "col", axis=1, tiled=True))
    column_blocks = as_blocks(lax.all_gather(point_data, "row", axis=1, tiled=True))
    row_count = row_blocks.shape[0]
    column_count = column_blocks.shape[0]
    lower_block = pair_list[0]
    upper_block = pair_list[1]
    this_device = my_row * col_devices + my_column
    device_of = (
        lower_block // blocks_here // col_devices * col_devices
        + upper_block // blocks_here % col_devices
    )
    roster_first_pair = jnp.sum((device_of < this_device).astype(jnp.int32))
    roster_pair_count = jnp.sum((device_of == this_device).astype(jnp.int32))
    roster_row_slot = jnp.clip(lower_block - my_row * col_devices * blocks_here, 0, row_count - 1)
    roster_column_slot = jnp.clip(
        upper_block // blocks_here // col_devices * blocks_here + upper_block % blocks_here,
        0,
        column_count - 1,
    )
    roster_step_count = (roster_pair_count + tiles_per_step - 1) // tiles_per_step
    plan = (
        roster_first_pair,
        roster_pair_count,
        roster_row_slot,
        roster_column_slot,
        roster_step_count,
        lower_block.shape[0],
    )
    first_pair, pair_count, row_slot, column_slot, step_count, listed = plan
    own_tiles = covariance_tiles(own_blocks, own_blocks).astype(jnp.bfloat16)

    def pick_tiles(step):
        offsets = step * tiles_per_step + jnp.arange(tiles_per_step)
        usable = offsets < pair_count
        picked = jnp.minimum(first_pair + offsets, listed - 1)
        row_pick = row_slot[picked]
        column_pick = column_slot[picked]
        tiles_now = covariance_tiles(row_blocks[row_pick], column_blocks[column_pick])
        tiles_now = jnp.where(usable[:, None, None], tiles_now, 0.0).astype(jnp.bfloat16)
        return (tiles_now, row_pick, column_pick)

    def inner(operands):
        stacked = jnp.stack(
            [jnp.sum(one_side * other_side, axis=1) for one_side, other_side in operands]
        )
        return lax.psum(stacked, ("row", "col"))

    solution = jnp.zeros_like(right_side)
    residual = right_side
    direction = right_side
    norm_now = inner(((residual, residual),))[0]
    for step in range(ITERS):
        rounded = direction.astype(jnp.bfloat16)
        product_row_direction = lax.all_gather(rounded, "col", axis=1, tiled=True)
        product_column_direction = lax.all_gather(rounded, "row", axis=1, tiled=True)
        row_direction = product_row_direction
        column_direction = product_column_direction
        row_direction = row_direction.reshape(realizations, row_count, BLOCK)
        column_direction = column_direction.reshape(realizations, column_count, BLOCK)

        def add_step(step, totals):
            into_rows, into_columns = totals
            tiles_now, row_pick, column_pick = pick_tiles(step)
            to_rows = jnp.einsum(
                "tij,ctj->cti",
                tiles_now,
                column_direction[:, column_pick],
                preferred_element_type=jnp.float32,
            )
            to_columns = jnp.einsum(
                "tij,cti->ctj",
                tiles_now,
                row_direction[:, row_pick],
                preferred_element_type=jnp.float32,
            )
            return (
                into_rows.at[:, row_pick].add(to_rows),
                into_columns.at[:, column_pick].add(to_columns),
            )

        empty_rows = jnp.zeros((realizations, row_count, BLOCK), jnp.float32)
        empty_columns = jnp.zeros((realizations, column_count, BLOCK), jnp.float32)
        into_rows, into_columns = lax.fori_loop(
            0, step_count, add_step, (empty_rows, empty_columns)
        )
        product_into_rows = into_rows.reshape(realizations, -1)
        product_into_columns = into_columns.reshape(realizations, -1)
        from_rows = lax.psum_scatter(product_into_rows, "col", scatter_dimension=1, tiled=True)
        from_columns = lax.psum_scatter(
            product_into_columns.astype(jnp.bfloat16), "row", scatter_dimension=1, tiled=True
        ).astype(jnp.float32)
        diagonal = jnp.einsum(
            "tij,ctj->cti",
            own_tiles,
            rounded.reshape(realizations, blocks_here, BLOCK),
            preferred_element_type=jnp.float32,
        )
        image = (
            nugget * direction + diagonal.reshape(realizations, points) + from_rows + from_columns
        )
        alpha = norm_now / inner(((direction, image),))[0]
        solution = solution + alpha[:, None] * direction
        residual = residual - alpha[:, None] * image
        if step + 1 < ITERS:
            norm_next = inner(((residual, residual),))[0]
            direction = residual + (norm_next / norm_now)[:, None] * direction
            norm_now = norm_next
    return (solution, residual)


def tile_schedule(listed, blocks):
    half = (listed + 1) // 2
    entries = half + blocks // 2
    sizes = range(12, 21)
    width = min(sizes, key=lambda size: (-(-entries // (2 * size)) * size, -size))
    steps = -(-entries // (2 * width)) * 2
    longest = (2 * half + blocks // 2 + 3 * blocks) // chunk
    chunks = -(-longest // chunks_per_step) * chunks_per_step + chunks_per_step
    return half, width, steps, chunks


def packing_kernel(point_hbm, field_hbm, outgoing_ref, point_ref, field_ref, arrived):
    devices, blocks_here = outgoing_ref.shape[0:2]
    copies = (
        pltpu.make_async_copy(point_hbm, point_ref, arrived.at[0]),
        pltpu.make_async_copy(field_hbm, field_ref, arrived.at[1]),
    )
    for copy in copies:
        copy.start()
    for copy in copies:
        copy.wait()
    for chip in range(devices // 2):
        for block in range(blocks_here):
            place = pl.ds(block * BLOCK, BLOCK)
            fields = field_ref[pl.ds(chip * rows_here, rows_here), place]
            both = jnp.concatenate([fields, point_ref[:, place]], axis=0)
            outgoing_ref[2 * chip, block] = both
            outgoing_ref[2 * chip + 1, block] = both


def listing_kernel(
    plan,
    blocks,
    core_ref,
    pair_ref,
    owner_ref,
    entry_ref,
    count_ref,
    low_ref,
    high_ref,
    open_ref,
):
    half, width, steps, chunks = plan
    listed = pair_ref.shape[1]
    core = core_ref[0]
    slots = width * steps

    def clear(block, carry):
        open_ref[block] = 0
        return carry

    def pad(place, carry):
        entry_ref[place] = blocks
        return carry

    lax.fori_loop(0, blocks, clear, 0, unroll=16)
    lax.fori_loop(0, chunks * chunk, pad, 0, unroll=16)

    def append(block, entry, used):
        place = open_ref[block]
        fresh = (place & (chunk - 1)) == 0
        place = jnp.where(fresh, used, place)
        open_ref[block] = place + 1
        entry_ref[place] = entry
        owner_ref[place >> chunk_bits] = block
        return jnp.where(fresh, used + chunk, used)

    def list_pair(number, used):
        low = pair_ref[0, core * half + number]
        high = pair_ref[1, core * half + number]
        low_ref[number] = low
        high_ref[number] = high
        used = append(high, number * 65536 + low, used)
        return append(low, (slots + number) * 65536 + high, used)

    def list_diagonal(number, used):
        block = core * (blocks // 2) + number
        low_ref[half + number] = block
        high_ref[half + number] = block
        return append(block, (half + number) * 65536 + block, used)

    low_ref[half - 1] = blocks
    high_ref[half - 1] = blocks
    for number in range(half + blocks // 2, slots):
        low_ref[number] = blocks
        high_ref[number] = blocks
    used = lax.fori_loop(0, listed // 2, list_pair, 0, unroll=8)
    if listed % 2:
        used = lax.fori_loop(half - 1, half - core, list_pair, used)
    used = lax.fori_loop(0, blocks // 2, list_diagonal, used, unroll=8)
    used = used >> chunk_bits
    count_ref[0] = used
    for part in range(chunks_per_step):
        owner_ref[used + part] = blocks


def radial(squared):
    squared = jnp.maximum(squared, 1e-30)
    distance = squared * lax.rsqrt(squared)
    near = jnp.maximum(1.0 - distance * (1.0 / long_range), 0.0)
    near_square = near * near
    wide = near_square * near_square * (1.25 - near)
    close = jnp.maximum(1.0 - distance * (1.0 / short_range), 0.0).astype(bf16)
    close_square = close * close
    narrow = close_square * close_square * (jnp.asarray(1.25, bf16) - close)
    return wide.astype(bf16) + narrow


def three_parts(values):
    first = values.astype(bf16).astype(f32)
    rest = values - first
    second = rest.astype(bf16).astype(f32)
    return first, second, rest - second


def row_number(shape):
    return lax.broadcasted_iota(jnp.int32, shape, len(shape) - 2)


def store_scaled(fields_ref, direction, scale):
    scaled = jnp.where(row_number(direction.shape) < rows_here, direction * (4.0 * scale), 0.0)
    blocks = direction.shape[0]
    doubled = jnp.concatenate([scaled, jnp.zeros_like(scaled)], axis=1)
    fields_ref[0:blocks] = doubled.astype(bf16)
    fields_ref[blocks] = jnp.zeros((16, BLOCK), bf16)


def multiply(owner_ref, entry_ref, count, tiles_ref, fields_ref, totals_ref):
    totals_ref[...] = jnp.zeros_like(totals_ref)

    def step(number, carry):
        products = []
        for part in range(chunks_per_step):
            fields = []
            tiles = []
            for slot in range(chunk):
                entry = entry_ref[(number * chunks_per_step + part) * chunk + slot]
                fields.append(fields_ref[entry & 65535])
                tiles.append(tiles_ref[entry >> 16])
            product = jnp.dot(
                jnp.concatenate(fields, axis=1),
                jnp.concatenate(tiles, axis=0),
                preferred_element_type=f32,
            )
            products.append(product[0:8])
        for part in range(chunks_per_step):
            totals_ref[owner_ref[number * chunks_per_step + part]] += products[part]
        return carry

    lax.fori_loop(0, (count + chunks_per_step - 1) // chunks_per_step, step, 0)


def first_kernel(
    plan,
    low_ref,
    high_ref,
    gathered_ref,
    tiles_ref,
    product_ref,
    left_ref,
    right_ref,
    fields_ref,
    totals_ref,
    *stages,
):
    half, width, steps, _ = plan
    blocks = gathered_ref.shape[0]
    slots = width * steps
    highest = jnp.max(jnp.max(gathered_ref[...], axis=0), axis=1, keepdims=True)
    lowest = jnp.min(jnp.min(gathered_ref[...], axis=0), axis=1, keepdims=True)
    centre = 0.5 * (highest + lowest)

    def prepare(block, carry):
        row = row_number((8, BLOCK))
        is_coordinate = (row >= 4) & (row < 7)
        shifted = jnp.where(is_coordinate, gathered_ref[block] - centre, 0.0)
        squared = jnp.sum(shifted * shifted, axis=0, keepdims=True)
        left = jnp.where(row == 7, 1.0, jnp.where(row == 0, squared, shifted))
        right = jnp.where(row == 7, squared, jnp.where(row == 0, 1.0, -2.0 * shifted))
        left_1, left_2, left_3 = three_parts(left)
        right_1, right_2, right_3 = three_parts(right)
        left_all = jnp.concatenate([left_1, left_1, left_2, left_2, left_1, left_3], axis=0)
        right_all = jnp.concatenate([right_1, right_2, right_1, right_2, right_3, right_1], axis=0)
        left_ref[block] = left_all.T.astype(bf16)
        right_ref[block] = right_all.astype(bf16)
        return carry

    lax.fori_loop(0, blocks, prepare, 0, unroll=8)
    left_ref[blocks] = jnp.zeros((BLOCK, 48), bf16)
    right_ref[blocks] = jnp.zeros((48, BLOCK), bf16)
    store_scaled(fields_ref, gathered_ref[...], gathered_ref[:, 7:8, :])
    totals_ref[...] = jnp.zeros_like(totals_ref)

    def square(step, slot):
        number = step * width + slot
        return jnp.dot(
            left_ref[low_ref[number]], right_ref[high_ref[number]], preferred_element_type=f32
        )

    def make_tile(step, slot, stage, squared):
        number = step * width + slot
        tile = radial(squared)
        turned = tile.T
        tiles_ref[number] = tile
        tiles_ref[slots + number] = turned
        stage[0][slot] = tile
        stage[1][slot] = turned

    def use_tile(step, slot, stage):
        number = step * width + slot
        made = jnp.maximum(number, 0)
        low = jnp.where(number >= 0, low_ref[made], blocks)
        high = jnp.where(number >= 0, high_ref[made], blocks)
        is_pair = number < half
        ways = (
            (low, high),
            (jnp.where(is_pair, high, blocks), jnp.where(is_pair, low, blocks)),
        )
        products = []
        for (source, target), tiles in zip(ways, stage):
            product = jnp.dot(fields_ref[source], tiles[slot], preferred_element_type=f32)
            products.append((target, product[0:8]))
        return products

    def add_products(products):
        for target, product in products:
            totals_ref[target] += product

    def use_tiles(step, stage):
        for slot in range(width):
            add_products(use_tile(step, slot, stage))

    def both(step, new_stage, old_stage):
        waiting = []
        ahead = square(step, 0)
        for slot in range(width):
            squared = ahead
            if slot + 1 < width:
                ahead = square(step, slot + 1)
            make_tile(step, slot, new_stage, squared)
            waiting.append(use_tile(step - 1, slot, old_stage))
            if len(waiting) > 2:
                add_products(waiting.pop(0))
        for products in waiting:
            add_products(products)

    even, odd = stages[0:2], stages[2:4]

    def both_steps(pair, carry):
        both(2 * pair, even, odd)
        both(2 * pair + 1, odd, even)
        return carry

    lax.fori_loop(0, steps // 2, both_steps, 0)
    use_tiles(steps - 1, odd)
    product_ref[...] = totals_ref[0:blocks]


def total(values):
    return jnp.sum(jnp.sum(values, axis=0), axis=1, keepdims=True)[None]


def advance(mine_ref, other_ref, scale, direction, residual):
    row = row_number((1, 8, 1))
    image = nugget * direction + scale * (mine_ref[...] + other_ref[...])
    norm_now = total(residual * residual)
    along = total(direction * image)
    alpha = norm_now / jnp.where(row < rows_here, along, 1.0)
    return alpha * direction, residual - alpha * image, norm_now


def next_kernel(
    first,
    owner_ref,
    entry_ref,
    count_ref,
    gathered_ref,
    mine_ref,
    other_ref,
    *rest,
):
    if first:
        tiles_ref, product_ref, state_out_ref, fields_ref, totals_ref = rest
        row = row_number(gathered_ref.shape)
        direction = jnp.where(row < rows_here, gathered_ref[...], 0.0)
        residual = direction
    else:
        state_ref, tiles_ref, product_ref, state_out_ref, fields_ref, totals_ref = rest
        direction = state_ref[2]
        residual = state_ref[1]
    scale = gathered_ref[:, 7:8, :]
    moved, residual, norm_now = advance(mine_ref, other_ref, scale, direction, residual)
    norm_next = total(residual * residual)
    row = row_number((1, 8, 1))
    beta = norm_next / jnp.where(row < rows_here, norm_now, 1.0)
    direction = residual + beta * direction
    state_out_ref[0] = moved if first else state_ref[0] + moved
    state_out_ref[1] = residual
    state_out_ref[2] = direction
    store_scaled(fields_ref, direction, scale)
    multiply(owner_ref, entry_ref, count_ref[0], tiles_ref, fields_ref, totals_ref)
    product_ref[...] = totals_ref[0 : gathered_ref.shape[0]]


def last_kernel(core_ref, gathered_ref, mine_ref, other_ref, state_ref, result_ref):
    scale = gathered_ref[:, 7:8, :]
    moved, residual, _ = advance(mine_ref, other_ref, scale, state_ref[2], state_ref[1])
    chosen = jnp.where(core_ref[0] == 0, state_ref[0] + moved, residual)
    result_ref[...] = chosen[:, 0:rows_here, :].astype(bf16)


def by_realizations(point_data, right_side, pair_list):
    col_devices = lax.axis_size("col")
    devices = lax.axis_size("row") * col_devices
    chips = devices // 2
    blocks_here = point_data.shape[1] // BLOCK
    blocks = blocks_here * devices
    core = lax.rem(lax.axis_index("col"), 2).astype(jnp.int32).reshape(1)
    axes = ("row", "col")
    vector = pl.BlockSpec(memory_space=pltpu.VMEM)
    scalar = pl.BlockSpec(memory_space=pltpu.SMEM)
    plan = tile_schedule(pair_list.shape[1], blocks)
    half, width, steps, chunks = plan
    slots = width * steps

    limits = pltpu.CompilerParams(vmem_limit_bytes=kernel_bytes)
    outgoing = pl.pallas_call(
        packing_kernel,
        out_shape=jax.ShapeDtypeStruct((devices, blocks_here, 8, BLOCK), f32),
        in_specs=[pl.BlockSpec(memory_space=pltpu.HBM)] * 2,
        out_specs=vector,
        scratch_shapes=[
            pltpu.VMEM(point_data.shape, f32),
            pltpu.VMEM(right_side.shape, f32),
            pltpu.SemaphoreType.DMA((2,)),
        ],
        compiler_params=limits,
    )(
        pltpu.with_memory_space_constraint(point_data, pltpu.HBM),
        pltpu.with_memory_space_constraint(right_side, pltpu.HBM),
    )
    owner, entry, count, low, high = pl.pallas_call(
        functools.partial(listing_kernel, plan, blocks),
        out_shape=(
            pltpu.SMEM((chunks + 8,), jnp.int32),
            pltpu.SMEM((chunks * chunk + 8,), jnp.int32),
            pltpu.SMEM((1,), jnp.int32),
            pltpu.SMEM((slots,), jnp.int32),
            pltpu.SMEM((slots,), jnp.int32),
        ),
        in_specs=[scalar, scalar],
        out_specs=(scalar,) * 5,
        scratch_shapes=[pltpu.SMEM((blocks,), jnp.int32)],
        cost_estimate=pl.CostEstimate(flops=8_000_000_000, bytes_accessed=20_000_000, transcendentals=0),
        compiler_params=limits,
    )(core, pltpu.with_memory_space_constraint(pair_list, pltpu.HBM))
    gathered = lax.all_to_all(outgoing, axes, 0, 0, tiled=True).reshape(blocks, 8, BLOCK)

    field_shape = jax.ShapeDtypeStruct((blocks, 8, BLOCK), f32)
    state_shape = jax.ShapeDtypeStruct((3, blocks, 8, BLOCK), f32)
    work = [pltpu.VMEM((blocks + 1, 16, BLOCK), bf16), pltpu.VMEM((blocks + 1, 8, BLOCK), f32)]
    stage = pltpu.VMEM((width, BLOCK, BLOCK), bf16)
    tiles, mine = pl.pallas_call(
        functools.partial(first_kernel, plan),
        out_shape=(pltpu.VMEM((2 * slots, BLOCK, BLOCK), bf16), field_shape),
        in_specs=[scalar, scalar, vector],
        out_specs=(vector, vector),
        scratch_shapes=[
            pltpu.VMEM((blocks + 1, BLOCK, 48), bf16),
            pltpu.VMEM((blocks + 1, 48, BLOCK), bf16),
            *work,
            *[stage] * 4,
        ],
        compiler_params=limits,
    )(low, high, gathered)
    tiles = pltpu.with_memory_space_constraint(tiles, pltpu.VMEM)
    swap = [(place, place ^ 1) for place in range(col_devices)]
    state = None
    for step in range(1, ITERS):
        other = lax.ppermute(mine, "col", swap)
        first = step == 1
        carried = () if first else (state,)
        mine, state = pl.pallas_call(
            functools.partial(next_kernel, first),
            out_shape=(field_shape, state_shape),
            in_specs=[scalar, scalar, scalar] + [vector] * (4 + len(carried)),
            out_specs=(vector, vector),
            scratch_shapes=work,
            compiler_params=limits,
        )(owner, entry, count, gathered, mine, other, *carried, tiles)
    other = lax.ppermute(mine, "col", swap)
    result = pl.pallas_call(
        last_kernel,
        out_shape=jax.ShapeDtypeStruct((blocks, rows_here, BLOCK), bf16),
        in_specs=[scalar] + [vector] * 4,
        out_specs=vector,
        compiler_params=limits,
    )(core, gathered, mine, other, state)
    result = result.reshape(devices, blocks_here, rows_here, BLOCK)
    received = lax.all_to_all(result, axes, 0, 0, tiled=True)
    received = received.reshape(chips, 2, blocks_here, rows_here, BLOCK)
    received = received.transpose(1, 0, 3, 2, 4).reshape(2, right_side.shape[0], -1)
    return received[0].astype(f32), received[1].astype(f32)


def per_device(point_data, right_side, pair_list):
    col_devices = lax.axis_size("col")
    devices = lax.axis_size("row") * col_devices
    blocks = point_data.shape[1] // BLOCK * devices
    _, width, steps, _ = tile_schedule(pair_list.shape[1], blocks)
    tile_bytes = 2 * width * steps * BLOCK * BLOCK * 2
    paired = col_devices % 2 == 0 and blocks % 2 == 0
    if paired and right_side.shape[0] == rows_here * (devices // 2) and tile_bytes <= tile_bytes_limit:
        return by_realizations(point_data, right_side, pair_list)
    return by_points(point_data, right_side, pair_list)


def solution(mesh):
    placed = (P(None, ("row", "col")), P(None, ("row", "col")), P())
    return jax.shard_map(
        per_device,
        mesh=mesh,
        in_specs=placed,
        out_specs=(P(None, ("row", "col")), P(None, ("row", "col"))),
        check_vma=False,
    )
```

```python
import functools
import jax
import jax.numpy as jnp
from jax import lax
from jax.experimental import pallas as pl
from jax.experimental.pallas import tpu as pltpu
from jax.sharding import PartitionSpec as P

BLOCK = 128
ITERS = 3


long_range = 1.0
short_range = 0.35
nugget = 1.0
tiles_per_step = 8
rows_here = 4
chunk_bits = 2
chunk = 1 << chunk_bits
chunks_per_step = 32
tile_bytes_limit = 24 * 2**20
kernel_bytes = 12 * 2**20
f32 = jnp.float32
bf16 = jnp.bfloat16


def wendland(distance, reach):
    scaled = distance / reach
    remain = jnp.maximum(1.0 - scaled, 0.0)
    square = remain * remain
    return square * square * (4.0 * scaled + 1.0)


def covariance_tiles(row_points, column_points):
    delta_x = row_points[:, 0, :, None] - column_points[:, 0, None, :]
    delta_y = row_points[:, 1, :, None] - column_points[:, 1, None, :]
    delta_z = row_points[:, 2, :, None] - column_points[:, 2, None, :]
    distance = jnp.sqrt(delta_x * delta_x + delta_y * delta_y + delta_z * delta_z)
    kernel = wendland(distance, long_range) + wendland(distance, short_range)
    return row_points[:, 3, :, None] * kernel * column_points[:, 3, None, :]


def as_blocks(points):
    return points.reshape(4, -1, BLOCK).transpose(1, 0, 2)


def by_points(point_data, right_side, pair_list):
    col_devices = lax.axis_size("col")
    my_row = lax.axis_index("row")
    my_column = lax.axis_index("col")
    points = point_data.shape[1]
    blocks_here = points // BLOCK
    realizations = right_side.shape[0]
    own_blocks = as_blocks(point_data)
    row_blocks = as_blocks(lax.all_gather(point_data, "col", axis=1, tiled=True))
    column_blocks = as_blocks(lax.all_gather(point_data, "row", axis=1, tiled=True))
    row_count = row_blocks.shape[0]
    column_count = column_blocks.shape[0]
    lower_block = pair_list[0]
    upper_block = pair_list[1]
    this_device = my_row * col_devices + my_column
    device_of = (
        lower_block // blocks_here // col_devices * col_devices
        + upper_block // blocks_here % col_devices
    )
    roster_first_pair = jnp.sum((device_of < this_device).astype(jnp.int32))
    roster_pair_count = jnp.sum((device_of == this_device).astype(jnp.int32))
    roster_row_slot = jnp.clip(lower_block - my_row * col_devices * blocks_here, 0, row_count - 1)
    roster_column_slot = jnp.clip(
        upper_block // blocks_here // col_devices * blocks_here + upper_block % blocks_here,
        0,
        column_count - 1,
    )
    roster_step_count = (roster_pair_count + tiles_per_step - 1) // tiles_per_step
    plan = (
        roster_first_pair,
        roster_pair_count,
        roster_row_slot,
        roster_column_slot,
        roster_step_count,
        lower_block.shape[0],
    )
    first_pair, pair_count, row_slot, column_slot, step_count, listed = plan
    own_tiles = covariance_tiles(own_blocks, own_blocks).astype(jnp.bfloat16)

    def pick_tiles(step):
        offsets = step * tiles_per_step + jnp.arange(tiles_per_step)
        usable = offsets < pair_count
        picked = jnp.minimum(first_pair + offsets, listed - 1)
        row_pick = row_slot[picked]
        column_pick = column_slot[picked]
        tiles_now = covariance_tiles(row_blocks[row_pick], column_blocks[column_pick])
        tiles_now = jnp.where(usable[:, None, None], tiles_now, 0.0).astype(jnp.bfloat16)
        return (tiles_now, row_pick, column_pick)

    def inner(operands):
        stacked = jnp.stack(
            [jnp.sum(one_side * other_side, axis=1) for one_side, other_side in operands]
        )
        return lax.psum(stacked, ("row", "col"))

    solution = jnp.zeros_like(right_side)
    residual = right_side
    direction = right_side
    norm_now = inner(((residual, residual),))[0]
    for step in range(ITERS):
        rounded = direction.astype(jnp.bfloat16)
        product_row_direction = lax.all_gather(rounded, "col", axis=1, tiled=True)
        product_column_direction = lax.all_gather(rounded, "row", axis=1, tiled=True)
        row_direction = product_row_direction
        column_direction = product_column_direction
        row_direction = row_direction.reshape(realizations, row_count, BLOCK)
        column_direction = column_direction.reshape(realizations, column_count, BLOCK)

        def add_step(step, totals):
            into_rows, into_columns = totals
            tiles_now, row_pick, column_pick = pick_tiles(step)
            to_rows = jnp.einsum(
                "tij,ctj->cti",
                tiles_now,
                column_direction[:, column_pick],
                preferred_element_type=jnp.float32,
            )
            to_columns = jnp.einsum(
                "tij,cti->ctj",
                tiles_now,
                row_direction[:, row_pick],
                preferred_element_type=jnp.float32,
            )
            return (
                into_rows.at[:, row_pick].add(to_rows),
                into_columns.at[:, column_pick].add(to_columns),
            )

        empty_rows = jnp.zeros((realizations, row_count, BLOCK), jnp.float32)
        empty_columns = jnp.zeros((realizations, column_count, BLOCK), jnp.float32)
        into_rows, into_columns = lax.fori_loop(
            0, step_count, add_step, (empty_rows, empty_columns)
        )
        product_into_rows = into_rows.reshape(realizations, -1)
        product_into_columns = into_columns.reshape(realizations, -1)
        from_rows = lax.psum_scatter(product_into_rows, "col", scatter_dimension=1, tiled=True)
        from_columns = lax.psum_scatter(
            product_into_columns.astype(jnp.bfloat16), "row", scatter_dimension=1, tiled=True
        ).astype(jnp.float32)
        diagonal = jnp.einsum(
            "tij,ctj->cti",
            own_tiles,
            rounded.reshape(realizations, blocks_here, BLOCK),
            preferred_element_type=jnp.float32,
        )
        image = (
            nugget * direction + diagonal.reshape(realizations, points) + from_rows + from_columns
        )
        alpha = norm_now / inner(((direction, image),))[0]
        solution = solution + alpha[:, None] * direction
        residual = residual - alpha[:, None] * image
        if step + 1 < ITERS:
            norm_next = inner(((residual, residual),))[0]
            direction = residual + (norm_next / norm_now)[:, None] * direction
            norm_now = norm_next
    return (solution, residual)


def tile_schedule(listed, blocks):
    half = (listed + 1) // 2
    entries = half + blocks // 2
    sizes = range(12, 21)
    width = min(sizes, key=lambda size: (-(-entries // (2 * size)) * size, -size))
    steps = -(-entries // (2 * width)) * 2
    longest = (2 * half + blocks // 2 + 3 * blocks) // chunk
    chunks = -(-longest // chunks_per_step) * chunks_per_step + chunks_per_step
    return half, width, steps, chunks


def packing_kernel(point_hbm, field_hbm, outgoing_ref, point_ref, field_ref, arrived):
    devices = outgoing_ref.shape[0]
    copies = (
        pltpu.make_async_copy(point_hbm, point_ref, arrived.at[0]),
        pltpu.make_async_copy(field_hbm, field_ref, arrived.at[1]),
    )
    for copy in copies:
        copy.start()
    for copy in copies:
        copy.wait()
    first = point_ref[:, 0:BLOCK]
    second = point_ref[:, BLOCK : 2 * BLOCK]
    first_high = first.astype(bf16).astype(f32)
    second_high = second.astype(bf16).astype(f32)
    for chip in range(devices // 2):
        rows = pl.ds(chip * rows_here, rows_here)
        parts = (
            field_ref[rows, 0:BLOCK],
            first_high,
            field_ref[rows, BLOCK : 2 * BLOCK],
            second_high,
            second - second_high,
            first - first_high,
        )
        message = jnp.concatenate(parts, axis=0).astype(bf16)
        outgoing_ref[2 * chip] = message
        outgoing_ref[2 * chip + 1] = message


def listing_kernel(
    plan,
    blocks,
    core_ref,
    pair_hbm,
    owner_ref,
    entry_ref,
    count_ref,
    low_ref,
    high_ref,
    open_ref,
    pair_ref,
    arrived,
):
    copy = pltpu.make_async_copy(pair_hbm, pair_ref, arrived)
    copy.start()
    half, width, steps, chunks = plan
    listed = pair_ref.shape[1]
    core = core_ref[0]
    slots = width * steps

    def clear(block, carry):
        open_ref[block] = 0
        return carry

    def pad(place, carry):
        entry_ref[place] = blocks
        return carry

    lax.fori_loop(0, blocks, clear, 0, unroll=16)
    lax.fori_loop(0, chunks * chunk, pad, 0, unroll=16)

    def append(block, entry, used):
        place = open_ref[block]
        fresh = (place & (chunk - 1)) == 0
        place = jnp.where(fresh, used, place)
        open_ref[block] = place + 1
        entry_ref[place] = entry
        owner_ref[place >> chunk_bits] = block
        return jnp.where(fresh, used + chunk, used)

    def list_pair(number, used):
        low = pair_ref[0, core * half + number]
        high = pair_ref[1, core * half + number]
        low_ref[number] = low
        high_ref[number] = high
        used = append(high, number * 65536 + low, used)
        return append(low, (slots + number) * 65536 + high, used)

    def list_diagonal(number, used):
        block = core * (blocks // 2) + number
        low_ref[half + number] = block
        high_ref[half + number] = block
        return append(block, (half + number) * 65536 + block, used)

    low_ref[half - 1] = blocks
    high_ref[half - 1] = blocks
    for number in range(half + blocks // 2, slots):
        low_ref[number] = blocks
        high_ref[number] = blocks
    copy.wait()
    used = lax.fori_loop(0, listed // 2, list_pair, 0, unroll=13)
    if listed % 2:
        used = lax.fori_loop(half - 1, half - core, list_pair, used)
    used = lax.fori_loop(0, blocks // 2, list_diagonal, used, unroll=8)
    used = used >> chunk_bits
    count_ref[0] = used
    for part in range(chunks_per_step):
        owner_ref[used + part] = blocks


def radial(squared):
    squared = jnp.maximum(squared, 1e-30)
    distance = squared * lax.rsqrt(squared)
    near = jnp.maximum(1.0 - distance * (1.0 / long_range), 0.0)
    near_square = near * near
    wide = near_square * near_square * (1.25 - near)
    close = (1.0 - distance * (1.0 / short_range)).astype(bf16)
    close = jnp.maximum(close, jnp.asarray(0.0, bf16))
    close_square = close * close
    narrow = close_square * close_square * (jnp.asarray(1.25, bf16) - close)
    return wide.astype(bf16) + narrow


def three_parts(values):
    first = values.astype(bf16).astype(f32)
    rest = values - first
    second = rest.astype(bf16).astype(f32)
    return first, second, rest - second


def row_number(shape):
    return lax.broadcasted_iota(jnp.int32, shape, len(shape) - 2)


def store_scaled(fields_ref, direction, scale):
    blocks = direction.shape[0]
    blank = jnp.zeros((blocks, 16 - rows_here, BLOCK), f32)
    scaled = jnp.concatenate([direction * (4.0 * scale), blank], axis=1)
    fields_ref[0:blocks] = scaled.astype(bf16)
    fields_ref[blocks] = jnp.zeros((16, BLOCK), bf16)


def multiply(owner_ref, entry_ref, count, tiles_ref, fields_ref, totals_ref):
    totals_ref[...] = jnp.zeros_like(totals_ref)

    def step(number, carry):
        products = []
        for part in range(chunks_per_step):
            fields = []
            tiles = []
            for slot in range(chunk):
                entry = entry_ref[(number * chunks_per_step + part) * chunk + slot]
                fields.append(fields_ref[entry & 65535])
                tiles.append(tiles_ref[entry >> 16])
            product = jnp.dot(
                jnp.concatenate(fields, axis=1),
                jnp.concatenate(tiles, axis=0),
                preferred_element_type=f32,
            )
            products.append(product[0:8])
        for part in range(chunks_per_step):
            totals_ref[owner_ref[number * chunks_per_step + part]] += products[part]
        return carry

    lax.fori_loop(0, (count + chunks_per_step - 1) // chunks_per_step, step, 0)


def first_kernel(
    plan,
    low_ref,
    high_ref,
    received_ref,
    tiles_ref,
    product_ref,
    gathered_ref,
    left_ref,
    right_ref,
    fields_ref,
    totals_ref,
    *stages,
):
    half, width, steps, _ = plan
    blocks = gathered_ref.shape[0]
    slots = width * steps
    for device in range(blocks // 2):
        message = received_ref[device].astype(f32)
        lower = message[16:24]
        is_point = row_number((8, BLOCK)) >= rows_here
        first = message[0:8] + jnp.where(is_point, lower, 0.0)
        second = message[8:16] + jnp.where(is_point, pltpu.roll(lower, 4, axis=0), 0.0)
        gathered_ref[2 * device] = first
        gathered_ref[2 * device + 1] = second
    highest = jnp.max(jnp.max(gathered_ref[...], axis=0), axis=1, keepdims=True)
    lowest = jnp.min(jnp.min(gathered_ref[...], axis=0), axis=1, keepdims=True)
    centre = 0.5 * (highest + lowest)

    def prepare(block, carry):
        row = row_number((8, BLOCK))
        is_coordinate = (row >= 4) & (row < 7)
        shifted = jnp.where(is_coordinate, gathered_ref[block] - centre, 0.0)
        squared = jnp.sum(shifted * shifted, axis=0, keepdims=True)
        left = jnp.where(row == 7, 1.0, jnp.where(row == 0, squared, shifted))
        right = jnp.where(row == 7, squared, jnp.where(row == 0, 1.0, -2.0 * shifted))
        left_1, left_2, left_3 = three_parts(left)
        right_1, right_2, right_3 = three_parts(right)
        left_all = jnp.concatenate([left_1, left_1, left_2, left_2, left_1, left_3], axis=0)
        right_all = jnp.concatenate([right_1, right_2, right_1, right_2, right_3, right_1], axis=0)
        left_ref[block] = left_all.T.astype(bf16)
        right_ref[block] = right_all.astype(bf16)
        return carry

    lax.fori_loop(0, blocks, prepare, 0, unroll=8)
    left_ref[blocks] = jnp.zeros((BLOCK, 48), bf16)
    right_ref[blocks] = jnp.zeros((48, BLOCK), bf16)
    store_scaled(fields_ref, gathered_ref[:, 0:rows_here, :], gathered_ref[:, 7:8, :])
    totals_ref[...] = jnp.zeros_like(totals_ref)

    def square(step, slot):
        number = step * width + slot
        return jnp.dot(
            left_ref[low_ref[number]], right_ref[high_ref[number]], preferred_element_type=f32
        )

    def make_tile(step, slot, stage, squared):
        number = step * width + slot
        tile = radial(squared)
        turned = tile.T
        tiles_ref[number] = tile
        tiles_ref[slots + number] = turned
        stage[0][slot] = tile
        stage[1][slot] = turned

    def use_tile(step, slot, stage):
        number = step * width + slot
        made = jnp.maximum(number, 0)
        low = jnp.where(number >= 0, low_ref[made], blocks)
        high = jnp.where(number >= 0, high_ref[made], blocks)
        is_pair = number < half
        ways = (
            (low, high),
            (jnp.where(is_pair, high, blocks), jnp.where(is_pair, low, blocks)),
        )
        products = []
        for (source, target), tiles in zip(ways, stage):
            product = jnp.dot(fields_ref[source], tiles[slot], preferred_element_type=f32)
            products.append((target, product[0:8]))
        return products

    def add_products(products):
        for target, product in products:
            totals_ref[target] += product

    def use_tiles(step, stage):
        for slot in range(width):
            add_products(use_tile(step, slot, stage))

    def both(step, new_stage, old_stage):
        waiting = []
        ahead = square(step, 0)
        for slot in range(width):
            squared = ahead
            if slot + 1 < width:
                ahead = square(step, slot + 1)
            make_tile(step, slot, new_stage, squared)
            waiting.append(use_tile(step - 1, slot, old_stage))
            if len(waiting) > 2:
                add_products(waiting.pop(0))
        for products in waiting:
            add_products(products)

    even, odd = stages[0:2], stages[2:4]

    def both_steps(pair, carry):
        both(2 * pair, even, odd)
        both(2 * pair + 1, odd, even)
        return carry

    lax.fori_loop(0, steps // 2, both_steps, 0)
    use_tiles(steps - 1, odd)
    product_ref[...] = totals_ref[0:blocks, 0:rows_here, :]


def total(values):
    return jnp.sum(jnp.sum(values, axis=0), axis=1, keepdims=True)[None]


def advance(mine_ref, other_ref, scale, direction, residual):
    image = nugget * direction + scale * (mine_ref[...] + other_ref[...])
    norm_now = total(residual * residual)
    along = total(direction * image)
    alpha = norm_now / along
    return alpha * direction, residual - alpha * image, norm_now


def next_kernel(
    first,
    owner_ref,
    entry_ref,
    count_ref,
    gathered_ref,
    mine_ref,
    other_ref,
    *rest,
):
    if first:
        tiles_ref, product_ref, state_out_ref, fields_ref, totals_ref = rest
        direction = gathered_ref[:, 0:rows_here, :]
        residual = direction
    else:
        state_ref, tiles_ref, product_ref, state_out_ref, fields_ref, totals_ref = rest
        direction = state_ref[2]
        residual = state_ref[1]
    scale = gathered_ref[:, 7:8, :]
    moved, residual, norm_now = advance(mine_ref, other_ref, scale, direction, residual)
    norm_next = total(residual * residual)
    direction = residual + (norm_next / norm_now) * direction
    state_out_ref[0] = moved if first else state_ref[0] + moved
    state_out_ref[1] = residual
    state_out_ref[2] = direction
    store_scaled(fields_ref, direction, scale)
    multiply(owner_ref, entry_ref, count_ref[0], tiles_ref, fields_ref, totals_ref)
    product_ref[...] = totals_ref[0 : gathered_ref.shape[0], 0:rows_here, :]


def last_kernel(core_ref, gathered_ref, mine_ref, other_ref, state_ref, result_ref):
    scale = gathered_ref[:, 7:8, :]
    moved, residual, _ = advance(mine_ref, other_ref, scale, state_ref[2], state_ref[1])
    chosen = jnp.where(core_ref[0] == 0, state_ref[0] + moved, residual)
    result_ref[...] = chosen.astype(bf16)


def by_realizations(point_data, right_side, pair_list):
    col_devices = lax.axis_size("col")
    devices = lax.axis_size("row") * col_devices
    chips = devices // 2
    blocks_here = point_data.shape[1] // BLOCK
    blocks = blocks_here * devices
    core = lax.rem(lax.axis_index("col"), 2).astype(jnp.int32).reshape(1)
    axes = ("row", "col")
    vector = pl.BlockSpec(memory_space=pltpu.VMEM)
    scalar = pl.BlockSpec(memory_space=pltpu.SMEM)
    plan = tile_schedule(pair_list.shape[1], blocks)
    half, width, steps, chunks = plan
    slots = width * steps

    limits = pltpu.CompilerParams(vmem_limit_bytes=kernel_bytes)
    outgoing = pl.pallas_call(
        packing_kernel,
        out_shape=jax.ShapeDtypeStruct((devices, 24, BLOCK), bf16),
        in_specs=[pl.BlockSpec(memory_space=pltpu.HBM)] * 2,
        out_specs=vector,
        scratch_shapes=[
            pltpu.VMEM(point_data.shape, f32),
            pltpu.VMEM(right_side.shape, f32),
            pltpu.SemaphoreType.DMA((2,)),
        ],
        compiler_params=limits,
    )(
        pltpu.with_memory_space_constraint(point_data, pltpu.HBM),
        pltpu.with_memory_space_constraint(right_side, pltpu.HBM),
    )
    owner, entry, count, low, high = pl.pallas_call(
        functools.partial(listing_kernel, plan, blocks),
        out_shape=(
            pltpu.SMEM((chunks + 8,), jnp.int32),
            pltpu.SMEM((chunks * chunk + 8,), jnp.int32),
            pltpu.SMEM((1,), jnp.int32),
            pltpu.SMEM((slots,), jnp.int32),
            pltpu.SMEM((slots,), jnp.int32),
        ),
        in_specs=[scalar, pl.BlockSpec(memory_space=pltpu.HBM)],
        out_specs=(scalar,) * 5,
        scratch_shapes=[
            pltpu.SMEM((blocks,), jnp.int32),
            pltpu.SMEM(pair_list.shape, jnp.int32),
            pltpu.SemaphoreType.DMA,
        ],
        cost_estimate=pl.CostEstimate(flops=8_000_000_000, bytes_accessed=20_000_000, transcendentals=0),
        compiler_params=limits,
    )(core, pltpu.with_memory_space_constraint(pair_list, pltpu.HBM))
    received = lax.all_to_all(outgoing, axes, 0, 0, tiled=True)

    field_shape = jax.ShapeDtypeStruct((blocks, 8, BLOCK), f32)
    product_shape = jax.ShapeDtypeStruct((blocks, rows_here, BLOCK), f32)
    state_shape = jax.ShapeDtypeStruct((3, blocks, rows_here, BLOCK), f32)
    work = [pltpu.VMEM((blocks + 1, 16, BLOCK), bf16), pltpu.VMEM((blocks + 1, 8, BLOCK), f32)]
    stage = pltpu.VMEM((width, BLOCK, BLOCK), bf16)
    tiles, mine, gathered = pl.pallas_call(
        functools.partial(first_kernel, plan),
        out_shape=(pltpu.VMEM((2 * slots, BLOCK, BLOCK), bf16), product_shape, field_shape),
        in_specs=[scalar, scalar, vector],
        out_specs=(vector, vector, vector),
        scratch_shapes=[
            pltpu.VMEM((blocks + 1, BLOCK, 48), bf16),
            pltpu.VMEM((blocks + 1, 48, BLOCK), bf16),
            *work,
            *[stage] * 4,
        ],
        compiler_params=limits,
    )(low, high, received)
    tiles = pltpu.with_memory_space_constraint(tiles, pltpu.VMEM)
    swap = [(place, place ^ 1) for place in range(col_devices)]
    state = None
    for step in range(1, ITERS):
        other = lax.ppermute(mine, "col", swap)
        first = step == 1
        carried = () if first else (state,)
        mine, state = pl.pallas_call(
            functools.partial(next_kernel, first),
            out_shape=(product_shape, state_shape),
            in_specs=[scalar, scalar, scalar] + [vector] * (4 + len(carried)),
            out_specs=(vector, vector),
            scratch_shapes=work,
            compiler_params=limits,
        )(owner, entry, count, gathered, mine, other, *carried, tiles)
    other = lax.ppermute(mine, "col", swap)
    result = pl.pallas_call(
        last_kernel,
        out_shape=jax.ShapeDtypeStruct((blocks, rows_here, BLOCK), bf16),
        in_specs=[scalar] + [vector] * 4,
        out_specs=vector,
        compiler_params=limits,
    )(core, gathered, mine, other, state)
    result = result.reshape(devices, blocks_here, rows_here, BLOCK)
    received = lax.all_to_all(result, axes, 0, 0, tiled=True)
    received = received.reshape(chips, 2, blocks_here, rows_here, BLOCK)
    received = received.transpose(1, 0, 3, 2, 4).reshape(2, right_side.shape[0], -1)
    return received[0].astype(f32), received[1].astype(f32)


def per_device(point_data, right_side, pair_list):
    col_devices = lax.axis_size("col")
    devices = lax.axis_size("row") * col_devices
    blocks = point_data.shape[1] // BLOCK * devices
    _, width, steps, _ = tile_schedule(pair_list.shape[1], blocks)
    tile_bytes = 2 * width * steps * BLOCK * BLOCK * 2
    paired = col_devices % 2 == 0 and blocks == 2 * devices
    if paired and right_side.shape[0] == rows_here * (devices // 2) and tile_bytes <= tile_bytes_limit:
        return by_realizations(point_data, right_side, pair_list)
    return by_points(point_data, right_side, pair_list)


def solution(mesh):
    placed = (P(None, ("row", "col")), P(None, ("row", "col")), P())
    return jax.shard_map(
        per_device,
        mesh=mesh,
        in_specs=placed,
        out_specs=(P(None, ("row", "col")), P(None, ("row", "col"))),
        check_vma=False,
    )
```

```python
import functools
import jax
import jax.numpy as jnp
from jax import lax
from jax.experimental import pallas as pl
from jax.experimental.pallas import tpu as pltpu
from jax.sharding import PartitionSpec as P

BLOCK = 128
ITERS = 3


long_range = 1.0
short_range = 0.35
nugget = 1.0
tiles_per_step = 8
rows_here = 4
chunk_bits = 2
chunk = 1 << chunk_bits
chunks_per_step = 40
tile_bytes_limit = 24 * 2**20
kernel_bytes = 12 * 2**20
f32 = jnp.float32
bf16 = jnp.bfloat16


def wendland(distance, reach):
    scaled = distance / reach
    remain = jnp.maximum(1.0 - scaled, 0.0)
    square = remain * remain
    return square * square * (4.0 * scaled + 1.0)


def covariance_tiles(row_points, column_points):
    delta_x = row_points[:, 0, :, None] - column_points[:, 0, None, :]
    delta_y = row_points[:, 1, :, None] - column_points[:, 1, None, :]
    delta_z = row_points[:, 2, :, None] - column_points[:, 2, None, :]
    distance = jnp.sqrt(delta_x * delta_x + delta_y * delta_y + delta_z * delta_z)
    kernel = wendland(distance, long_range) + wendland(distance, short_range)
    return row_points[:, 3, :, None] * kernel * column_points[:, 3, None, :]


def as_blocks(points):
    return points.reshape(4, -1, BLOCK).transpose(1, 0, 2)


def by_points(point_data, right_side, pair_list):
    col_devices = lax.axis_size("col")
    my_row = lax.axis_index("row")
    my_column = lax.axis_index("col")
    points = point_data.shape[1]
    blocks_here = points // BLOCK
    realizations = right_side.shape[0]
    own_blocks = as_blocks(point_data)
    row_blocks = as_blocks(lax.all_gather(point_data, "col", axis=1, tiled=True))
    column_blocks = as_blocks(lax.all_gather(point_data, "row", axis=1, tiled=True))
    row_count = row_blocks.shape[0]
    column_count = column_blocks.shape[0]
    lower_block = pair_list[0]
    upper_block = pair_list[1]
    this_device = my_row * col_devices + my_column
    device_of = (
        lower_block // blocks_here // col_devices * col_devices
        + upper_block // blocks_here % col_devices
    )
    roster_first_pair = jnp.sum((device_of < this_device).astype(jnp.int32))
    roster_pair_count = jnp.sum((device_of == this_device).astype(jnp.int32))
    roster_row_slot = jnp.clip(lower_block - my_row * col_devices * blocks_here, 0, row_count - 1)
    roster_column_slot = jnp.clip(
        upper_block // blocks_here // col_devices * blocks_here + upper_block % blocks_here,
        0,
        column_count - 1,
    )
    roster_step_count = (roster_pair_count + tiles_per_step - 1) // tiles_per_step
    plan = (
        roster_first_pair,
        roster_pair_count,
        roster_row_slot,
        roster_column_slot,
        roster_step_count,
        lower_block.shape[0],
    )
    first_pair, pair_count, row_slot, column_slot, step_count, listed = plan
    own_tiles = covariance_tiles(own_blocks, own_blocks).astype(jnp.bfloat16)

    def pick_tiles(step):
        offsets = step * tiles_per_step + jnp.arange(tiles_per_step)
        usable = offsets < pair_count
        picked = jnp.minimum(first_pair + offsets, listed - 1)
        row_pick = row_slot[picked]
        column_pick = column_slot[picked]
        tiles_now = covariance_tiles(row_blocks[row_pick], column_blocks[column_pick])
        tiles_now = jnp.where(usable[:, None, None], tiles_now, 0.0).astype(jnp.bfloat16)
        return (tiles_now, row_pick, column_pick)

    def inner(operands):
        stacked = jnp.stack(
            [jnp.sum(one_side * other_side, axis=1) for one_side, other_side in operands]
        )
        return lax.psum(stacked, ("row", "col"))

    solution = jnp.zeros_like(right_side)
    residual = right_side
    direction = right_side
    norm_now = inner(((residual, residual),))[0]
    for step in range(ITERS):
        rounded = direction.astype(jnp.bfloat16)
        product_row_direction = lax.all_gather(rounded, "col", axis=1, tiled=True)
        product_column_direction = lax.all_gather(rounded, "row", axis=1, tiled=True)
        row_direction = product_row_direction
        column_direction = product_column_direction
        row_direction = row_direction.reshape(realizations, row_count, BLOCK)
        column_direction = column_direction.reshape(realizations, column_count, BLOCK)

        def add_step(step, totals):
            into_rows, into_columns = totals
            tiles_now, row_pick, column_pick = pick_tiles(step)
            to_rows = jnp.einsum(
                "tij,ctj->cti",
                tiles_now,
                column_direction[:, column_pick],
                preferred_element_type=jnp.float32,
            )
            to_columns = jnp.einsum(
                "tij,cti->ctj",
                tiles_now,
                row_direction[:, row_pick],
                preferred_element_type=jnp.float32,
            )
            return (
                into_rows.at[:, row_pick].add(to_rows),
                into_columns.at[:, column_pick].add(to_columns),
            )

        empty_rows = jnp.zeros((realizations, row_count, BLOCK), jnp.float32)
        empty_columns = jnp.zeros((realizations, column_count, BLOCK), jnp.float32)
        into_rows, into_columns = lax.fori_loop(
            0, step_count, add_step, (empty_rows, empty_columns)
        )
        product_into_rows = into_rows.reshape(realizations, -1)
        product_into_columns = into_columns.reshape(realizations, -1)
        from_rows = lax.psum_scatter(product_into_rows, "col", scatter_dimension=1, tiled=True)
        from_columns = lax.psum_scatter(
            product_into_columns.astype(jnp.bfloat16), "row", scatter_dimension=1, tiled=True
        ).astype(jnp.float32)
        diagonal = jnp.einsum(
            "tij,ctj->cti",
            own_tiles,
            rounded.reshape(realizations, blocks_here, BLOCK),
            preferred_element_type=jnp.float32,
        )
        image = (
            nugget * direction + diagonal.reshape(realizations, points) + from_rows + from_columns
        )
        alpha = norm_now / inner(((direction, image),))[0]
        solution = solution + alpha[:, None] * direction
        residual = residual - alpha[:, None] * image
        if step + 1 < ITERS:
            norm_next = inner(((residual, residual),))[0]
            direction = residual + (norm_next / norm_now)[:, None] * direction
            norm_now = norm_next
    return (solution, residual)


def tile_schedule(listed, blocks):
    half = (listed + 1) // 2
    entries = half + blocks // 2
    sizes = range(20, 39)
    width = min(sizes, key=lambda size: (-(-entries // (2 * size)) * size, -size))
    steps = -(-entries // (2 * width)) * 2
    longest = (2 * half + blocks // 2 + 3 * blocks) // chunk
    chunks = -(-longest // chunks_per_step) * chunks_per_step + chunks_per_step
    return half, width, steps, chunks


def packing_kernel(point_hbm, field_hbm, outgoing_ref, point_ref, field_ref, arrived):
    devices = outgoing_ref.shape[0]
    copies = (
        pltpu.make_async_copy(point_hbm, point_ref, arrived.at[0]),
        pltpu.make_async_copy(field_hbm, field_ref, arrived.at[1]),
    )
    for copy in copies:
        copy.start()
    for copy in copies:
        copy.wait()
    first = point_ref[:, 0:BLOCK]
    second = point_ref[:, BLOCK : 2 * BLOCK]
    first_high = first.astype(bf16).astype(f32)
    second_high = second.astype(bf16).astype(f32)
    for chip in range(devices // 2):
        rows = pl.ds(chip * rows_here, rows_here)
        parts = (
            field_ref[rows, 0:BLOCK],
            first_high,
            field_ref[rows, BLOCK : 2 * BLOCK],
            second_high,
            second - second_high,
            first - first_high,
        )
        message = jnp.concatenate(parts, axis=0).astype(bf16)
        outgoing_ref[2 * chip] = message
        outgoing_ref[2 * chip + 1] = message


def listing_kernel(
    plan,
    blocks,
    core_ref,
    pair_hbm,
    owner_ref,
    entry_ref,
    count_ref,
    low_ref,
    high_ref,
    open_ref,
    pair_ref,
    arrived,
):
    copy = pltpu.make_async_copy(pair_hbm, pair_ref, arrived)
    copy.start()
    half, width, steps, chunks = plan
    listed = pair_ref.shape[1]
    core = core_ref[0]
    slots = width * steps

    def clear(block, carry):
        open_ref[block] = 0
        return carry

    def pad(place, carry):
        entry_ref[place] = blocks
        return carry

    lax.fori_loop(0, blocks, clear, 0, unroll=16)
    lax.fori_loop(0, chunks * chunk, pad, 0, unroll=16)

    def append(block, entry, used):
        place = open_ref[block]
        fresh = (place & (chunk - 1)) == 0
        place = jnp.where(fresh, used, place)
        open_ref[block] = place + 1
        entry_ref[place] = entry
        owner_ref[place >> chunk_bits] = block
        return jnp.where(fresh, used + chunk, used)

    def list_pair(number, used):
        low = pair_ref[0, core * half + number]
        high = pair_ref[1, core * half + number]
        low_ref[number] = low
        high_ref[number] = high
        used = append(high, number * 65536 + low, used)
        return append(low, (slots + number) * 65536 + high, used)

    def list_diagonal(number, used):
        block = core * (blocks // 2) + number
        low_ref[half + number] = block
        high_ref[half + number] = block
        return append(block, (half + number) * 65536 + block, used)

    low_ref[half - 1] = blocks
    high_ref[half - 1] = blocks
    for number in range(half + blocks // 2, slots):
        low_ref[number] = blocks
        high_ref[number] = blocks
    copy.wait()
    used = lax.fori_loop(0, listed // 2, list_pair, 0, unroll=13)
    if listed % 2:
        used = lax.fori_loop(half - 1, half - core, list_pair, used)
    used = lax.fori_loop(0, blocks // 2, list_diagonal, used, unroll=8)
    used = used >> chunk_bits
    count_ref[0] = used
    for part in range(chunks_per_step):
        owner_ref[used + part] = blocks


def radial(squared):
    squared = jnp.maximum(squared, 1e-30)
    distance = squared * lax.rsqrt(squared)
    near = jnp.maximum(1.0 - distance * (1.0 / long_range), 0.0)
    near_square = near * near
    wide = near_square * near_square * (1.25 - near)
    close = jnp.asarray(1.0, bf16) - distance.astype(bf16) * jnp.asarray(1.0 / short_range, bf16)
    close = jnp.maximum(close, jnp.asarray(0.0, bf16))
    close_square = close * close
    narrow = close_square * close_square * (jnp.asarray(1.25, bf16) - close)
    return wide.astype(bf16) + narrow


def three_parts(values):
    first = values.astype(bf16).astype(f32)
    rest = values - first
    second = rest.astype(bf16).astype(f32)
    return first, second, rest - second


def row_number(shape):
    return lax.broadcasted_iota(jnp.int32, shape, len(shape) - 2)


def store_scaled(fields_ref, direction, scale):
    blocks = direction.shape[0]
    blank = jnp.zeros((blocks, 16 - rows_here, BLOCK), f32)
    scaled = jnp.concatenate([direction * (4.0 * scale), blank], axis=1)
    fields_ref[0:blocks] = scaled.astype(bf16)
    fields_ref[blocks] = jnp.zeros((16, BLOCK), bf16)


def multiply(owner_ref, entry_ref, count, tiles_ref, fields_ref, totals_ref):
    totals_ref[...] = jnp.zeros_like(totals_ref)

    def step(number, carry):
        products = []
        for part in range(chunks_per_step):
            fields = []
            tiles = []
            for slot in range(chunk):
                entry = entry_ref[(number * chunks_per_step + part) * chunk + slot]
                fields.append(fields_ref[entry & 65535])
                tiles.append(tiles_ref[entry >> 16])
            product = jnp.dot(
                jnp.concatenate(fields, axis=1),
                jnp.concatenate(tiles, axis=0),
                preferred_element_type=f32,
            )
            products.append(product[0:8])
        for part in range(chunks_per_step):
            totals_ref[owner_ref[number * chunks_per_step + part]] += products[part]
        return carry

    lax.fori_loop(0, (count + chunks_per_step - 1) // chunks_per_step, step, 0)


def first_kernel(
    plan,
    low_ref,
    high_ref,
    received_ref,
    tiles_ref,
    product_ref,
    gathered_ref,
    left_ref,
    right_ref,
    fields_ref,
    totals_ref,
    *stages,
):
    half, width, steps, _ = plan
    blocks = gathered_ref.shape[0]
    slots = width * steps
    for device in range(blocks // 2):
        message = received_ref[device].astype(f32)
        lower = message[16:24]
        is_point = row_number((8, BLOCK)) >= rows_here
        first = message[0:8] + jnp.where(is_point, lower, 0.0)
        second = message[8:16] + jnp.where(is_point, pltpu.roll(lower, 4, axis=0), 0.0)
        gathered_ref[2 * device] = first
        gathered_ref[2 * device + 1] = second
    highest = jnp.max(jnp.max(gathered_ref[...], axis=0), axis=1, keepdims=True)
    lowest = jnp.min(jnp.min(gathered_ref[...], axis=0), axis=1, keepdims=True)
    centre = 0.5 * (highest + lowest)

    def prepare(block, carry):
        row = row_number((8, BLOCK))
        is_coordinate = (row >= 4) & (row < 7)
        shifted = jnp.where(is_coordinate, gathered_ref[block] - centre, 0.0)
        squared = jnp.sum(shifted * shifted, axis=0, keepdims=True)
        left = jnp.where(row == 7, 1.0, jnp.where(row == 0, squared, shifted))
        right = jnp.where(row == 7, squared, jnp.where(row == 0, 1.0, -2.0 * shifted))
        left_1, left_2, left_3 = three_parts(left)
        right_1, right_2, right_3 = three_parts(right)
        left_all = jnp.concatenate([left_1, left_1, left_2, left_2, left_1, left_3], axis=0)
        right_all = jnp.concatenate([right_1, right_2, right_1, right_2, right_3, right_1], axis=0)
        left_ref[block] = left_all.T.astype(bf16)
        right_ref[block] = right_all.astype(bf16)
        return carry

    lax.fori_loop(0, blocks, prepare, 0, unroll=32)
    left_ref[blocks] = jnp.zeros((BLOCK, 48), bf16)
    right_ref[blocks] = jnp.zeros((48, BLOCK), bf16)
    store_scaled(fields_ref, gathered_ref[:, 0:rows_here, :], gathered_ref[:, 7:8, :])
    totals_ref[...] = jnp.zeros_like(totals_ref)

    def square(step, slot):
        number = step * width + slot
        return jnp.dot(
            left_ref[low_ref[number]], right_ref[high_ref[number]], preferred_element_type=f32
        )

    def make_tile(step, slot, stage, squared):
        number = step * width + slot
        tile = radial(squared)
        turned = tile.T
        tiles_ref[number] = tile
        tiles_ref[slots + number] = turned
        stage[0][slot] = tile
        stage[1][slot] = turned

    def use_tile(step, slot, stage):
        number = step * width + slot
        made = jnp.maximum(number, 0)
        low = jnp.where(number >= 0, low_ref[made], blocks)
        high = jnp.where(number >= 0, high_ref[made], blocks)
        is_pair = number < half
        ways = (
            (low, high),
            (jnp.where(is_pair, high, blocks), jnp.where(is_pair, low, blocks)),
        )
        products = []
        for (source, target), tiles in zip(ways, stage):
            product = jnp.dot(fields_ref[source], tiles[slot], preferred_element_type=f32)
            products.append((target, product[0:8]))
        return products

    def add_products(products):
        for target, product in products:
            totals_ref[target] += product

    def use_tiles(step, stage):
        for slot in range(width):
            add_products(use_tile(step, slot, stage))

    def both(step, new_stage, old_stage):
        waiting = []
        ahead = square(step, 0)
        for slot in range(width):
            squared = ahead
            if slot + 1 < width:
                ahead = square(step, slot + 1)
            make_tile(step, slot, new_stage, squared)
            waiting.append(use_tile(step - 1, slot, old_stage))
            if len(waiting) > 2:
                add_products(waiting.pop(0))
        for products in waiting:
            add_products(products)

    even, odd = stages[0:2], stages[2:4]

    def both_steps(pair, carry):
        both(2 * pair, even, odd)
        both(2 * pair + 1, odd, even)
        return carry

    lax.fori_loop(0, steps // 2, both_steps, 0)
    use_tiles(steps - 1, odd)
    product_ref[...] = totals_ref[0:blocks, 0:rows_here, :]


def total(values):
    return jnp.sum(jnp.sum(values, axis=0), axis=1, keepdims=True)[None]


def advance(mine_ref, other_ref, scale, direction, residual):
    image = nugget * direction + scale * (mine_ref[...] + other_ref[...])
    norm_now = total(residual * residual)
    along = total(direction * image)
    alpha = norm_now / along
    return alpha * direction, residual - alpha * image, norm_now


def next_kernel(
    first,
    owner_ref,
    entry_ref,
    count_ref,
    gathered_ref,
    mine_ref,
    other_ref,
    *rest,
):
    if first:
        tiles_ref, product_ref, state_out_ref, fields_ref, totals_ref = rest
        direction = gathered_ref[:, 0:rows_here, :]
        residual = direction
    else:
        state_ref, tiles_ref, product_ref, state_out_ref, fields_ref, totals_ref = rest
        direction = state_ref[2]
        residual = state_ref[1]
    scale = gathered_ref[:, 7:8, :]
    moved, residual, norm_now = advance(mine_ref, other_ref, scale, direction, residual)
    norm_next = total(residual * residual)
    direction = residual + (norm_next / norm_now) * direction
    state_out_ref[0] = moved if first else state_ref[0] + moved
    state_out_ref[1] = residual
    state_out_ref[2] = direction
    store_scaled(fields_ref, direction, scale)
    multiply(owner_ref, entry_ref, count_ref[0], tiles_ref, fields_ref, totals_ref)
    product_ref[...] = totals_ref[0 : gathered_ref.shape[0], 0:rows_here, :]


def last_kernel(core_ref, gathered_ref, mine_ref, other_ref, state_ref, result_ref):
    scale = gathered_ref[:, 7:8, :]
    moved, residual, _ = advance(mine_ref, other_ref, scale, state_ref[2], state_ref[1])
    chosen = jnp.where(core_ref[0] == 0, state_ref[0] + moved, residual)
    result_ref[...] = chosen.astype(bf16)


def by_realizations(point_data, right_side, pair_list):
    col_devices = lax.axis_size("col")
    devices = lax.axis_size("row") * col_devices
    chips = devices // 2
    blocks_here = point_data.shape[1] // BLOCK
    blocks = blocks_here * devices
    core = lax.rem(lax.axis_index("col"), 2).astype(jnp.int32).reshape(1)
    axes = ("row", "col")
    vector = pl.BlockSpec(memory_space=pltpu.VMEM)
    scalar = pl.BlockSpec(memory_space=pltpu.SMEM)
    plan = tile_schedule(pair_list.shape[1], blocks)
    half, width, steps, chunks = plan
    slots = width * steps

    limits = pltpu.CompilerParams(vmem_limit_bytes=kernel_bytes)
    outgoing = pl.pallas_call(
        packing_kernel,
        out_shape=jax.ShapeDtypeStruct((devices, 24, BLOCK), bf16),
        in_specs=[pl.BlockSpec(memory_space=pltpu.HBM)] * 2,
        out_specs=vector,
        scratch_shapes=[
            pltpu.VMEM(point_data.shape, f32),
            pltpu.VMEM(right_side.shape, f32),
            pltpu.SemaphoreType.DMA((2,)),
        ],
        compiler_params=limits,
    )(
        pltpu.with_memory_space_constraint(point_data, pltpu.HBM),
        pltpu.with_memory_space_constraint(right_side, pltpu.HBM),
    )
    owner, entry, count, low, high = pl.pallas_call(
        functools.partial(listing_kernel, plan, blocks),
        out_shape=(
            pltpu.SMEM((chunks + 8,), jnp.int32),
            pltpu.SMEM((chunks * chunk + 8,), jnp.int32),
            pltpu.SMEM((1,), jnp.int32),
            pltpu.SMEM((slots,), jnp.int32),
            pltpu.SMEM((slots,), jnp.int32),
        ),
        in_specs=[scalar, pl.BlockSpec(memory_space=pltpu.HBM)],
        out_specs=(scalar,) * 5,
        scratch_shapes=[
            pltpu.SMEM((blocks,), jnp.int32),
            pltpu.SMEM(pair_list.shape, jnp.int32),
            pltpu.SemaphoreType.DMA,
        ],
        cost_estimate=pl.CostEstimate(flops=8_000_000_000, bytes_accessed=20_000_000, transcendentals=0),
        compiler_params=limits,
    )(core, pltpu.with_memory_space_constraint(pair_list, pltpu.HBM))
    received = lax.all_to_all(outgoing, axes, 0, 0, tiled=True)

    field_shape = jax.ShapeDtypeStruct((blocks, 8, BLOCK), f32)
    product_shape = jax.ShapeDtypeStruct((blocks, rows_here, BLOCK), f32)
    state_shape = jax.ShapeDtypeStruct((3, blocks, rows_here, BLOCK), f32)
    work = [pltpu.VMEM((blocks + 1, 16, BLOCK), bf16), pltpu.VMEM((blocks + 1, 8, BLOCK), f32)]
    stage = pltpu.VMEM((width, BLOCK, BLOCK), bf16)
    tiles, mine, gathered = pl.pallas_call(
        functools.partial(first_kernel, plan),
        out_shape=(pltpu.VMEM((2 * slots, BLOCK, BLOCK), bf16), product_shape, field_shape),
        in_specs=[scalar, scalar, vector],
        out_specs=(vector, vector, vector),
        scratch_shapes=[
            pltpu.VMEM((blocks + 1, BLOCK, 48), bf16),
            pltpu.VMEM((blocks + 1, 48, BLOCK), bf16),
            *work,
            *[stage] * 4,
        ],
        compiler_params=limits,
    )(low, high, received)
    tiles = pltpu.with_memory_space_constraint(tiles, pltpu.VMEM)
    swap = [(place, place ^ 1) for place in range(col_devices)]
    state = None
    for step in range(1, ITERS):
        other = lax.ppermute(mine, "col", swap)
        first = step == 1
        carried = () if first else (state,)
        mine, state = pl.pallas_call(
            functools.partial(next_kernel, first),
            out_shape=(product_shape, state_shape),
            in_specs=[scalar, scalar, scalar] + [vector] * (4 + len(carried)),
            out_specs=(vector, vector),
            scratch_shapes=work,
            compiler_params=limits,
        )(owner, entry, count, gathered, mine, other, *carried, tiles)
    other = lax.ppermute(mine, "col", swap)
    result = pl.pallas_call(
        last_kernel,
        out_shape=jax.ShapeDtypeStruct((blocks, rows_here, BLOCK), bf16),
        in_specs=[scalar] + [vector] * 4,
        out_specs=vector,
        compiler_params=limits,
    )(core, gathered, mine, other, state)
    result = result.reshape(devices, blocks_here, rows_here, BLOCK)
    received = lax.all_to_all(result, axes, 0, 0, tiled=True)
    received = received.reshape(chips, 2, blocks_here, rows_here, BLOCK)
    received = received.transpose(1, 0, 3, 2, 4).reshape(2, right_side.shape[0], -1)
    return received[0].astype(f32), received[1].astype(f32)


def per_device(point_data, right_side, pair_list):
    col_devices = lax.axis_size("col")
    devices = lax.axis_size("row") * col_devices
    blocks = point_data.shape[1] // BLOCK * devices
    _, width, steps, _ = tile_schedule(pair_list.shape[1], blocks)
    tile_bytes = 2 * width * steps * BLOCK * BLOCK * 2
    paired = col_devices % 2 == 0 and blocks == 2 * devices
    if paired and right_side.shape[0] == rows_here * (devices // 2) and tile_bytes <= tile_bytes_limit:
        return by_realizations(point_data, right_side, pair_list)
    return by_points(point_data, right_side, pair_list)


def solution(mesh):
    placed = (P(None, ("row", "col")), P(None, ("row", "col")), P())
    return jax.shard_map(
        per_device,
        mesh=mesh,
        in_specs=placed,
        out_specs=(P(None, ("row", "col")), P(None, ("row", "col"))),
        check_vma=False,
    )
```

```python
import functools
import jax
import jax.numpy as jnp
from jax import lax
from jax.experimental import pallas as pl
from jax.experimental.pallas import tpu as pltpu
from jax.sharding import PartitionSpec as P

BLOCK = 128
ITERS = 3


long_range = 1.0
short_range = 0.35
nugget = 1.0
tiles_per_step = 8
rows_here = 4
chunk_bits = 1
chunk = 1 << chunk_bits
chunks_per_step = 135
tile_bytes_limit = 24 * 2**20
kernel_bytes = 12 * 2**20
f32 = jnp.float32
bf16 = jnp.bfloat16


def wendland(distance, reach):
    scaled = distance / reach
    remain = jnp.maximum(1.0 - scaled, 0.0)
    square = remain * remain
    return square * square * (4.0 * scaled + 1.0)


def covariance_tiles(row_points, column_points):
    delta_x = row_points[:, 0, :, None] - column_points[:, 0, None, :]
    delta_y = row_points[:, 1, :, None] - column_points[:, 1, None, :]
    delta_z = row_points[:, 2, :, None] - column_points[:, 2, None, :]
    distance = jnp.sqrt(delta_x * delta_x + delta_y * delta_y + delta_z * delta_z)
    kernel = wendland(distance, long_range) + wendland(distance, short_range)
    return row_points[:, 3, :, None] * kernel * column_points[:, 3, None, :]


def as_blocks(points):
    return points.reshape(4, -1, BLOCK).transpose(1, 0, 2)


def by_points(point_data, right_side, pair_list):
    col_devices = lax.axis_size("col")
    my_row = lax.axis_index("row")
    my_column = lax.axis_index("col")
    points = point_data.shape[1]
    blocks_here = points // BLOCK
    realizations = right_side.shape[0]
    own_blocks = as_blocks(point_data)
    row_blocks = as_blocks(lax.all_gather(point_data, "col", axis=1, tiled=True))
    column_blocks = as_blocks(lax.all_gather(point_data, "row", axis=1, tiled=True))
    row_count = row_blocks.shape[0]
    column_count = column_blocks.shape[0]
    lower_block = pair_list[0]
    upper_block = pair_list[1]
    this_device = my_row * col_devices + my_column
    device_of = (
        lower_block // blocks_here // col_devices * col_devices
        + upper_block // blocks_here % col_devices
    )
    roster_first_pair = jnp.sum((device_of < this_device).astype(jnp.int32))
    roster_pair_count = jnp.sum((device_of == this_device).astype(jnp.int32))
    roster_row_slot = jnp.clip(lower_block - my_row * col_devices * blocks_here, 0, row_count - 1)
    roster_column_slot = jnp.clip(
        upper_block // blocks_here // col_devices * blocks_here + upper_block % blocks_here,
        0,
        column_count - 1,
    )
    roster_step_count = (roster_pair_count + tiles_per_step - 1) // tiles_per_step
    plan = (
        roster_first_pair,
        roster_pair_count,
        roster_row_slot,
        roster_column_slot,
        roster_step_count,
        lower_block.shape[0],
    )
    first_pair, pair_count, row_slot, column_slot, step_count, listed = plan
    own_tiles = covariance_tiles(own_blocks, own_blocks).astype(jnp.bfloat16)

    def pick_tiles(step):
        offsets = step * tiles_per_step + jnp.arange(tiles_per_step)
        usable = offsets < pair_count
        picked = jnp.minimum(first_pair + offsets, listed - 1)
        row_pick = row_slot[picked]
        column_pick = column_slot[picked]
        tiles_now = covariance_tiles(row_blocks[row_pick], column_blocks[column_pick])
        tiles_now = jnp.where(usable[:, None, None], tiles_now, 0.0).astype(jnp.bfloat16)
        return (tiles_now, row_pick, column_pick)

    def inner(operands):
        stacked = jnp.stack(
            [jnp.sum(one_side * other_side, axis=1) for one_side, other_side in operands]
        )
        return lax.psum(stacked, ("row", "col"))

    solution = jnp.zeros_like(right_side)
    residual = right_side
    direction = right_side
    norm_now = inner(((residual, residual),))[0]
    for step in range(ITERS):
        rounded = direction.astype(jnp.bfloat16)
        product_row_direction = lax.all_gather(rounded, "col", axis=1, tiled=True)
        product_column_direction = lax.all_gather(rounded, "row", axis=1, tiled=True)
        row_direction = product_row_direction
        column_direction = product_column_direction
        row_direction = row_direction.reshape(realizations, row_count, BLOCK)
        column_direction = column_direction.reshape(realizations, column_count, BLOCK)

        def add_step(step, totals):
            into_rows, into_columns = totals
            tiles_now, row_pick, column_pick = pick_tiles(step)
            to_rows = jnp.einsum(
                "tij,ctj->cti",
                tiles_now,
                column_direction[:, column_pick],
                preferred_element_type=jnp.float32,
            )
            to_columns = jnp.einsum(
                "tij,cti->ctj",
                tiles_now,
                row_direction[:, row_pick],
                preferred_element_type=jnp.float32,
            )
            return (
                into_rows.at[:, row_pick].add(to_rows),
                into_columns.at[:, column_pick].add(to_columns),
            )

        empty_rows = jnp.zeros((realizations, row_count, BLOCK), jnp.float32)
        empty_columns = jnp.zeros((realizations, column_count, BLOCK), jnp.float32)
        into_rows, into_columns = lax.fori_loop(
            0, step_count, add_step, (empty_rows, empty_columns)
        )
        product_into_rows = into_rows.reshape(realizations, -1)
        product_into_columns = into_columns.reshape(realizations, -1)
        from_rows = lax.psum_scatter(product_into_rows, "col", scatter_dimension=1, tiled=True)
        from_columns = lax.psum_scatter(
            product_into_columns.astype(jnp.bfloat16), "row", scatter_dimension=1, tiled=True
        ).astype(jnp.float32)
        diagonal = jnp.einsum(
            "tij,ctj->cti",
            own_tiles,
            rounded.reshape(realizations, blocks_here, BLOCK),
            preferred_element_type=jnp.float32,
        )
        image = (
            nugget * direction + diagonal.reshape(realizations, points) + from_rows + from_columns
        )
        alpha = norm_now / inner(((direction, image),))[0]
        solution = solution + alpha[:, None] * direction
        residual = residual - alpha[:, None] * image
        if step + 1 < ITERS:
            norm_next = inner(((residual, residual),))[0]
            direction = residual + (norm_next / norm_now)[:, None] * direction
            norm_now = norm_next
    return (solution, residual)


def tile_schedule(listed, blocks):
    half = (listed + 1) // 2
    entries = half + blocks // 2
    sizes = range(40, 48)
    width = min(sizes, key=lambda size: (-(-entries // (2 * size)) * size, -size))
    steps = -(-entries // (2 * width)) * 2
    longest = (2 * half + blocks // 2 + 3 * blocks) // chunk
    chunks = -(-longest // chunks_per_step) * chunks_per_step + chunks_per_step
    return half, width, steps, chunks


def packing_kernel(point_hbm, field_hbm, outgoing_ref, point_ref, field_ref, arrived):
    devices = outgoing_ref.shape[0]
    copies = (
        pltpu.make_async_copy(point_hbm, point_ref, arrived.at[0]),
        pltpu.make_async_copy(field_hbm, field_ref, arrived.at[1]),
    )
    for copy in copies:
        copy.start()
    for copy in copies:
        copy.wait()
    row = row_number((8, BLOCK))
    blank = jnp.zeros((4, BLOCK), f32)
    high_parts, low_parts = [], []
    for block in range(2):
        points = point_ref[:, block * BLOCK : (block + 1) * BLOCK]
        high = points.astype(bf16).astype(f32)
        high_parts.append(jnp.concatenate([blank, high], axis=0))
        low_parts.append(points - high)
    low = jnp.concatenate([low_parts[1], low_parts[0]], axis=0)
    for pair in range(devices // 4):
        rows = pl.ds(8 * pair, 8)
        fields = [field_ref[rows, block * BLOCK : (block + 1) * BLOCK] for block in range(2)]
        turned = [pltpu.roll(field, 4, axis=0) for field in fields]
        for side, chosen in enumerate((fields, turned)):
            parts = [jnp.where(row < 4, chosen[block], high_parts[block]) for block in range(2)]
            message = jnp.concatenate([*parts, low], axis=0).astype(bf16)
            outgoing_ref[4 * pair + 2 * side] = message
            outgoing_ref[4 * pair + 2 * side + 1] = message


def listing_kernel(
    plan,
    blocks,
    core_ref,
    pair_hbm,
    owner_ref,
    entry_ref,
    count_ref,
    low_ref,
    high_ref,
    open_ref,
    pair_ref,
    arrived,
):
    copy = pltpu.make_async_copy(pair_hbm, pair_ref, arrived)
    copy.start()
    half, width, steps, chunks = plan
    listed = pair_ref.shape[1]
    core = core_ref[0]
    slots = width * steps

    def clear(block, carry):
        open_ref[block] = 0
        return carry

    def pad(place, carry):
        entry_ref[place] = blocks
        return carry

    lax.fori_loop(0, blocks, clear, 0, unroll=16)
    lax.fori_loop(0, chunks * chunk, pad, 0, unroll=16)

    def append(block, entry, used):
        place = open_ref[block]
        fresh = (place & (chunk - 1)) == 0
        place = jnp.where(fresh, used, place)
        open_ref[block] = place + 1
        entry_ref[place] = entry
        owner_ref[place >> chunk_bits] = block
        return jnp.where(fresh, used + chunk, used)

    def list_pair(number, used):
        low = pair_ref[0, core * half + number]
        high = pair_ref[1, core * half + number]
        low_ref[number] = low
        high_ref[number] = high
        used = append(high, number * 65536 + low, used)
        return append(low, (slots + number) * 65536 + high, used)

    def list_diagonal(number, used):
        block = core * (blocks // 2) + number
        low_ref[half + number] = block
        high_ref[half + number] = block
        return append(block, (half + number) * 65536 + block, used)

    low_ref[half - 1] = blocks
    high_ref[half - 1] = blocks
    for number in range(half + blocks // 2, slots):
        low_ref[number] = blocks
        high_ref[number] = blocks
    copy.wait()
    used = lax.fori_loop(0, listed // 2, list_pair, 0, unroll=13)
    if listed % 2:
        used = lax.fori_loop(half - 1, half - core, list_pair, used)
    used = lax.fori_loop(0, blocks // 2, list_diagonal, used, unroll=8)
    used = used >> chunk_bits
    count_ref[0] = used
    for part in range(chunks_per_step):
        owner_ref[used + part] = blocks


def radial(squared):
    squared = jnp.maximum(squared, 1e-30)
    distance = squared * lax.rsqrt(squared)
    near = jnp.maximum(1.0 - distance * (1.0 / long_range), 0.0)
    near_square = near * near
    wide = near_square * near_square * (1.25 - near)
    close = jnp.asarray(1.0, bf16) - distance.astype(bf16) * jnp.asarray(1.0 / short_range, bf16)
    close = jnp.maximum(close, jnp.asarray(0.0, bf16))
    close_square = close * close
    narrow = close_square * close_square * (jnp.asarray(1.25, bf16) - close)
    return wide.astype(bf16) + narrow


def three_parts(values):
    first = values.astype(bf16).astype(f32)
    rest = values - first
    second = rest.astype(bf16).astype(f32)
    return first, second, rest - second


def row_number(shape):
    return lax.broadcasted_iota(jnp.int32, shape, len(shape) - 2)


def store_scaled(fields_ref, direction, scale):
    blocks = direction.shape[0]
    blank = jnp.zeros((blocks, 16 - rows_here, BLOCK), f32)
    scaled = jnp.concatenate([direction * (4.0 * scale), blank], axis=1)
    fields_ref[0:blocks] = scaled.astype(bf16)
    fields_ref[blocks] = jnp.zeros((16, BLOCK), bf16)


def multiply(owner_ref, entry_ref, count, tiles_ref, fields_ref, totals_ref):
    totals_ref[...] = jnp.zeros_like(totals_ref)

    def step(number, carry):
        waiting = []

        def add(item):
            place, product = item
            totals_ref[owner_ref[place]] += product

        for part in range(chunks_per_step):
            place = number * chunks_per_step + part
            fields = []
            tiles = []
            for slot in range(chunk):
                entry = entry_ref[place * chunk + slot]
                fields.append(fields_ref[entry & 65535])
                tiles.append(tiles_ref[entry >> 16])
            product = jnp.dot(
                jnp.concatenate(fields, axis=1),
                jnp.concatenate(tiles, axis=0),
                preferred_element_type=f32,
            )
            waiting.append((place, product[0:8]))
            if len(waiting) > 8:
                add(waiting.pop(0))
        for item in waiting:
            add(item)
        return carry

    lax.fori_loop(0, (count + chunks_per_step - 1) // chunks_per_step, step, 0)


def first_kernel(
    plan,
    low_ref,
    high_ref,
    received_ref,
    tiles_ref,
    product_ref,
    gathered_ref,
    left_ref,
    right_ref,
    fields_ref,
    totals_ref,
    *stages,
):
    half, width, steps, _ = plan
    blocks = gathered_ref.shape[0]
    slots = width * steps
    for device in range(blocks // 2):
        message = received_ref[device].astype(f32)
        lower = message[16:24]
        is_point = row_number((8, BLOCK)) >= rows_here
        first = message[0:8] + jnp.where(is_point, lower, 0.0)
        second = message[8:16] + jnp.where(is_point, pltpu.roll(lower, 4, axis=0), 0.0)
        gathered_ref[2 * device] = first
        gathered_ref[2 * device + 1] = second
    highest = jnp.max(jnp.max(gathered_ref[...], axis=0), axis=1, keepdims=True)
    lowest = jnp.min(jnp.min(gathered_ref[...], axis=0), axis=1, keepdims=True)
    centre = 0.5 * (highest + lowest)

    def prepare(block, carry):
        row = row_number((8, BLOCK))
        is_coordinate = (row >= 4) & (row < 7)
        shifted = jnp.where(is_coordinate, gathered_ref[block] - centre, 0.0)
        squared = jnp.sum(shifted * shifted, axis=0, keepdims=True)
        left = jnp.where(row == 7, 1.0, jnp.where(row == 0, squared, shifted))
        right = jnp.where(row == 7, squared, jnp.where(row == 0, 1.0, -2.0 * shifted))
        left_1, left_2, left_3 = three_parts(left)
        right_1, right_2, right_3 = three_parts(right)
        left_all = jnp.concatenate([left_1, left_1, left_2, left_2, left_1, left_3], axis=0)
        right_all = jnp.concatenate([right_1, right_2, right_1, right_2, right_3, right_1], axis=0)
        left_ref[block] = left_all.T.astype(bf16)
        right_ref[block] = right_all.astype(bf16)
        return carry

    lax.fori_loop(0, blocks, prepare, 0, unroll=32)
    left_ref[blocks] = jnp.zeros((BLOCK, 48), bf16)
    right_ref[blocks] = jnp.zeros((48, BLOCK), bf16)
    store_scaled(fields_ref, gathered_ref[:, 0:rows_here, :], gathered_ref[:, 7:8, :])
    totals_ref[...] = jnp.zeros_like(totals_ref)

    def square(step, slot):
        number = step * width + slot
        return jnp.dot(
            left_ref[low_ref[number]], right_ref[high_ref[number]], preferred_element_type=f32
        )

    def make_tile(step, slot, stage, squared):
        number = step * width + slot
        tile = radial(squared)
        turned = tile.T
        tiles_ref[number] = tile
        tiles_ref[slots + number] = turned
        stage[0][slot] = tile
        stage[1][slot] = turned

    def use_tile(step, slot, stage):
        number = step * width + slot
        made = jnp.maximum(number, 0)
        low = jnp.where(number >= 0, low_ref[made], blocks)
        high = jnp.where(number >= 0, high_ref[made], blocks)
        is_pair = number < half
        ways = (
            (low, high),
            (jnp.where(is_pair, high, blocks), jnp.where(is_pair, low, blocks)),
        )
        products = []
        for (source, target), tiles in zip(ways, stage):
            product = jnp.dot(fields_ref[source], tiles[slot], preferred_element_type=f32)
            products.append((target, product[0:8]))
        return products

    def add_products(products):
        for target, product in products:
            totals_ref[target] += product

    def use_tiles(step, stage):
        for slot in range(width):
            add_products(use_tile(step, slot, stage))

    def both(step, new_stage, old_stage):
        waiting = []
        ahead = square(step, 0)
        for slot in range(width):
            squared = ahead
            if slot + 1 < width:
                ahead = square(step, slot + 1)
            make_tile(step, slot, new_stage, squared)
            waiting.append(use_tile(step - 1, slot, old_stage))
            if len(waiting) > 2:
                add_products(waiting.pop(0))
        for products in waiting:
            add_products(products)

    even, odd = stages[0:2], stages[2:4]

    def both_steps(pair, carry):
        both(2 * pair, even, odd)
        both(2 * pair + 1, odd, even)
        return carry

    lax.fori_loop(0, steps // 2, both_steps, 0)
    use_tiles(steps - 1, odd)
    product_ref[...] = totals_ref[0:blocks, 0:rows_here, :]


def total(values):
    return jnp.sum(jnp.sum(values, axis=0), axis=1, keepdims=True)[None]


def advance(mine_ref, other_ref, scale, direction, residual):
    image = nugget * direction + scale * (mine_ref[...] + other_ref[...])
    norm_now = total(residual * residual)
    along = total(direction * image)
    alpha = norm_now / along
    return alpha * direction, residual - alpha * image, norm_now


def next_kernel(
    first,
    owner_ref,
    entry_ref,
    count_ref,
    gathered_ref,
    mine_ref,
    other_ref,
    *rest,
):
    if first:
        tiles_ref, product_ref, state_out_ref, fields_ref, totals_ref = rest
        direction = gathered_ref[:, 0:rows_here, :]
        residual = direction
    else:
        state_ref, tiles_ref, product_ref, state_out_ref, fields_ref, totals_ref = rest
        direction = state_ref[2]
        residual = state_ref[1]
    scale = gathered_ref[:, 7:8, :]
    moved, residual, norm_now = advance(mine_ref, other_ref, scale, direction, residual)
    norm_next = total(residual * residual)
    direction = residual + (norm_next / norm_now) * direction
    state_out_ref[0] = moved if first else state_ref[0] + moved
    state_out_ref[1] = residual
    state_out_ref[2] = direction
    store_scaled(fields_ref, direction, scale)
    multiply(owner_ref, entry_ref, count_ref[0], tiles_ref, fields_ref, totals_ref)
    product_ref[...] = totals_ref[0 : gathered_ref.shape[0], 0:rows_here, :]


def last_kernel(core_ref, gathered_ref, mine_ref, other_ref, state_ref, result_ref):
    scale = gathered_ref[:, 7:8, :]
    moved, residual, _ = advance(mine_ref, other_ref, scale, state_ref[2], state_ref[1])
    chosen = jnp.where(core_ref[0] == 0, state_ref[0] + moved, residual)
    result_ref[...] = chosen.astype(bf16)


def by_realizations(point_data, right_side, pair_list):
    col_devices = lax.axis_size("col")
    devices = lax.axis_size("row") * col_devices
    chips = devices // 2
    blocks_here = point_data.shape[1] // BLOCK
    blocks = blocks_here * devices
    core = lax.rem(lax.axis_index("col"), 2).astype(jnp.int32).reshape(1)
    axes = ("row", "col")
    vector = pl.BlockSpec(memory_space=pltpu.VMEM)
    scalar = pl.BlockSpec(memory_space=pltpu.SMEM)
    plan = tile_schedule(pair_list.shape[1], blocks)
    half, width, steps, chunks = plan
    slots = width * steps

    limits = pltpu.CompilerParams(vmem_limit_bytes=kernel_bytes)
    outgoing = pl.pallas_call(
        packing_kernel,
        out_shape=jax.ShapeDtypeStruct((devices, 24, BLOCK), bf16),
        in_specs=[pl.BlockSpec(memory_space=pltpu.HBM)] * 2,
        out_specs=vector,
        scratch_shapes=[
            pltpu.VMEM(point_data.shape, f32),
            pltpu.VMEM(right_side.shape, f32),
            pltpu.SemaphoreType.DMA((2,)),
        ],
        compiler_params=limits,
    )(
        pltpu.with_memory_space_constraint(point_data, pltpu.HBM),
        pltpu.with_memory_space_constraint(right_side, pltpu.HBM),
    )
    owner, entry, count, low, high = pl.pallas_call(
        functools.partial(listing_kernel, plan, blocks),
        out_shape=(
            pltpu.SMEM((chunks + 8,), jnp.int32),
            pltpu.SMEM((chunks * chunk + 8,), jnp.int32),
            pltpu.SMEM((1,), jnp.int32),
            pltpu.SMEM((slots,), jnp.int32),
            pltpu.SMEM((slots,), jnp.int32),
        ),
        in_specs=[scalar, pl.BlockSpec(memory_space=pltpu.HBM)],
        out_specs=(scalar,) * 5,
        scratch_shapes=[
            pltpu.SMEM((blocks,), jnp.int32),
            pltpu.SMEM(pair_list.shape, jnp.int32),
            pltpu.SemaphoreType.DMA,
        ],
        cost_estimate=pl.CostEstimate(flops=8_000_000_000, bytes_accessed=20_000_000, transcendentals=0),
        compiler_params=limits,
    )(core, pltpu.with_memory_space_constraint(pair_list, pltpu.HBM))
    received = lax.all_to_all(outgoing, axes, 0, 0, tiled=True)

    field_shape = jax.ShapeDtypeStruct((blocks, 8, BLOCK), f32)
    product_shape = jax.ShapeDtypeStruct((blocks, rows_here, BLOCK), f32)
    state_shape = jax.ShapeDtypeStruct((3, blocks, rows_here, BLOCK), f32)
    work = [pltpu.VMEM((blocks + 1, 16, BLOCK), bf16), pltpu.VMEM((blocks + 1, 8, BLOCK), f32)]
    stage = pltpu.VMEM((width, BLOCK, BLOCK), bf16)
    tiles, mine, gathered = pl.pallas_call(
        functools.partial(first_kernel, plan),
        out_shape=(pltpu.VMEM((2 * slots, BLOCK, BLOCK), bf16), product_shape, field_shape),
        in_specs=[scalar, scalar, vector],
        out_specs=(vector, vector, vector),
        scratch_shapes=[
            pltpu.VMEM((blocks + 1, BLOCK, 48), bf16),
            pltpu.VMEM((blocks + 1, 48, BLOCK), bf16),
            *work,
            *[stage] * 4,
        ],
        compiler_params=limits,
    )(low, high, received)
    tiles = pltpu.with_memory_space_constraint(tiles, pltpu.VMEM)
    swap = [(place, place ^ 1) for place in range(col_devices)]
    state = None
    for step in range(1, ITERS):
        other = lax.ppermute(mine, "col", swap)
        first = step == 1
        carried = () if first else (state,)
        mine, state = pl.pallas_call(
            functools.partial(next_kernel, first),
            out_shape=(product_shape, state_shape),
            in_specs=[scalar, scalar, scalar] + [vector] * (4 + len(carried)),
            out_specs=(vector, vector),
            scratch_shapes=work,
            compiler_params=limits,
        )(owner, entry, count, gathered, mine, other, *carried, tiles)
    other = lax.ppermute(mine, "col", swap)
    result = pl.pallas_call(
        last_kernel,
        out_shape=jax.ShapeDtypeStruct((blocks, rows_here, BLOCK), bf16),
        in_specs=[scalar] + [vector] * 4,
        out_specs=vector,
        compiler_params=limits,
    )(core, gathered, mine, other, state)
    result = result.reshape(devices, blocks_here, rows_here, BLOCK)
    received = lax.all_to_all(result, axes, 0, 0, tiled=True)
    received = received.reshape(chips, 2, blocks_here, rows_here, BLOCK)
    received = received.transpose(1, 0, 3, 2, 4).reshape(2, right_side.shape[0], -1)
    return received[0].astype(f32), received[1].astype(f32)


def per_device(point_data, right_side, pair_list):
    col_devices = lax.axis_size("col")
    devices = lax.axis_size("row") * col_devices
    blocks = point_data.shape[1] // BLOCK * devices
    _, width, steps, _ = tile_schedule(pair_list.shape[1], blocks)
    tile_bytes = 2 * width * steps * BLOCK * BLOCK * 2
    paired = devices % 4 == 0 and col_devices % 2 == 0 and blocks == 2 * devices
    if paired and right_side.shape[0] == rows_here * (devices // 2) and tile_bytes <= tile_bytes_limit:
        return by_realizations(point_data, right_side, pair_list)
    return by_points(point_data, right_side, pair_list)


def solution(mesh):
    placed = (P(None, ("row", "col")), P(None, ("row", "col")), P())
    return jax.shard_map(
        per_device,
        mesh=mesh,
        in_specs=placed,
        out_specs=(P(None, ("row", "col")), P(None, ("row", "col"))),
        check_vma=False,
    )
```

```python
import functools
import jax
import jax.numpy as jnp
from jax import lax
from jax.experimental import pallas as pl
from jax.experimental.pallas import tpu as pltpu
from jax.sharding import PartitionSpec as P

BLOCK = 128
ITERS = 3


long_range = 1.0
short_range = 0.35
nugget = 1.0
tiles_per_step = 8
rows_here = 4
chunk_bits = 1
chunk = 1 << chunk_bits
chunks_per_step = 135
tile_bytes_limit = 24 * 2**20
kernel_bytes = 12 * 2**20
f32 = jnp.float32
bf16 = jnp.bfloat16


def wendland(distance, reach):
    scaled = distance / reach
    remain = jnp.maximum(1.0 - scaled, 0.0)
    square = remain * remain
    return square * square * (4.0 * scaled + 1.0)


def covariance_tiles(row_points, column_points):
    delta_x = row_points[:, 0, :, None] - column_points[:, 0, None, :]
    delta_y = row_points[:, 1, :, None] - column_points[:, 1, None, :]
    delta_z = row_points[:, 2, :, None] - column_points[:, 2, None, :]
    distance = jnp.sqrt(delta_x * delta_x + delta_y * delta_y + delta_z * delta_z)
    kernel = wendland(distance, long_range) + wendland(distance, short_range)
    return row_points[:, 3, :, None] * kernel * column_points[:, 3, None, :]


def as_blocks(points):
    return points.reshape(4, -1, BLOCK).transpose(1, 0, 2)


def by_points(point_data, right_side, pair_list):
    col_devices = lax.axis_size("col")
    my_row = lax.axis_index("row")
    my_column = lax.axis_index("col")
    points = point_data.shape[1]
    blocks_here = points // BLOCK
    realizations = right_side.shape[0]
    own_blocks = as_blocks(point_data)
    row_blocks = as_blocks(lax.all_gather(point_data, "col", axis=1, tiled=True))
    column_blocks = as_blocks(lax.all_gather(point_data, "row", axis=1, tiled=True))
    row_count = row_blocks.shape[0]
    column_count = column_blocks.shape[0]
    lower_block = pair_list[0]
    upper_block = pair_list[1]
    this_device = my_row * col_devices + my_column
    device_of = (
        lower_block // blocks_here // col_devices * col_devices
        + upper_block // blocks_here % col_devices
    )
    roster_first_pair = jnp.sum((device_of < this_device).astype(jnp.int32))
    roster_pair_count = jnp.sum((device_of == this_device).astype(jnp.int32))
    roster_row_slot = jnp.clip(lower_block - my_row * col_devices * blocks_here, 0, row_count - 1)
    roster_column_slot = jnp.clip(
        upper_block // blocks_here // col_devices * blocks_here + upper_block % blocks_here,
        0,
        column_count - 1,
    )
    roster_step_count = (roster_pair_count + tiles_per_step - 1) // tiles_per_step
    plan = (
        roster_first_pair,
        roster_pair_count,
        roster_row_slot,
        roster_column_slot,
        roster_step_count,
        lower_block.shape[0],
    )
    first_pair, pair_count, row_slot, column_slot, step_count, listed = plan
    own_tiles = covariance_tiles(own_blocks, own_blocks).astype(jnp.bfloat16)

    def pick_tiles(step):
        offsets = step * tiles_per_step + jnp.arange(tiles_per_step)
        usable = offsets < pair_count
        picked = jnp.minimum(first_pair + offsets, listed - 1)
        row_pick = row_slot[picked]
        column_pick = column_slot[picked]
        tiles_now = covariance_tiles(row_blocks[row_pick], column_blocks[column_pick])
        tiles_now = jnp.where(usable[:, None, None], tiles_now, 0.0).astype(jnp.bfloat16)
        return (tiles_now, row_pick, column_pick)

    def inner(operands):
        stacked = jnp.stack(
            [jnp.sum(one_side * other_side, axis=1) for one_side, other_side in operands]
        )
        return lax.psum(stacked, ("row", "col"))

    solution = jnp.zeros_like(right_side)
    residual = right_side
    direction = right_side
    norm_now = inner(((residual, residual),))[0]
    for step in range(ITERS):
        rounded = direction.astype(jnp.bfloat16)
        product_row_direction = lax.all_gather(rounded, "col", axis=1, tiled=True)
        product_column_direction = lax.all_gather(rounded, "row", axis=1, tiled=True)
        row_direction = product_row_direction
        column_direction = product_column_direction
        row_direction = row_direction.reshape(realizations, row_count, BLOCK)
        column_direction = column_direction.reshape(realizations, column_count, BLOCK)

        def add_step(step, totals):
            into_rows, into_columns = totals
            tiles_now, row_pick, column_pick = pick_tiles(step)
            to_rows = jnp.einsum(
                "tij,ctj->cti",
                tiles_now,
                column_direction[:, column_pick],
                preferred_element_type=jnp.float32,
            )
            to_columns = jnp.einsum(
                "tij,cti->ctj",
                tiles_now,
                row_direction[:, row_pick],
                preferred_element_type=jnp.float32,
            )
            return (
                into_rows.at[:, row_pick].add(to_rows),
                into_columns.at[:, column_pick].add(to_columns),
            )

        empty_rows = jnp.zeros((realizations, row_count, BLOCK), jnp.float32)
        empty_columns = jnp.zeros((realizations, column_count, BLOCK), jnp.float32)
        into_rows, into_columns = lax.fori_loop(
            0, step_count, add_step, (empty_rows, empty_columns)
        )
        product_into_rows = into_rows.reshape(realizations, -1)
        product_into_columns = into_columns.reshape(realizations, -1)
        from_rows = lax.psum_scatter(product_into_rows, "col", scatter_dimension=1, tiled=True)
        from_columns = lax.psum_scatter(
            product_into_columns.astype(jnp.bfloat16), "row", scatter_dimension=1, tiled=True
        ).astype(jnp.float32)
        diagonal = jnp.einsum(
            "tij,ctj->cti",
            own_tiles,
            rounded.reshape(realizations, blocks_here, BLOCK),
            preferred_element_type=jnp.float32,
        )
        image = (
            nugget * direction + diagonal.reshape(realizations, points) + from_rows + from_columns
        )
        alpha = norm_now / inner(((direction, image),))[0]
        solution = solution + alpha[:, None] * direction
        residual = residual - alpha[:, None] * image
        if step + 1 < ITERS:
            norm_next = inner(((residual, residual),))[0]
            direction = residual + (norm_next / norm_now)[:, None] * direction
            norm_now = norm_next
    return (solution, residual)


def tile_schedule(listed, blocks):
    half = (listed + 1) // 2
    entries = half + blocks // 2
    sizes = range(40, 48)
    width = min(sizes, key=lambda size: (-(-entries // (2 * size)) * size, -size))
    steps = -(-entries // (2 * width)) * 2
    longest = (2 * half + blocks // 2 + 3 * blocks) // chunk
    chunks = -(-longest // chunks_per_step) * chunks_per_step + chunks_per_step
    return half, width, steps, chunks


def packing_kernel(point_hbm, field_hbm, outgoing_ref, point_ref, field_ref, arrived):
    devices = outgoing_ref.shape[0]
    copies = (
        pltpu.make_async_copy(point_hbm, point_ref, arrived.at[0]),
        pltpu.make_async_copy(field_hbm, field_ref, arrived.at[1]),
    )
    for copy in copies:
        copy.start()
    for copy in copies:
        copy.wait()
    row = row_number((8, BLOCK))
    blank = jnp.zeros((4, BLOCK), f32)
    high_parts, low_parts = [], []
    for block in range(2):
        points = point_ref[:, block * BLOCK : (block + 1) * BLOCK]
        high = points.astype(bf16).astype(f32)
        high_parts.append(jnp.concatenate([blank, high], axis=0))
        low_parts.append(points - high)
    low = jnp.concatenate([low_parts[1], low_parts[0]], axis=0)
    for pair in range(devices // 4):
        rows = pl.ds(8 * pair, 8)
        fields = [field_ref[rows, block * BLOCK : (block + 1) * BLOCK] for block in range(2)]
        turned = [pltpu.roll(field, 4, axis=0) for field in fields]
        for side, chosen in enumerate((fields, turned)):
            parts = [jnp.where(row < 4, chosen[block], high_parts[block]) for block in range(2)]
            message = jnp.concatenate([*parts, low], axis=0).astype(bf16)
            outgoing_ref[4 * pair + 2 * side] = message
            outgoing_ref[4 * pair + 2 * side + 1] = message


def listing_kernel(
    plan,
    blocks,
    core_ref,
    pair_hbm,
    owner_ref,
    entry_ref,
    count_ref,
    low_ref,
    high_ref,
    open_ref,
    pair_ref,
    arrived,
):
    copy = pltpu.make_async_copy(pair_hbm, pair_ref, arrived)
    copy.start()
    half, width, steps, chunks = plan
    listed = pair_ref.shape[1]
    core = core_ref[0]
    slots = width * steps

    def clear(block, carry):
        open_ref[block] = 0
        return carry

    def pad(place, carry):
        entry_ref[place] = blocks
        return carry

    lax.fori_loop(0, blocks, clear, 0, unroll=16)
    lax.fori_loop(0, chunks * chunk, pad, 0, unroll=16)

    def append(block, entry, used):
        place = open_ref[block]
        fresh = (place & (chunk - 1)) == 0
        place = jnp.where(fresh, used, place)
        open_ref[block] = place + 1
        entry_ref[place] = entry
        owner_ref[place >> chunk_bits] = block
        return jnp.where(fresh, used + chunk, used)

    def list_pair(number, used):
        low = pair_ref[0, core * half + number]
        high = pair_ref[1, core * half + number]
        low_ref[number] = low
        high_ref[number] = high
        used = append(high, number * 65536 + low, used)
        return append(low, (slots + number) * 65536 + high, used)

    def list_diagonal(number, used):
        block = core * (blocks // 2) + number
        low_ref[half + number] = block
        high_ref[half + number] = block
        return append(block, (half + number) * 65536 + block, used)

    low_ref[half - 1] = blocks
    high_ref[half - 1] = blocks
    for number in range(half + blocks // 2, slots):
        low_ref[number] = blocks
        high_ref[number] = blocks
    copy.wait()
    used = lax.fori_loop(0, listed // 2, list_pair, 0, unroll=13)
    if listed % 2:
        used = lax.fori_loop(half - 1, half - core, list_pair, used)
    used = lax.fori_loop(0, blocks // 2, list_diagonal, used, unroll=8)
    used = used >> chunk_bits
    count_ref[0] = used
    for part in range(chunks_per_step):
        owner_ref[used + part] = blocks


def radial(squared):
    squared = jnp.maximum(squared, 1e-30)
    distance = squared * lax.rsqrt(squared)
    near = jnp.maximum(1.0 - distance * (1.0 / long_range), 0.0)
    near_square = near * near
    wide = near_square * near_square * (0.25 + distance)
    close = jnp.asarray(1.0, bf16) - distance.astype(bf16) * jnp.asarray(1.0 / short_range, bf16)
    close = jnp.maximum(close, jnp.asarray(0.0, bf16))
    close_square = close * close
    narrow = close_square * close_square * (jnp.asarray(1.25, bf16) - close)
    return wide.astype(bf16) + narrow


def three_parts(values):
    first = values.astype(bf16).astype(f32)
    rest = values - first
    second = rest.astype(bf16).astype(f32)
    return first, second, rest - second


def row_number(shape):
    return lax.broadcasted_iota(jnp.int32, shape, len(shape) - 2)


def store_scaled(fields_ref, direction, scale):
    blocks = direction.shape[0]
    blank = jnp.zeros((blocks, 16 - rows_here, BLOCK), f32)
    scaled = jnp.concatenate([direction * (4.0 * scale), blank], axis=1)
    fields_ref[0:blocks] = scaled.astype(bf16)
    fields_ref[blocks] = jnp.zeros((16, BLOCK), bf16)


def multiply(owner_ref, entry_ref, count, tiles_ref, fields_ref, totals_ref):
    totals_ref[...] = jnp.zeros_like(totals_ref)

    def step(number, carry):
        waiting = []

        def add(item):
            place, product = item
            totals_ref[owner_ref[place]] += product

        for part in range(chunks_per_step):
            place = number * chunks_per_step + part
            fields = []
            tiles = []
            for slot in range(chunk):
                entry = entry_ref[place * chunk + slot]
                fields.append(fields_ref[entry & 65535])
                tiles.append(tiles_ref[entry >> 16])
            product = jnp.dot(
                jnp.concatenate(fields, axis=1),
                jnp.concatenate(tiles, axis=0),
                preferred_element_type=f32,
            )
            waiting.append((place, product[0:8]))
            if len(waiting) > 8:
                add(waiting.pop(0))
        for item in waiting:
            add(item)
        return carry

    lax.fori_loop(0, (count + chunks_per_step - 1) // chunks_per_step, step, 0)


def first_kernel(
    plan,
    low_ref,
    high_ref,
    received_ref,
    tiles_ref,
    product_ref,
    gathered_ref,
    left_ref,
    right_ref,
    fields_ref,
    totals_ref,
    *stages,
):
    half, width, steps, _ = plan
    blocks = gathered_ref.shape[0]
    slots = width * steps
    for device in range(blocks // 2):
        message = received_ref[device].astype(f32)
        lower = message[16:24]
        is_point = row_number((8, BLOCK)) >= rows_here
        first = message[0:8] + jnp.where(is_point, lower, 0.0)
        second = message[8:16] + jnp.where(is_point, pltpu.roll(lower, 4, axis=0), 0.0)
        gathered_ref[2 * device] = first
        gathered_ref[2 * device + 1] = second
    highest = jnp.max(jnp.max(gathered_ref[...], axis=0), axis=1, keepdims=True)
    lowest = jnp.min(jnp.min(gathered_ref[...], axis=0), axis=1, keepdims=True)
    centre = 0.5 * (highest + lowest)

    def prepare(block, carry):
        row = row_number((8, BLOCK))
        is_coordinate = (row >= 4) & (row < 7)
        shifted = jnp.where(is_coordinate, gathered_ref[block] - centre, 0.0)
        squared = jnp.sum(shifted * shifted, axis=0, keepdims=True)
        left = jnp.where(row == 7, 1.0, jnp.where(row == 0, squared, shifted))
        right = jnp.where(row == 7, squared, jnp.where(row == 0, 1.0, -2.0 * shifted))
        left_1, left_2, left_3 = three_parts(left)
        right_1, right_2, right_3 = three_parts(right)
        left_all = jnp.concatenate([left_1, left_1, left_2, left_2, left_1, left_3], axis=0)
        right_all = jnp.concatenate([right_1, right_2, right_1, right_2, right_3, right_1], axis=0)
        left_ref[block] = left_all.T.astype(bf16)
        right_ref[block] = right_all.astype(bf16)
        return carry

    lax.fori_loop(0, blocks, prepare, 0, unroll=32)
    left_ref[blocks] = jnp.zeros((BLOCK, 48), bf16)
    right_ref[blocks] = jnp.zeros((48, BLOCK), bf16)
    store_scaled(fields_ref, gathered_ref[:, 0:rows_here, :], gathered_ref[:, 7:8, :])
    totals_ref[...] = jnp.zeros_like(totals_ref)

    def square(step, slot):
        number = step * width + slot
        return jnp.dot(
            left_ref[low_ref[number]], right_ref[high_ref[number]], preferred_element_type=f32
        )

    def make_tile(step, slot, stage, squared):
        number = step * width + slot
        tile = radial(squared)
        turned = tile.T
        tiles_ref[number] = tile
        tiles_ref[slots + number] = turned
        stage[0][slot] = tile
        stage[1][slot] = turned

    def use_tile(step, slot, stage):
        number = step * width + slot
        made = jnp.maximum(number, 0)
        low = jnp.where(number >= 0, low_ref[made], blocks)
        high = jnp.where(number >= 0, high_ref[made], blocks)
        is_pair = number < half
        ways = (
            (low, high),
            (jnp.where(is_pair, high, blocks), jnp.where(is_pair, low, blocks)),
        )
        products = []
        for (source, target), tiles in zip(ways, stage):
            product = jnp.dot(fields_ref[source], tiles[slot], preferred_element_type=f32)
            products.append((target, product[0:8]))
        return products

    def add_products(products):
        for target, product in products:
            totals_ref[target] += product

    def use_tiles(step, stage):
        for slot in range(width):
            add_products(use_tile(step, slot, stage))

    def both(step, new_stage, old_stage):
        waiting = []
        ahead = square(step, 0)
        for slot in range(width):
            squared = ahead
            if slot + 1 < width:
                ahead = square(step, slot + 1)
            make_tile(step, slot, new_stage, squared)
            waiting.append(use_tile(step - 1, slot, old_stage))
            if len(waiting) > 2:
                add_products(waiting.pop(0))
        for products in waiting:
            add_products(products)

    even, odd = stages[0:2], stages[2:4]

    def both_steps(pair, carry):
        both(2 * pair, even, odd)
        both(2 * pair + 1, odd, even)
        return carry

    lax.fori_loop(0, steps // 2, both_steps, 0)
    use_tiles(steps - 1, odd)
    product_ref[...] = totals_ref[0:blocks, 0:rows_here, :]


def total(values):
    return jnp.sum(jnp.sum(values, axis=0), axis=1, keepdims=True)[None]


def advance(mine_ref, other_ref, scale, direction, residual):
    image = nugget * direction + scale * (mine_ref[...] + other_ref[...])
    norm_now = total(residual * residual)
    along = total(direction * image)
    alpha = norm_now / along
    return alpha * direction, residual - alpha * image, norm_now


def next_kernel(
    first,
    owner_ref,
    entry_ref,
    count_ref,
    gathered_ref,
    mine_ref,
    other_ref,
    *rest,
):
    if first:
        tiles_ref, product_ref, state_out_ref, fields_ref, totals_ref = rest
        direction = gathered_ref[:, 0:rows_here, :]
        residual = direction
    else:
        state_ref, tiles_ref, product_ref, state_out_ref, fields_ref, totals_ref = rest
        direction = state_ref[2]
        residual = state_ref[1]
    scale = gathered_ref[:, 7:8, :]
    moved, residual, norm_now = advance(mine_ref, other_ref, scale, direction, residual)
    norm_next = total(residual * residual)
    direction = residual + (norm_next / norm_now) * direction
    state_out_ref[0] = moved if first else state_ref[0] + moved
    state_out_ref[1] = residual
    state_out_ref[2] = direction
    store_scaled(fields_ref, direction, scale)
    multiply(owner_ref, entry_ref, count_ref[0], tiles_ref, fields_ref, totals_ref)
    product_ref[...] = totals_ref[0 : gathered_ref.shape[0], 0:rows_here, :]


def last_kernel(core_ref, gathered_ref, mine_ref, other_ref, state_ref, result_ref):
    scale = gathered_ref[:, 7:8, :]
    moved, residual, _ = advance(mine_ref, other_ref, scale, state_ref[2], state_ref[1])
    chosen = jnp.where(core_ref[0] == 0, state_ref[0] + moved, residual)
    for device in range(result_ref.shape[0]):
        both = jnp.concatenate([chosen[2 * device], chosen[2 * device + 1]], axis=0)
        result_ref[device] = both.astype(bf16)


def unpacking_kernel(received_ref, solution_ref, residual_ref):
    row = row_number((8, BLOCK))
    for pair in range(received_ref.shape[0] // 4):
        for side, output_ref in enumerate((solution_ref, residual_ref)):
            even = received_ref[4 * pair + side].astype(f32)
            odd = received_ref[4 * pair + 2 + side].astype(f32)
            rows = pl.ds(8 * pair, 8)
            turned = pltpu.roll(odd, 4, axis=0)
            output_ref[rows, 0:BLOCK] = jnp.where(row < 4, even, turned)
            turned = pltpu.roll(even, 4, axis=0)
            output_ref[rows, BLOCK : 2 * BLOCK] = jnp.where(row < 4, turned, odd)


def by_realizations(point_data, right_side, pair_list):
    col_devices = lax.axis_size("col")
    devices = lax.axis_size("row") * col_devices
    chips = devices // 2
    blocks_here = point_data.shape[1] // BLOCK
    blocks = blocks_here * devices
    core = lax.rem(lax.axis_index("col"), 2).astype(jnp.int32).reshape(1)
    axes = ("row", "col")
    vector = pl.BlockSpec(memory_space=pltpu.VMEM)
    scalar = pl.BlockSpec(memory_space=pltpu.SMEM)
    plan = tile_schedule(pair_list.shape[1], blocks)
    half, width, steps, chunks = plan
    slots = width * steps

    limits = pltpu.CompilerParams(vmem_limit_bytes=kernel_bytes)
    outgoing = pl.pallas_call(
        packing_kernel,
        out_shape=jax.ShapeDtypeStruct((devices, 24, BLOCK), bf16),
        in_specs=[pl.BlockSpec(memory_space=pltpu.HBM)] * 2,
        out_specs=vector,
        scratch_shapes=[
            pltpu.VMEM(point_data.shape, f32),
            pltpu.VMEM(right_side.shape, f32),
            pltpu.SemaphoreType.DMA((2,)),
        ],
        compiler_params=limits,
    )(
        pltpu.with_memory_space_constraint(point_data, pltpu.HBM),
        pltpu.with_memory_space_constraint(right_side, pltpu.HBM),
    )
    owner, entry, count, low, high = pl.pallas_call(
        functools.partial(listing_kernel, plan, blocks),
        out_shape=(
            pltpu.SMEM((chunks + 8,), jnp.int32),
            pltpu.SMEM((chunks * chunk + 8,), jnp.int32),
            pltpu.SMEM((1,), jnp.int32),
            pltpu.SMEM((slots,), jnp.int32),
            pltpu.SMEM((slots,), jnp.int32),
        ),
        in_specs=[scalar, pl.BlockSpec(memory_space=pltpu.HBM)],
        out_specs=(scalar,) * 5,
        scratch_shapes=[
            pltpu.SMEM((blocks,), jnp.int32),
            pltpu.SMEM(pair_list.shape, jnp.int32),
            pltpu.SemaphoreType.DMA,
        ],
        cost_estimate=pl.CostEstimate(flops=8_000_000_000, bytes_accessed=20_000_000, transcendentals=0),
        compiler_params=limits,
    )(core, pltpu.with_memory_space_constraint(pair_list, pltpu.HBM))
    received = lax.all_to_all(outgoing, axes, 0, 0, tiled=True)

    field_shape = jax.ShapeDtypeStruct((blocks, 8, BLOCK), f32)
    product_shape = jax.ShapeDtypeStruct((blocks, rows_here, BLOCK), f32)
    state_shape = jax.ShapeDtypeStruct((3, blocks, rows_here, BLOCK), f32)
    work = [pltpu.VMEM((blocks + 1, 16, BLOCK), bf16), pltpu.VMEM((blocks + 1, 8, BLOCK), f32)]
    stage = pltpu.VMEM((width, BLOCK, BLOCK), bf16)
    tiles, mine, gathered = pl.pallas_call(
        functools.partial(first_kernel, plan),
        out_shape=(pltpu.VMEM((2 * slots, BLOCK, BLOCK), bf16), product_shape, field_shape),
        in_specs=[scalar, scalar, vector],
        out_specs=(vector, vector, vector),
        scratch_shapes=[
            pltpu.VMEM((blocks + 1, BLOCK, 48), bf16),
            pltpu.VMEM((blocks + 1, 48, BLOCK), bf16),
            *work,
            *[stage] * 4,
        ],
        compiler_params=limits,
    )(low, high, received)
    tiles = pltpu.with_memory_space_constraint(tiles, pltpu.VMEM)
    swap = [(place, place ^ 1) for place in range(col_devices)]
    state = None
    for step in range(1, ITERS):
        other = lax.ppermute(mine, "col", swap)
        first = step == 1
        carried = () if first else (state,)
        mine, state = pl.pallas_call(
            functools.partial(next_kernel, first),
            out_shape=(product_shape, state_shape),
            in_specs=[scalar, scalar, scalar] + [vector] * (4 + len(carried)),
            out_specs=(vector, vector),
            scratch_shapes=work,
            compiler_params=limits,
        )(owner, entry, count, gathered, mine, other, *carried, tiles)
    other = lax.ppermute(mine, "col", swap)
    result = pl.pallas_call(
        last_kernel,
        out_shape=jax.ShapeDtypeStruct((devices, 2 * rows_here, BLOCK), bf16),
        in_specs=[scalar] + [vector] * 4,
        out_specs=vector,
        compiler_params=limits,
    )(core, gathered, mine, other, state)
    received = lax.all_to_all(result, axes, 0, 0, tiled=True)
    output_shape = jax.ShapeDtypeStruct(right_side.shape, f32)
    return pl.pallas_call(
        unpacking_kernel,
        out_shape=(output_shape, output_shape),
        in_specs=[vector],
        out_specs=(vector, vector),
        compiler_params=limits,
    )(received)


def per_device(point_data, right_side, pair_list):
    col_devices = lax.axis_size("col")
    devices = lax.axis_size("row") * col_devices
    blocks = point_data.shape[1] // BLOCK * devices
    _, width, steps, _ = tile_schedule(pair_list.shape[1], blocks)
    tile_bytes = 2 * width * steps * BLOCK * BLOCK * 2
    paired = devices % 4 == 0 and col_devices % 2 == 0 and blocks == 2 * devices
    if paired and right_side.shape[0] == rows_here * (devices // 2) and tile_bytes <= tile_bytes_limit:
        return by_realizations(point_data, right_side, pair_list)
    return by_points(point_data, right_side, pair_list)


def solution(mesh):
    placed = (P(None, ("row", "col")), P(None, ("row", "col")), P())
    return jax.shard_map(
        per_device,
        mesh=mesh,
        in_specs=placed,
        out_specs=(P(None, ("row", "col")), P(None, ("row", "col"))),
        check_vma=False,
    )
```

```python
import functools
import jax
import jax.numpy as jnp
from jax import lax
from jax.experimental import pallas as pl
from jax.experimental.pallas import tpu as pltpu
from jax.sharding import PartitionSpec as P

BLOCK = 128
ITERS = 3


long_range = 1.0
short_range = 0.35
nugget = 1.0
tiles_per_step = 8
rows_here = 4
chunk_bits = 1
chunk = 1 << chunk_bits
chunks_per_step = 135
tile_bytes_limit = 24 * 2**20
kernel_bytes = 12 * 2**20
f32 = jnp.float32
bf16 = jnp.bfloat16


def wendland(distance, reach):
    scaled = distance / reach
    remain = jnp.maximum(1.0 - scaled, 0.0)
    square = remain * remain
    return square * square * (4.0 * scaled + 1.0)


def covariance_tiles(row_points, column_points):
    delta_x = row_points[:, 0, :, None] - column_points[:, 0, None, :]
    delta_y = row_points[:, 1, :, None] - column_points[:, 1, None, :]
    delta_z = row_points[:, 2, :, None] - column_points[:, 2, None, :]
    distance = jnp.sqrt(delta_x * delta_x + delta_y * delta_y + delta_z * delta_z)
    kernel = wendland(distance, long_range) + wendland(distance, short_range)
    return row_points[:, 3, :, None] * kernel * column_points[:, 3, None, :]


def as_blocks(points):
    return points.reshape(4, -1, BLOCK).transpose(1, 0, 2)


def by_points(point_data, right_side, pair_list):
    col_devices = lax.axis_size("col")
    my_row = lax.axis_index("row")
    my_column = lax.axis_index("col")
    points = point_data.shape[1]
    blocks_here = points // BLOCK
    realizations = right_side.shape[0]
    own_blocks = as_blocks(point_data)
    row_blocks = as_blocks(lax.all_gather(point_data, "col", axis=1, tiled=True))
    column_blocks = as_blocks(lax.all_gather(point_data, "row", axis=1, tiled=True))
    row_count = row_blocks.shape[0]
    column_count = column_blocks.shape[0]
    lower_block = pair_list[0]
    upper_block = pair_list[1]
    this_device = my_row * col_devices + my_column
    device_of = (
        lower_block // blocks_here // col_devices * col_devices
        + upper_block // blocks_here % col_devices
    )
    roster_first_pair = jnp.sum((device_of < this_device).astype(jnp.int32))
    roster_pair_count = jnp.sum((device_of == this_device).astype(jnp.int32))
    roster_row_slot = jnp.clip(lower_block - my_row * col_devices * blocks_here, 0, row_count - 1)
    roster_column_slot = jnp.clip(
        upper_block // blocks_here // col_devices * blocks_here + upper_block % blocks_here,
        0,
        column_count - 1,
    )
    roster_step_count = (roster_pair_count + tiles_per_step - 1) // tiles_per_step
    plan = (
        roster_first_pair,
        roster_pair_count,
        roster_row_slot,
        roster_column_slot,
        roster_step_count,
        lower_block.shape[0],
    )
    first_pair, pair_count, row_slot, column_slot, step_count, listed = plan
    own_tiles = covariance_tiles(own_blocks, own_blocks).astype(jnp.bfloat16)

    def pick_tiles(step):
        offsets = step * tiles_per_step + jnp.arange(tiles_per_step)
        usable = offsets < pair_count
        picked = jnp.minimum(first_pair + offsets, listed - 1)
        row_pick = row_slot[picked]
        column_pick = column_slot[picked]
        tiles_now = covariance_tiles(row_blocks[row_pick], column_blocks[column_pick])
        tiles_now = jnp.where(usable[:, None, None], tiles_now, 0.0).astype(jnp.bfloat16)
        return (tiles_now, row_pick, column_pick)

    def inner(operands):
        stacked = jnp.stack(
            [jnp.sum(one_side * other_side, axis=1) for one_side, other_side in operands]
        )
        return lax.psum(stacked, ("row", "col"))

    solution = jnp.zeros_like(right_side)
    residual = right_side
    direction = right_side
    norm_now = inner(((residual, residual),))[0]
    for step in range(ITERS):
        rounded = direction.astype(jnp.bfloat16)
        product_row_direction = lax.all_gather(rounded, "col", axis=1, tiled=True)
        product_column_direction = lax.all_gather(rounded, "row", axis=1, tiled=True)
        row_direction = product_row_direction
        column_direction = product_column_direction
        row_direction = row_direction.reshape(realizations, row_count, BLOCK)
        column_direction = column_direction.reshape(realizations, column_count, BLOCK)

        def add_step(step, totals):
            into_rows, into_columns = totals
            tiles_now, row_pick, column_pick = pick_tiles(step)
            to_rows = jnp.einsum(
                "tij,ctj->cti",
                tiles_now,
                column_direction[:, column_pick],
                preferred_element_type=jnp.float32,
            )
            to_columns = jnp.einsum(
                "tij,cti->ctj",
                tiles_now,
                row_direction[:, row_pick],
                preferred_element_type=jnp.float32,
            )
            return (
                into_rows.at[:, row_pick].add(to_rows),
                into_columns.at[:, column_pick].add(to_columns),
            )

        empty_rows = jnp.zeros((realizations, row_count, BLOCK), jnp.float32)
        empty_columns = jnp.zeros((realizations, column_count, BLOCK), jnp.float32)
        into_rows, into_columns = lax.fori_loop(
            0, step_count, add_step, (empty_rows, empty_columns)
        )
        product_into_rows = into_rows.reshape(realizations, -1)
        product_into_columns = into_columns.reshape(realizations, -1)
        from_rows = lax.psum_scatter(product_into_rows, "col", scatter_dimension=1, tiled=True)
        from_columns = lax.psum_scatter(
            product_into_columns.astype(jnp.bfloat16), "row", scatter_dimension=1, tiled=True
        ).astype(jnp.float32)
        diagonal = jnp.einsum(
            "tij,ctj->cti",
            own_tiles,
            rounded.reshape(realizations, blocks_here, BLOCK),
            preferred_element_type=jnp.float32,
        )
        image = (
            nugget * direction + diagonal.reshape(realizations, points) + from_rows + from_columns
        )
        alpha = norm_now / inner(((direction, image),))[0]
        solution = solution + alpha[:, None] * direction
        residual = residual - alpha[:, None] * image
        if step + 1 < ITERS:
            norm_next = inner(((residual, residual),))[0]
            direction = residual + (norm_next / norm_now)[:, None] * direction
            norm_now = norm_next
    return (solution, residual)


def tile_schedule(listed, blocks):
    half = (listed + 1) // 2
    entries = half + blocks // 2
    sizes = range(64, 70)
    width = min(sizes, key=lambda size: (-(-entries // (2 * size)) * size, -size))
    steps = -(-entries // (2 * width)) * 2
    longest = (2 * half + blocks // 2 + (chunk - 1) * blocks) // chunk
    chunks = -(-longest // chunks_per_step) * chunks_per_step + chunks_per_step
    return half, width, steps, chunks


def packing_kernel(point_hbm, field_hbm, outgoing_ref, point_ref, field_ref, arrived):
    devices = outgoing_ref.shape[0]
    copies = (
        pltpu.make_async_copy(point_hbm, point_ref, arrived.at[0]),
        pltpu.make_async_copy(field_hbm, field_ref, arrived.at[1]),
    )
    for copy in copies:
        copy.start()
    for copy in copies:
        copy.wait()
    row = row_number((8, BLOCK))
    blank = jnp.zeros((4, BLOCK), f32)
    high_parts, low_parts = [], []
    for block in range(2):
        points = point_ref[:, block * BLOCK : (block + 1) * BLOCK]
        high = points.astype(bf16).astype(f32)
        high_parts.append(jnp.concatenate([blank, high], axis=0))
        low_parts.append(points - high)
    low = jnp.concatenate([low_parts[1], low_parts[0]], axis=0)
    for pair in range(devices // 4):
        rows = pl.ds(8 * pair, 8)
        fields = [field_ref[rows, block * BLOCK : (block + 1) * BLOCK] for block in range(2)]
        turned = [pltpu.roll(field, 4, axis=0) for field in fields]
        for side, chosen in enumerate((fields, turned)):
            parts = [jnp.where(row < 4, chosen[block], high_parts[block]) for block in range(2)]
            message = jnp.concatenate([*parts, low], axis=0).astype(bf16)
            outgoing_ref[4 * pair + 2 * side] = message
            outgoing_ref[4 * pair + 2 * side + 1] = message


def listing_kernel(
    plan,
    blocks,
    core_ref,
    pair_hbm,
    owner_ref,
    entry_ref,
    count_ref,
    low_ref,
    high_ref,
    open_ref,
    pair_ref,
    arrived,
):
    copy = pltpu.make_async_copy(pair_hbm, pair_ref, arrived)
    copy.start()
    half, width, steps, chunks = plan
    listed = pair_ref.shape[1]
    core = core_ref[0]
    slots = width * steps

    def clear(block, carry):
        open_ref[block] = 0
        return carry

    lax.fori_loop(0, blocks, clear, 0, unroll=16)

    def append(block, entry, used):
        place = open_ref[block]
        fresh = (place & (chunk - 1)) == 0
        place = jnp.where(fresh, used, place)
        open_ref[block] = place + 1
        for slot in range(1, chunk):
            entry_ref[place | slot] = blocks
        entry_ref[place] = entry
        owner_ref[place >> chunk_bits] = block
        return jnp.where(fresh, used + chunk, used)

    def list_pair(number, used):
        low = pair_ref[0, core * half + number]
        high = pair_ref[1, core * half + number]
        low_ref[number] = low
        high_ref[number] = high
        used = append(high, number * 65536 + low, used)
        return append(low, (slots + number) * 65536 + high, used)

    def list_diagonal(number, used):
        block = core * (blocks // 2) + number
        low_ref[half + number] = block
        high_ref[half + number] = block
        return append(block, (half + number) * 65536 + block, used)

    low_ref[half - 1] = blocks
    high_ref[half - 1] = blocks
    for number in range(half + blocks // 2, slots):
        low_ref[number] = blocks
        high_ref[number] = blocks
    copy.wait()
    used = lax.fori_loop(0, listed // 2, list_pair, 0, unroll=13)
    if listed % 2:
        used = lax.fori_loop(half - 1, half - core, list_pair, used)
    used = lax.fori_loop(0, blocks // 2, list_diagonal, used, unroll=8)
    used = used >> chunk_bits
    count_ref[0] = used
    for part in range(chunks_per_step):
        owner_ref[used + part] = blocks
        for slot in range(chunk):
            entry_ref[(used + part) * chunk + slot] = blocks


def radial(squared):
    squared = jnp.maximum(squared, 1e-30)
    distance = squared * lax.rsqrt(squared)
    near = jnp.maximum(1.0 - distance * (1.0 / long_range), 0.0)
    near_square = near * near
    wide = near_square * near_square * (1.25 - near)
    close = jnp.asarray(1.0, bf16) - distance.astype(bf16) * jnp.asarray(1.0 / short_range, bf16)
    close = jnp.maximum(close, jnp.asarray(0.0, bf16))
    close_square = close * close
    narrow = close_square * close_square * (jnp.asarray(1.25, bf16) - close)
    return wide.astype(bf16) + narrow


def three_parts(values):
    first = values.astype(bf16).astype(f32)
    rest = values - first
    second = rest.astype(bf16).astype(f32)
    return first, second, rest - second


def row_number(shape):
    return lax.broadcasted_iota(jnp.int32, shape, len(shape) - 2)


def store_scaled(fields_ref, direction, scale):
    blocks = direction.shape[0]
    blank = jnp.zeros((blocks, 16 - rows_here, BLOCK), f32)
    scaled = jnp.concatenate([direction * (4.0 * scale), blank], axis=1)
    fields_ref[0:blocks] = scaled.astype(bf16)
    fields_ref[blocks] = jnp.zeros((16, BLOCK), bf16)


def multiply(owner_ref, entry_ref, count, tiles_ref, fields_ref, totals_ref):
    totals_ref[...] = jnp.zeros_like(totals_ref)

    def step(number, carry):
        waiting = []

        def add(item):
            place, product = item
            totals_ref[owner_ref[place]] += product

        for part in range(chunks_per_step):
            place = number * chunks_per_step + part
            fields = []
            tiles = []
            for slot in range(chunk):
                entry = entry_ref[place * chunk + slot]
                fields.append(fields_ref[entry & 65535])
                tiles.append(tiles_ref[entry >> 16])
            product = jnp.dot(
                jnp.concatenate(fields, axis=1),
                jnp.concatenate(tiles, axis=0),
                preferred_element_type=f32,
            )
            waiting.append((place, product[0:8]))
            if len(waiting) > 8:
                add(waiting.pop(0))
        for item in waiting:
            add(item)
        return carry

    lax.fori_loop(0, (count + chunks_per_step - 1) // chunks_per_step, step, 0)


def first_kernel(
    plan,
    low_ref,
    high_ref,
    received_ref,
    tiles_ref,
    product_ref,
    gathered_ref,
    left_ref,
    right_ref,
    fields_ref,
    totals_ref,
    *stages,
):
    half, width, steps, _ = plan
    blocks = gathered_ref.shape[0]
    slots = width * steps
    for device in range(blocks // 2):
        message = received_ref[device].astype(f32)
        lower = message[16:24]
        is_point = row_number((8, BLOCK)) >= rows_here
        first = message[0:8] + jnp.where(is_point, lower, 0.0)
        second = message[8:16] + jnp.where(is_point, pltpu.roll(lower, 4, axis=0), 0.0)
        gathered_ref[2 * device] = first
        gathered_ref[2 * device + 1] = second
    highest = jnp.max(jnp.max(gathered_ref[...], axis=0), axis=1, keepdims=True)
    lowest = jnp.min(jnp.min(gathered_ref[...], axis=0), axis=1, keepdims=True)
    centre = 0.5 * (highest + lowest)

    def prepare(block, carry):
        row = row_number((8, BLOCK))
        is_coordinate = (row >= 4) & (row < 7)
        shifted = jnp.where(is_coordinate, gathered_ref[block] - centre, 0.0)
        squared = jnp.sum(shifted * shifted, axis=0, keepdims=True)
        left = jnp.where(row == 7, 1.0, jnp.where(row == 0, squared, shifted))
        right = jnp.where(row == 7, squared, jnp.where(row == 0, 1.0, -2.0 * shifted))
        left_1, left_2, left_3 = three_parts(left)
        right_1, right_2, right_3 = three_parts(right)
        left_all = jnp.concatenate([left_1, left_1, left_2, left_2, left_1, left_3], axis=0)
        right_all = jnp.concatenate([right_1, right_2, right_1, right_2, right_3, right_1], axis=0)
        left_ref[block] = left_all.T.astype(bf16)
        right_ref[block] = right_all.astype(bf16)
        return carry

    lax.fori_loop(0, blocks, prepare, 0, unroll=32)
    left_ref[blocks] = jnp.zeros((BLOCK, 48), bf16)
    right_ref[blocks] = jnp.zeros((48, BLOCK), bf16)
    store_scaled(fields_ref, gathered_ref[:, 0:rows_here, :], gathered_ref[:, 7:8, :])
    totals_ref[...] = jnp.zeros_like(totals_ref)

    def square(step, slot):
        number = step * width + slot
        return jnp.dot(
            left_ref[low_ref[number]], right_ref[high_ref[number]], preferred_element_type=f32
        )

    def make_tile(step, slot, stage, squared):
        number = step * width + slot
        tile = radial(squared)
        turned = tile.T
        tiles_ref[number] = tile
        tiles_ref[slots + number] = turned
        stage[0][slot] = tile
        stage[1][slot] = turned

    def use_tile(step, slot, stage):
        number = step * width + slot
        made = jnp.maximum(number, 0)
        low = jnp.where(number >= 0, low_ref[made], blocks)
        high = jnp.where(number >= 0, high_ref[made], blocks)
        is_pair = number < half
        ways = (
            (low, high),
            (jnp.where(is_pair, high, blocks), jnp.where(is_pair, low, blocks)),
        )
        products = []
        for (source, target), tiles in zip(ways, stage):
            product = jnp.dot(fields_ref[source], tiles[slot], preferred_element_type=f32)
            products.append((target, product[0:8]))
        return products

    def add_products(products):
        for target, product in products:
            totals_ref[target] += product

    def use_tiles(step, stage):
        for slot in range(width):
            add_products(use_tile(step, slot, stage))

    def both(step, new_stage, old_stage):
        waiting = []
        ahead = square(step, 0)
        for slot in range(width):
            squared = ahead
            if slot + 1 < width:
                ahead = square(step, slot + 1)
            make_tile(step, slot, new_stage, squared)
            waiting.append(use_tile(step - 1, slot, old_stage))
            if len(waiting) > 2:
                add_products(waiting.pop(0))
        for products in waiting:
            add_products(products)

    even, odd = stages[0:2], stages[2:4]

    def both_steps(pair, carry):
        both(2 * pair, even, odd)
        both(2 * pair + 1, odd, even)
        return carry

    lax.fori_loop(0, steps // 2, both_steps, 0)
    use_tiles(steps - 1, odd)
    product_ref[...] = totals_ref[0:blocks, 0:rows_here, :]


def total(values):
    return jnp.sum(jnp.sum(values, axis=0), axis=1, keepdims=True)[None]


def advance(mine_ref, other_ref, scale, direction, residual):
    image = nugget * direction + scale * (mine_ref[...] + other_ref[...])
    norm_now = total(residual * residual)
    along = total(direction * image)
    alpha = norm_now / along
    return alpha * direction, residual - alpha * image, norm_now


def next_kernel(
    first,
    owner_ref,
    entry_ref,
    count_ref,
    gathered_ref,
    mine_ref,
    other_ref,
    *rest,
):
    if first:
        tiles_ref, product_ref, state_out_ref, fields_ref, totals_ref = rest
        direction = gathered_ref[:, 0:rows_here, :]
        residual = direction
    else:
        state_ref, tiles_ref, product_ref, state_out_ref, fields_ref, totals_ref = rest
        direction = state_ref[2]
        residual = state_ref[1]
    scale = gathered_ref[:, 7:8, :]
    moved, residual, norm_now = advance(mine_ref, other_ref, scale, direction, residual)
    norm_next = total(residual * residual)
    direction = residual + (norm_next / norm_now) * direction
    state_out_ref[0] = moved if first else state_ref[0] + moved
    state_out_ref[1] = residual
    state_out_ref[2] = direction
    store_scaled(fields_ref, direction, scale)
    multiply(owner_ref, entry_ref, count_ref[0], tiles_ref, fields_ref, totals_ref)
    product_ref[...] = totals_ref[0 : gathered_ref.shape[0], 0:rows_here, :]


def last_kernel(core_ref, gathered_ref, mine_ref, other_ref, state_ref, result_ref):
    scale = gathered_ref[:, 7:8, :]
    moved, residual, _ = advance(mine_ref, other_ref, scale, state_ref[2], state_ref[1])
    chosen = jnp.where(core_ref[0] == 0, state_ref[0] + moved, residual)
    result_ref[...] = chosen.astype(bf16)


def by_realizations(point_data, right_side, pair_list):
    col_devices = lax.axis_size("col")
    devices = lax.axis_size("row") * col_devices
    chips = devices // 2
    blocks_here = point_data.shape[1] // BLOCK
    blocks = blocks_here * devices
    core = lax.rem(lax.axis_index("col"), 2).astype(jnp.int32).reshape(1)
    axes = ("row", "col")
    vector = pl.BlockSpec(memory_space=pltpu.VMEM)
    scalar = pl.BlockSpec(memory_space=pltpu.SMEM)
    plan = tile_schedule(pair_list.shape[1], blocks)
    half, width, steps, chunks = plan
    slots = width * steps

    limits = pltpu.CompilerParams(vmem_limit_bytes=kernel_bytes)
    outgoing = pl.pallas_call(
        packing_kernel,
        out_shape=jax.ShapeDtypeStruct((devices, 24, BLOCK), bf16),
        in_specs=[pl.BlockSpec(memory_space=pltpu.HBM)] * 2,
        out_specs=vector,
        scratch_shapes=[
            pltpu.VMEM(point_data.shape, f32),
            pltpu.VMEM(right_side.shape, f32),
            pltpu.SemaphoreType.DMA((2,)),
        ],
        compiler_params=limits,
    )(
        pltpu.with_memory_space_constraint(point_data, pltpu.HBM),
        pltpu.with_memory_space_constraint(right_side, pltpu.HBM),
    )
    owner, entry, count, low, high = pl.pallas_call(
        functools.partial(listing_kernel, plan, blocks),
        out_shape=(
            pltpu.SMEM((chunks + 8,), jnp.int32),
            pltpu.SMEM((chunks * chunk + 8,), jnp.int32),
            pltpu.SMEM((1,), jnp.int32),
            pltpu.SMEM((slots,), jnp.int32),
            pltpu.SMEM((slots,), jnp.int32),
        ),
        in_specs=[scalar, pl.BlockSpec(memory_space=pltpu.HBM)],
        out_specs=(scalar,) * 5,
        scratch_shapes=[
            pltpu.SMEM((blocks,), jnp.int32),
            pltpu.SMEM(pair_list.shape, jnp.int32),
            pltpu.SemaphoreType.DMA,
        ],
        cost_estimate=pl.CostEstimate(flops=8_000_000_000, bytes_accessed=20_000_000, transcendentals=0),
        compiler_params=limits,
    )(core, pltpu.with_memory_space_constraint(pair_list, pltpu.HBM))
    received = lax.all_to_all(outgoing, axes, 0, 0, tiled=True)

    field_shape = jax.ShapeDtypeStruct((blocks, 8, BLOCK), f32)
    product_shape = jax.ShapeDtypeStruct((blocks, rows_here, BLOCK), f32)
    state_shape = jax.ShapeDtypeStruct((3, blocks, rows_here, BLOCK), f32)
    work = [pltpu.VMEM((blocks + 1, 16, BLOCK), bf16), pltpu.VMEM((blocks + 1, 8, BLOCK), f32)]
    stage = pltpu.VMEM((width, BLOCK, BLOCK), bf16)
    tiles, mine, gathered = pl.pallas_call(
        functools.partial(first_kernel, plan),
        out_shape=(pltpu.VMEM((2 * slots, BLOCK, BLOCK), bf16), product_shape, field_shape),
        in_specs=[scalar, scalar, vector],
        out_specs=(vector, vector, vector),
        scratch_shapes=[
            pltpu.VMEM((blocks + 1, BLOCK, 48), bf16),
            pltpu.VMEM((blocks + 1, 48, BLOCK), bf16),
            *work,
            *[stage] * 4,
        ],
        compiler_params=limits,
    )(low, high, received)
    tiles = pltpu.with_memory_space_constraint(tiles, pltpu.VMEM)
    swap = [(place, place ^ 1) for place in range(col_devices)]
    state = None
    for step in range(1, ITERS):
        other = lax.ppermute(mine, "col", swap)
        first = step == 1
        carried = () if first else (state,)
        mine, state = pl.pallas_call(
            functools.partial(next_kernel, first),
            out_shape=(product_shape, state_shape),
            in_specs=[scalar, scalar, scalar] + [vector] * (4 + len(carried)),
            out_specs=(vector, vector),
            scratch_shapes=work,
            compiler_params=limits,
        )(owner, entry, count, gathered, mine, other, *carried, tiles)
    other = lax.ppermute(mine, "col", swap)
    result = pl.pallas_call(
        last_kernel,
        out_shape=jax.ShapeDtypeStruct((blocks, rows_here, BLOCK), bf16),
        in_specs=[scalar] + [vector] * 4,
        out_specs=vector,
        compiler_params=limits,
    )(core, gathered, mine, other, state)
    result = result.reshape(devices, blocks_here, rows_here, BLOCK)
    received = lax.all_to_all(result, axes, 0, 0, tiled=True)
    received = received.reshape(chips, 2, blocks_here, rows_here, BLOCK)
    received = received.transpose(1, 0, 3, 2, 4).reshape(2, right_side.shape[0], -1)
    return received[0].astype(f32), received[1].astype(f32)


def per_device(point_data, right_side, pair_list):
    col_devices = lax.axis_size("col")
    devices = lax.axis_size("row") * col_devices
    blocks = point_data.shape[1] // BLOCK * devices
    _, width, steps, _ = tile_schedule(pair_list.shape[1], blocks)
    tile_bytes = 2 * width * steps * BLOCK * BLOCK * 2
    paired = devices % 4 == 0 and col_devices % 2 == 0 and blocks == 2 * devices
    if paired and right_side.shape[0] == rows_here * (devices // 2) and tile_bytes <= tile_bytes_limit:
        return by_realizations(point_data, right_side, pair_list)
    return by_points(point_data, right_side, pair_list)


def solution(mesh):
    placed = (P(None, ("row", "col")), P(None, ("row", "col")), P())
    return jax.shard_map(
        per_device,
        mesh=mesh,
        in_specs=placed,
        out_specs=(P(None, ("row", "col")), P(None, ("row", "col"))),
        check_vma=False,
    )
```
